256 devices in a mesh: view: 8 (over x, z_hi), tile: 32 (over y, z_lo, core).
Axes of the slice: x: 4, y: 4, z: 8 (z_hi: 2, z_lo: 4; z = z_hi * 4 + z_lo), core: 2. Of those that a mesh axis runs over, the one named last changes fastest.
Arguments:
- estimate: float32 [512, 12288], P('tile'), may hold values from 0.5 to 2
- recorded: float32 [8, 512, 12288], P('view', 'tile'), may hold values from 0.5 to 4
- kernels: float32 [8, 31, 192], P('view'), may hold values from 0.01 to 0.06
- illuminated: int32 [8, 32], P('view', 'tile'), may hold values 0 or 1
- detection: int32 [8], P('view'), may hold values from 0 to 2, as said below
Outputs:
- deconvolved: float32 [512, 12288], P('tile')
The draws below stay inside these ranges and needn't reach their ends.
Inputs may be any that keep to these rules, and one draw needn't show every extreme that they name: `detection`: each of 0, 1 and 2 is some view's value when there are three views or more; 0 is always some view's value.
All inputs are finite; a program needn't handle non-finite values. No bound on the sum of `illuminated` on one device may be relied on, other than what follows from the above.
Results may differ from the reference program's by a relative error of at most 0.0003.
Values sent between devices are 32-bit elements; how exact they have to be, the bound alone decides.
A program may use at most 128 MiB of HBM per device.

```python
import math
import jax
import jax.numpy as jnp
from jax import lax

CX = 16
YW = 64
Z = 192
HALF = 15
ITERS = 2
TAPS = 31
X = 512
PLANE = 12288
N_VIEW = 8
N_TILE = 32


def draw_detection(key, part):
    key = jax.random.fold_in(key, 1)
    return (jax.random.permutation(key, N_VIEW) % 3).astype(jnp.int32)


def touch_ends(values, rng, smallest, top_value):
    longest = values.shape.index(max(values.shape))
    spots = []
    for shift in (0, 1):
        where = [jax.random.randint(jax.random.fold_in(rng, axis), (), 0, length) for axis, length in enumerate(values.shape)]
        where[longest] = (where[longest] + shift) % values.shape[longest]
        spots.append(tuple(where))
    return values.at[spots[0]].set(smallest).at[spots[1]].set(top_value)


def steps_of(rng, dims, shards, smallest, high):
    factor_of = 1.0
    for dim, blocks in shards:
        draws = jax.random.uniform(jax.random.fold_in(jax.random.fold_in(rng, 6), dim), (blocks,), jnp.float32, smallest / len(shards), high / len(shards))
        factor_of = factor_of * jnp.repeat(jnp.exp(draws), dims[dim] // blocks).reshape((-1,) + (1,) * (len(dims) - 1 - dim))
    return factor_of


def setup_inputs(seed: int = 0) -> dict:
    splits = jax.random.split(jax.random.key(seed), 6)
    estimate = jnp.clip(jnp.exp(math.log(2.0) - 1.3862944 * jax.random.uniform(splits[0], (X, PLANE), jnp.float32) ** steps_of(splits[0], (X, PLANE), ((0, 32),), -0.2, 0.2)), 0.5, 2.0)
    recorded = jnp.clip(jnp.exp(math.log(4.0) - 2.0794415 * jax.random.uniform(splits[1], (N_VIEW, X, PLANE), jnp.float32) ** steps_of(splits[1], (N_VIEW, X, PLANE), ((0, 8), (1, 32)), -0.2, 0.2)), 0.5, 4.0)
    kernels = jnp.clip(jnp.exp(math.log(0.06) - 1.7917595 * jax.random.uniform(splits[2], (N_VIEW, TAPS, Z), jnp.float32) ** steps_of(splits[2], (N_VIEW, TAPS, Z), ((0, 8),), -0.2, 0.2)), 0.01, 0.06)
    illuminated = touch_ends((jax.random.randint(splits[3], (N_VIEW, N_TILE), 0, 4) < 3).astype(jnp.int32), jax.random.fold_in(splits[3], 1), 0, 1)
    detection = draw_detection(jax.random.fold_in(splits[5], 71), 0)
    return {"estimate": estimate, "recorded": recorded, "kernels": kernels, "illuminated": illuminated, "detection": detection}


def forward_axis(volume, taps, axis):
    length = volume.shape[axis]
    widths = [(0, 0), (0, 0), (0, 0)]
    widths[axis] = (HALF, HALF)
    padded = jnp.pad(volume, widths)
    result = jnp.zeros(volume.shape, jnp.float32)
    for offset in range(2 * HALF + 1):
        result = result + taps[offset] * lax.slice_in_dim(padded, offset, offset + length, axis=axis)
    return result


def adjoint_axis(ratio, taps, axis):
    length = ratio.shape[axis]
    widths = [(0, 0), (0, 0), (0, 0)]
    widths[axis] = (HALF, HALF)
    padded = jnp.pad(ratio, widths)
    result = jnp.zeros(ratio.shape, jnp.float32)
    for offset in range(2 * HALF + 1):
        result = result + taps[offset] * lax.slice_in_dim(padded, 2 * HALF - offset, 2 * HALF - offset + length, axis=axis)
    return result


def adjoint_depth(ratio, taps):
    length = ratio.shape[2]
    result = jnp.zeros(ratio.shape, jnp.float32)
    for offset in range(2 * HALF + 1):
        padded = jnp.pad(taps[offset] * ratio, ((0, 0), (0, 0), (HALF, HALF)))
        result = result + lax.slice_in_dim(padded, 2 * HALF - offset, 2 * HALF - offset + length, axis=2)
    return result


def forward_first(volume, taps):
    return forward_axis(volume, taps, 0)


def forward_second(volume, taps):
    return forward_axis(volume, taps, 1)


def forward_depth(volume, taps):
    return forward_axis(volume, taps, 2)


def adjoint_first(ratio, taps):
    return adjoint_axis(ratio, taps, 0)


def adjoint_second(ratio, taps):
    return adjoint_axis(ratio, taps, 1)


def reference(estimate, recorded, kernels, illuminated, detection):
    volume = estimate.reshape(X, YW, Z)
    measured_all = recorded.reshape(N_VIEW, X, YW, Z)
    for iteration in range(ITERS):
        summed_all = jnp.zeros(volume.shape, jnp.float32)
        for view_index in range(N_VIEW):
            taps = kernels[view_index]
            detect_axis = detection[view_index]
            blurred = lax.switch(detect_axis, [forward_first, forward_second, forward_depth], volume, taps)
            ratio = measured_all[view_index] / blurred
            spread = lax.switch(detect_axis, [adjoint_first, adjoint_second, adjoint_depth], ratio, taps)
            tile_lit = jnp.repeat(illuminated[view_index], CX)[:, None, None] > 0
            summed_all = summed_all + jnp.where(tile_lit, spread, 1.0)
        volume = volume * summed_all / N_VIEW
    return volume.reshape(X, YW * Z)
```

```python
import jax
import jax.numpy as jnp
from jax import lax
from jax.experimental import pallas as pl
from jax.experimental.pallas import tpu as pltpu
from jax.sharding import PartitionSpec as P


YW = 64
Z = 192
TAPS = 31
HALF = 15
ITERS = 2
VIEWS = 8
XC = 4
TILES = 32
CX = 16
ROWS = 16
DEPTH = 96
LANES = 128
RIM = 16
CHUNK = ROWS * Z
PACKED = 12
PIECES = 2
MESH = pl.DeviceIdType.MESH
F32 = jnp.float32
HIGH = lax.Precision.HIGHEST


def lane_of(shape):
    return lax.broadcasted_iota(jnp.int32, shape, len(shape) - 1)


def roll(a, shift):
    return pltpu.roll(a, shift, a.ndim - 1)


def pair_halves(t0, t1, t2):
    lane = lane_of(t0.shape)
    a0 = roll(t0, 16)
    a1 = jnp.where(lane < 48, roll(t0, 48), roll(t1, 48))
    b0 = jnp.where(lane < 80, roll(t1, 80), roll(t2, 80))
    b1 = roll(t2, 112)
    return (a0, b0), (a1, b1)


def halves_pair(a0, a1, b0, b1):
    lane = lane_of(a0.shape)
    a1r, b0r = roll(a1, 80), roll(b0, 48)
    t0 = jnp.where(lane < 96, roll(a0, 112), a1r)
    t1 = jnp.where(lane < 64, a1r, b0r)
    t2 = jnp.where(lane < 32, b0r, roll(b1, 16))
    return t0, t1, t2


def pack(rows):
    lane = lane_of(rows[0].shape)
    inner = (lane >= RIM) & (lane < RIM + DEPTH)
    return [jnp.where(inner, rows[i], roll(rows[3], 96 - 32 * i)) for i in range(3)]


def unpack(tiles):
    lane = lane_of(tiles[0].shape)
    r = [roll(tiles[i], 32 + 32 * i) for i in range(3)]
    return [tiles[0], tiles[1], tiles[2], jnp.where(lane < 48, r[0], jnp.where(lane < 80, r[1], r[2]))]


def swap(a):
    return jnp.swapaxes(a, 0, 1)


def pack_rim(a, shift):
    lane = lane_of((32, LANES))
    out = jnp.zeros((32, LANES), F32)
    for g in range(8):
        moved = roll(a[32 * g : 32 * g + 32], lax.rem(shift + 16 * g, 128))
        out = jnp.where((lane >= 16 * g) & (lane < 16 * g + 16), moved, out)
    return out


def unpack_rim(p, first):
    lane = lane_of((32, LANES))
    keep = (lane >= first) & (lane < first + 16)
    return jnp.concatenate(
        [jnp.where(keep, roll(p, lax.rem(first + 128 - 16 * g, 128)), 0.0) for g in range(8)], axis=0
    )


def kernel(
    est_hbm, rec_hbm, ker_ref, lit_ref, det_ref, out_ref,
    est, rec, kpad, send, got, tap_send, tap_got, meta_send, meta_got, lit_send, lit_got,
    weight, band, grid, depth_in, rec_in, blurred, total, land, rim_send, rim_land, gathered,
    in_sem, a_s, a_r, t_s, t_r, m_s, m_r, l_s, l_r, h_s, h_r, g_s, g_r, z_s, z_r, f_s, f_r,
):
    view = lax.axis_index("view")
    tile = lax.axis_index("tile")
    cx, zh = view // 2, lax.rem(view, 2)
    upper = zh == 1

    def at(dx, dz):
        return lax.rem(cx + dx, XC) * 2 + lax.rem(zh + dz, 2)

    others = [(0, 1), (1, 1), (3, 1), (2, 1), (1, 0), (3, 0), (2, 0)]

    to_device = [
        (view, lax.rem(tile + TILES - 1, TILES)),
        (view, lax.rem(tile + 1, TILES)),
        (lax.rem(view + VIEWS - 2, VIEWS), tile),
        (lax.rem(view + 2, VIEWS), tile),
        (view + 1 - 2 * zh, tile),
    ]
    goes = [tile > 0, tile < TILES - 1, cx > 0, cx < XC - 1, None]
    comes = [tile < TILES - 1, tile > 0, cx < XC - 1, cx > 0, None]

    def when(cond, f):
        if cond is None:
            f()
        else:
            pl.when(cond)(f)

    barrier = pltpu.get_barrier_semaphore()

    def greet(device):
        pl.semaphore_signal(barrier, inc=1, device_id=device, device_id_type=MESH)

    for d in (0, 1):
        when(goes[d], lambda d=d: greet(to_device[d]))
    for dx, dz in others:
        greet((at(dx, dz), tile))

    est_in = pltpu.make_async_copy(est_hbm, est.at[:, pl.ds(CHUNK, YW * Z)], in_sem.at[0])
    rec_copy = pltpu.make_async_copy(rec_hbm.at[0], rec, in_sem.at[1])
    est_in.start()
    rec_copy.start()

    def rim_copy(phase, d, src, dst):
        return pltpu.make_async_remote_copy(
            src_ref=src, dst_ref=dst, send_sem=h_s.at[phase, d], recv_sem=h_r.at[phase, d],
            device_id=to_device[d], device_id_type=MESH,
        )

    def volume_rim(phase, d):
        if d == 4:
            return rim_copy(phase, d, rim_send.at[phase], rim_land.at[phase])
        layout = 1 if d < 2 else 0
        if d % 2 == 0:
            return rim_copy(phase, d, grid.at[layout, pl.ds(16, 15)], grid.at[layout, pl.ds(32, 15)])
        return rim_copy(phase, d, grid.at[layout, pl.ds(17, 15)], grid.at[layout, pl.ds(1, 15)])

    def sum_rim(phase, d):
        if d == 4:
            return rim_copy(phase, d, rim_send.at[phase], rim_land.at[phase])
        layout = 1 if d < 2 else 0
        first = 1 if d % 2 == 0 else 32
        return rim_copy(phase, d, total.at[layout, pl.ds(first, 15)], land.at[phase // 2, d])

    def start_rims(make, phase, dirs):
        for d in dirs:
            when(goes[d], lambda d=d: make(phase, d).start())

    def recv_rims(make, phase, dirs):
        for d in dirs:
            when(comes[d], lambda d=d: make(phase, d).wait_recv())

    def sent_rims(make, phase, dirs):
        for d in dirs:
            when(goes[d], lambda d=d: make(phase, d).wait_send())

    zero_rim = jnp.zeros((16, 16, LANES), F32)
    for d, into in ((0, 32), (1, 0)):
        @pl.when(jnp.logical_not(comes[d]))
        def _(d=d, into=into):
            grid[1, into : into + 16] = zero_rim
            lit_got[d] = jnp.zeros((8, LANES), F32)

    for d in range(4):
        @pl.when(jnp.logical_not(comes[d]))
        def _(d=d):
            for i in range(ITERS):
                land[i, d] = zero_rim[:15]

    lane32 = lane_of((32, LANES))
    inner32 = (lane32 >= RIM) & (lane32 < RIM + DEPTH)
    kpad[...] = jnp.zeros((32, 2 * LANES), F32)
    kpad[0:TAPS, 0:Z] = ker_ref[0]
    k0, k1 = kpad[:, 0:LANES], kpad[:, LANES : 2 * LANES]
    row8 = lax.broadcasted_iota(jnp.int32, (8, LANES), 0)
    axis_now = det_ref[0]
    flags = jnp.where(row8 == axis_now, 1.0, 0.0).astype(F32)
    tap_send[0, 0:32] = jnp.where(inner32, roll(k0, 16), 0.0)
    tap_send[1, 0:32] = jnp.where(inner32, jnp.where(lane32 < 48, roll(k0, 48), roll(k1, 48)), 0.0)
    tap_send[0, 32:40] = flags
    tap_send[1, 32:40] = flags
    tap_got[view] = tap_send[zh]
    lit_now = (lit_ref[0, 0] > 0).astype(F32)
    lit_send[...] = jnp.full((8, LANES), lit_now, F32)

    est[:, 0:CHUNK] = jnp.zeros((CX, CHUNK), F32)
    est[:, CHUNK + YW * Z : 2 * CHUNK + YW * Z] = jnp.zeros((CX, CHUNK), F32)
    est_in.wait()
    lane16 = lane_of((CX, LANES))
    edge = (lane16 >= jnp.where(upper, 0, RIM)) & (lane16 < jnp.where(upper, RIM + DEPTH, LANES))
    high_half = jnp.broadcast_to(zh, (CX, LANES)) == 1

    def est_pair(j, carry):
        base = pl.multiple_of(cx * CHUNK + j * 2 * Z, LANES)
        tiles = [est[:, pl.ds(base + LANES * i, LANES)] for i in range(3)]
        low, high = pair_halves(*tiles)
        for i in range(2):
            grid[0, 2 * j + i] = jnp.where(edge, jnp.where(high_half, high[i], low[i]), 0.0)
        return carry

    lax.fori_loop(0, 24, est_pair, 0)
    centre = grid[0, 16:32]
    depth_in[...] = centre
    grid[1, 16:32] = swap(centre)

    rec_copy.wait()

    def pack_rows(step, carry):
        rows, part = step // 4, lax.rem(step, 4)
        rows = lax.rem(cx + rows, XC)
        base = pl.multiple_of(rows * CHUNK + part * 4 * Z, LANES)
        tiles = [rec[:, pl.ds(base + LANES * i, LANES)] for i in range(6)]
        one, two = pair_halves(*tiles[:3]), pair_halves(*tiles[3:])
        for half in range(2):
            packed = pack([*one[half], *two[half]])
            for i in range(3):
                send[rows * 2 + half, part * 3 + i] = packed[i]
        return carry

    lax.fori_loop(0, 16, pack_rows, 0)
    got[view] = send[view]

    pl.semaphore_wait(barrier, 7 + (tile > 0).astype(jnp.int32) + (tile < TILES - 1).astype(jnp.int32))

    def to_view(v, src, dst, s, r):
        return pltpu.make_async_remote_copy(
            src_ref=src, dst_ref=dst, send_sem=s.at[v], recv_sem=r.at[v], device_id=(v, tile), device_id_type=MESH
        )

    def lit_copy(d):
        return pltpu.make_async_remote_copy(
            src_ref=lit_send, dst_ref=lit_got.at[d], send_sem=l_s.at[d], recv_sem=l_r.at[d],
            device_id=to_device[d], device_id_type=MESH,
        )

    def out_to(v, src, dst, s, r):
        return pltpu.make_async_remote_copy(
            src_ref=src, dst_ref=dst, send_sem=s.at[v], recv_sem=r.at[view], device_id=(v, tile), device_id_type=MESH
        )

    for d in (0, 1):
        when(goes[d], lambda d=d: lit_copy(d).start())
    for dx, dz in others:
        v = at(dx, dz)
        out_to(v, tap_send.at[lax.rem(v, 2)], tap_got.at[view], t_s, t_r).start()
    start_rims(volume_rim, 0, (0, 1))
    for dx, dz in others:
        v = at(dx, dz)
        out_to(v, send.at[v], got.at[view], a_s, a_r).start()

    for d in (0, 1):
        when(comes[d], lambda d=d: lit_copy(d).wait_recv())
    meta_send[...] = jnp.where(row8 == 0, lit_now, jnp.where(row8 == 1, lit_got[1], lit_got[0]))
    meta_got[view] = meta_send[...]
    for dx, dz in others:
        out_to(at(dx, dz), meta_send, meta_got.at[view], m_s, m_r).start()

    for dx, dz in others:
        v = at(dx, dz)
        to_view(v, tap_send.at[0], tap_got.at[v], t_s, t_r).wait_recv()

    def prepare(v, carry):
        taps = tap_got[v, 0:32]
        along_x = tap_got[v, 32:33]
        along_y = tap_got[v, 33:34]
        along_z = tap_got[v, 34:35]
        weight[v] = taps * (along_x + along_y)
        deep = jnp.concatenate([taps * along_z, jnp.zeros((LANES - 32, LANES), F32)], axis=0)
        band[v] = pltpu.roll(jnp.transpose(deep), LANES - HALF, 1, stride=1, stride_axis=0)
        return carry

    lax.fori_loop(0, VIEWS, prepare, 0)

    def blur_view(v, carry):
        first_dim = jnp.broadcast_to(tap_got[v, 32:33], (8, LANES)) > 0.5
        deep = lax.dot_general(
            depth_in[...].reshape(256, LANES), band[v], (((1,), (1,)), ((), ())),
            precision=HIGH, preferred_element_type=F32,
        ).reshape(16, 16, LANES)
        for s in range(2):
            for h in range(2):
                window = jnp.where(
                    first_dim[None],
                    grid[1, 8 * h + 1 : 8 * h + 39, 8 * s : 8 * s + 8],
                    grid[0, 8 * h + 1 : 8 * h + 39, 8 * s : 8 * s + 8],
                )
                acc = deep[8 * h : 8 * h + 8, 8 * s : 8 * s + 8]
                for k in range(TAPS):
                    acc = acc + window[k : k + 8] * weight[v, k : k + 1][None]
                blurred[v, 8 * h : 8 * h + 8, 8 * s : 8 * s + 8] = acc
        return carry

    lane3 = lane_of((16, 16, LANES))
    inner3 = (lane3 >= RIM) & (lane3 < RIM + DEPTH)

    def spread_view(v):
        along_x = jnp.broadcast_to(tap_got[v, 32:33], (8, LANES))
        along_y = jnp.broadcast_to(tap_got[v, 33:34], (8, LANES))
        lit = [jnp.broadcast_to(meta_got[v, i : i + 1], (8, LANES)) for i in range(3)]
        first_dim = along_x > 0.5
        ratio = jnp.where(
            inner3, jnp.where(jnp.broadcast_to(first_dim[:1][None], (16, 16, LANES)), rec_in[1, v], rec_in[0, v]) / blurred[v], 0.0
        )
        deep = lax.dot_general(
            ratio.reshape(256, LANES), band[v], (((1,), (0,)), ((), ())), precision=HIGH, preferred_element_type=F32
        ).reshape(16, 16, LANES)
        own = lit[0][:1][None]
        total[0, 16:32] += deep * own
        for s in range(2):
            r = ratio[:, 8 * s : 8 * s + 8]
            for block in range(3):
                first = (-HALF, 0, 16)[block]
                count = (HALF, 16, HALF)[block]
                acc = jnp.zeros((count, 8, LANES), F32)
                for k in range(TAPS):
                    lo = max(first, k - HALF)
                    hi = min(first + count, 16 + k - HALF)
                    if lo >= hi:
                        continue
                    part = r[lo - k + HALF : hi - k + HALF] * weight[v, k : k + 1][None]
                    pieces = []
                    if lo > first:
                        pieces.append(acc[: lo - first])
                    pieces.append(acc[lo - first : hi - first] + part)
                    if hi < first + count:
                        pieces.append(acc[hi - first :])
                    acc = jnp.concatenate(pieces, axis=0) if len(pieces) > 1 else pieces[0]
                where = slice(first + 16, first + 16 + count)
                lit_x = (lit[1], lit[0], lit[2])[block]
                total[1, where, 8 * s : 8 * s + 8] += acc * (along_x * lit_x)[None]
                total[0, where, 8 * s : 8 * s + 8] += acc * (along_y * lit[0])[None]

    def update(phase):
        for d in range(4):
            layout = 1 if d < 2 else 0
            first = 17 if d % 2 == 0 else 16
            total[layout, first : first + 15] += land[phase // 2, d]
        unlit = jnp.zeros((1, LANES), F32)
        for v in range(VIEWS):
            unlit = unlit + (1.0 - meta_got[v, 0:1])
        rim = unpack_rim(rim_land[phase], jnp.where(upper, 16, 96)).reshape(16, 16, LANES)
        summed = total[0, 16:32] + swap(total[1, 16:32]) + rim + unlit[None]
        return jnp.where(inner3, grid[0, 16:32] * summed * (1.0 / VIEWS), 0.0)

    recv_rims(volume_rim, 0, (0, 1))
    lax.fori_loop(0, VIEWS, blur_view, 0)

    def arrive(v):
        for part in range(4):
            rows = unpack([got[v, 3 * part + i] for i in range(3)])
            for i in range(4):
                rec_in[0, v, 4 * part + i] = rows[i]
        rec_in[1, v] = swap(rec_in[0, v])

    for dx, dz in others:
        v = at(dx, dz)
        to_view(v, meta_send, meta_got.at[v], m_s, m_r).wait_recv()

    total[...] = jnp.zeros((2, 48, 16, LANES), F32)
    arrive(view)
    spread_view(view)

    def spread_arrived(step, carry):
        order = lax.rem(step, 4)
        v = lax.rem(cx + order, XC) * 2 + lax.rem(zh + step // 4, 2)
        to_view(v, send.at[v], got.at[v], a_s, a_r).wait_recv()
        arrive(v)
        spread_view(v)
        return carry

    lax.fori_loop(1, VIEWS, spread_arrived, 0)

    def send_sums(phase):
        rim_send[phase] = pack_rim(total[0, 16:32].reshape(256, LANES), jnp.where(upper, 0, 16))
        start_rims(sum_rim, phase, range(5))

    sent_rims(volume_rim, 0, (0, 1))
    send_sums(1)
    recv_rims(sum_rim, 1, range(5))
    sent_rims(sum_rim, 1, range(5))
    fresh = update(1)
    grid[0, 16:32] = fresh
    start_rims(volume_rim, 2, (2, 3))
    grid[1, 16:32] = swap(fresh)
    start_rims(volume_rim, 2, (0, 1))
    rim_send[2] = pack_rim(fresh.reshape(256, LANES), jnp.where(upper, 112, 32))
    start_rims(volume_rim, 2, (4,))
    total[...] = jnp.zeros((2, 48, 16, LANES), F32)
    recv_rims(volume_rim, 2, range(5))
    depth_in[...] = grid[0, 16:32] + unpack_rim(rim_land[2], jnp.where(upper, 0, 112)).reshape(16, 16, LANES)

    def second(v, carry):
        blur_view(v, 0)
        spread_view(v)
        return carry

    lax.fori_loop(0, VIEWS, second, 0)
    send_sums(3)
    recv_rims(sum_rim, 3, range(5))
    fresh = update(3)

    for part in range(4):
        packed = pack([fresh[4 * part + i] for i in range(4)])
        for i in range(3):
            gathered[view, 3 * part + i] = packed[i]
    mate = at(0, 1)
    size = PACKED // PIECES

    def half_copy(i, block):
        cells = gathered.at[block, pl.ds(size * i, size)]
        return pltpu.make_async_remote_copy(
            src_ref=cells, dst_ref=cells, send_sem=z_s.at[i], recv_sem=z_r.at[i], device_id=(mate, tile), device_id_type=MESH
        )

    def row_copy(dx, block):
        cells = gathered.at[block]
        return pltpu.make_async_remote_copy(
            src_ref=cells, dst_ref=cells, send_sem=g_s.at[dx - 1], recv_sem=g_r.at[dx - 1],
            device_id=(at(dx, 0), tile), device_id_type=MESH,
        )

    def forward_copy(dx, i, block):
        cells = gathered.at[block, pl.ds(size * i, size)]
        return pltpu.make_async_remote_copy(
            src_ref=cells, dst_ref=cells, send_sem=f_s.at[dx - 1, i], recv_sem=f_r.at[dx - 1, i],
            device_id=(at(dx, 0), tile), device_id_type=MESH,
        )

    for i in range(PIECES):
        half_copy(i, view).start()
    for dx in (1, 3, 2):
        row_copy(dx, view).start()
    for i in range(PIECES):
        half_copy(i, mate).wait_recv()
        for dx in (1, 3, 2):
            forward_copy(dx, i, mate).start()

    def unpack_out(rows):
        for part in range(4):
            low = unpack([gathered[2 * rows, 3 * part + i] for i in range(3)])
            high = unpack([gathered[2 * rows + 1, 3 * part + i] for i in range(3)])
            base = pl.multiple_of(rows * CHUNK + part * 4 * Z, LANES)
            for p in range(2):
                for i, t in enumerate(halves_pair(low[2 * p], high[2 * p], low[2 * p + 1], high[2 * p + 1])):
                    out_ref[:, pl.ds(base + LANES * (3 * p + i), LANES)] = t

    unpack_out(cx)
    for dx in (1, 3, 2):
        source = at(XC - dx, 0)
        row_copy(dx, source).wait_recv()
        for i in range(PIECES):
            forward_copy(dx, i, at(XC - dx, 1)).wait_recv()
        unpack_out(source // 2)

    for d in (0, 1):
        when(goes[d], lambda d=d: lit_copy(d).wait_send())
    for dx, dz in others:
        v = at(dx, dz)
        out_to(v, tap_send.at[0], tap_got.at[view], t_s, t_r).wait_send()
        out_to(v, meta_send, meta_got.at[view], m_s, m_r).wait_send()
        out_to(v, send.at[v], got.at[view], a_s, a_r).wait_send()
    sent_rims(volume_rim, 2, range(5))
    sent_rims(sum_rim, 3, range(5))
    for i in range(PIECES):
        half_copy(i, view).wait_send()
    for dx in (1, 3, 2):
        row_copy(dx, view).wait_send()
        for i in range(PIECES):
            forward_copy(dx, i, mate).wait_send()


def on_device(estimate, recorded, kernels, illuminated, detection):
    dma = pltpu.SemaphoreType.DMA
    vmem = lambda *shape: pltpu.VMEM(shape, F32)
    return pl.pallas_call(
        kernel,
        out_shape=jax.ShapeDtypeStruct((CX, YW * Z), F32),
        in_specs=[
            pl.BlockSpec(memory_space=pl.ANY),
            pl.BlockSpec(memory_space=pl.ANY),
            pl.BlockSpec(memory_space=pltpu.VMEM),
            pl.BlockSpec(memory_space=pltpu.SMEM),
            pl.BlockSpec(memory_space=pltpu.SMEM),
        ],
        out_specs=pl.BlockSpec(memory_space=pltpu.VMEM),
        scratch_shapes=[
            vmem(CX, YW * Z + 2 * CHUNK),
            vmem(CX, YW * Z),
            vmem(32, 2 * LANES),
            vmem(VIEWS, PACKED, CX, LANES),
            vmem(VIEWS, PACKED, CX, LANES),
            vmem(2, 40, LANES),
            vmem(VIEWS, 40, LANES),
            vmem(8, LANES),
            vmem(VIEWS, 8, LANES),
            vmem(8, LANES),
            vmem(2, 8, LANES),
            vmem(VIEWS, 32, LANES),
            vmem(VIEWS, LANES, LANES),
            vmem(2, 48, 16, LANES),
            vmem(16, 16, LANES),
            vmem(2, VIEWS, 16, 16, LANES),
            vmem(VIEWS, 16, 16, LANES),
            vmem(2, 48, 16, LANES),
            vmem(ITERS, 4, HALF, 16, LANES),
            vmem(4, 32, LANES),
            vmem(4, 32, LANES),
            vmem(VIEWS, PACKED, CX, LANES),
            dma((2,)),
            dma((VIEWS,)), dma((VIEWS,)),
            dma((VIEWS,)), dma((VIEWS,)),
            dma((VIEWS,)), dma((VIEWS,)),
            dma((2,)), dma((2,)),
            dma((4, 5)), dma((4, 5)),
            dma((3,)), dma((3,)),
            dma((PIECES,)), dma((PIECES,)),
            dma((3, PIECES)), dma((3, PIECES)),
        ],
        compiler_params=pltpu.CompilerParams(
            collective_id=0, has_side_effects=True, vmem_limit_bytes=40 * 1024 * 1024
        ),
    )(estimate, recorded, kernels, illuminated, detection)


def solution(mesh):
    in_specs = (
        P("tile", None),
        P("view", "tile", None),
        P("view", None, None),
        P("view", "tile"),
        P("view"),
    )
    return jax.shard_map(
        on_device, mesh=mesh, in_specs=in_specs, out_specs=P("tile", None), check_vma=False
    )
```

```python
import jax
import jax.numpy as jnp
from jax import lax
from jax.experimental import pallas as pl
from jax.experimental.pallas import tpu as pltpu
from jax.sharding import PartitionSpec as P


YW = 64
Z = 192
TAPS = 31
HALF = 15
ITERS = 2
VIEWS = 8
XC = 4
TILES = 32
CX = 16
ROWS = 16
DEPTH = 96
LANES = 128
RIM = 16
CHUNK = ROWS * Z
PACKED = 12
PIECES = 4
VMEM_BYTES = 60 * 1024 * 1024
MESH = pl.DeviceIdType.MESH
F32 = jnp.float32
BF16 = jnp.bfloat16


def lane_of(shape):
    return lax.broadcasted_iota(jnp.int32, shape, len(shape) - 1)


def roll(a, shift):
    return pltpu.roll(a, shift, a.ndim - 1)


def pair_halves(t0, t1, t2):
    lane = lane_of(t0.shape)
    a0 = roll(t0, 16)
    a1 = jnp.where(lane < 48, roll(t0, 48), roll(t1, 48))
    b0 = jnp.where(lane < 80, roll(t1, 80), roll(t2, 80))
    b1 = roll(t2, 112)
    return (a0, b0), (a1, b1)


def halves_pair(a0, a1, b0, b1):
    lane = lane_of(a0.shape)
    a1r, b0r = roll(a1, 80), roll(b0, 48)
    t0 = jnp.where(lane < 96, roll(a0, 112), a1r)
    t1 = jnp.where(lane < 64, a1r, b0r)
    t2 = jnp.where(lane < 32, b0r, roll(b1, 16))
    return t0, t1, t2


def pack(rows):
    lane = lane_of(rows[0].shape)
    inner = (lane >= RIM) & (lane < RIM + DEPTH)
    return [jnp.where(inner, rows[i], roll(rows[3], 96 - 32 * i)) for i in range(3)]


def unpack(tiles):
    lane = lane_of(tiles[0].shape)
    r = [roll(tiles[i], 32 + 32 * i) for i in range(3)]
    return [tiles[0], tiles[1], tiles[2], jnp.where(lane < 48, r[0], jnp.where(lane < 80, r[1], r[2]))]


def swap(a):
    return jnp.swapaxes(a, 0, 1)


def pack_rim(a, shift):
    lane = lane_of((32, LANES))
    out = jnp.zeros((32, LANES), F32)
    for g in range(8):
        moved = roll(a[32 * g : 32 * g + 32], lax.rem(shift + 16 * g, 128))
        out = jnp.where((lane >= 16 * g) & (lane < 16 * g + 16), moved, out)
    return out


def unpack_rim(p, first):
    lane = lane_of((32, LANES))
    keep = (lane >= first) & (lane < first + 16)
    return jnp.concatenate(
        [jnp.where(keep, roll(p, lax.rem(first + 128 - 16 * g, 128)), 0.0) for g in range(8)], axis=0
    )


def split3(a, order):
    high = a.astype(BF16)
    low = (a - high.astype(F32)).astype(BF16)
    return jnp.concatenate([(high, low)[i] for i in order], axis=-1)


def kernel(
    est_hbm, rec_hbm, ker_hbm, lit_ref, det_ref, out_hbm,
    est, rec, kpad, send, got, tap_send, tap_got, lit_send, lit_got, flags_of,
    weight, band, band_t, grid, depth_in, rec_in, blurred, total, land, rim_send, rim_land, gathered, out,
    in_sem, out_sem, a_s, a_r, t_s, t_r, l_s, l_r, h_s, h_r, g_s, g_r, z_s, z_r, f_s, f_r,
):
    view = lax.axis_index("view")
    tile = lax.axis_index("tile")
    cx, zh = view // 2, lax.rem(view, 2)
    odd = lax.rem(tile // 8, 2)
    deep_half = lax.rem(zh + odd, 2)
    upper = deep_half == 1

    def at(dx, dz):
        return lax.rem(cx + dx, XC) * 2 + lax.rem(zh + dz, 2)

    mate = at(0, 1)
    others = [(0, 1), (1, 1), (1, 0), (3, 1), (3, 0), (2, 1), (2, 0)]

    to_device = [
        (jnp.where(lax.rem(tile, 8) == 0, mate, view), lax.rem(tile + TILES - 1, TILES)),
        (jnp.where(lax.rem(tile, 8) == 7, mate, view), lax.rem(tile + 1, TILES)),
        (lax.rem(view + VIEWS - 2, VIEWS), tile),
        (lax.rem(view + 2, VIEWS), tile),
        (mate, tile),
    ]
    goes = [tile > 0, tile < TILES - 1, cx > 0, cx < XC - 1, None]
    comes = [tile < TILES - 1, tile > 0, cx < XC - 1, cx > 0, None]

    def when(cond, f):
        if cond is None:
            f()
        else:
            pl.when(cond)(f)

    barrier = pltpu.get_barrier_semaphore()

    def greet(device):
        pl.semaphore_signal(barrier, inc=1, device_id=device, device_id_type=MESH)

    for dx, dz in others:
        greet((at(dx, dz), tile))
    for d in (0, 1):
        when(goes[d], lambda d=d: greet(to_device[d]))

    ROUND = (0, 1, 3, 2)

    def rec_in_copy(i):
        cells = pl.ds(pl.multiple_of(lax.rem(cx + ROUND[i], XC) * CHUNK, LANES), CHUNK)
        return pltpu.make_async_copy(rec_hbm.at[0, :, cells], rec.at[:, cells], in_sem.at[i])

    ker_copy = pltpu.make_async_copy(ker_hbm.at[0], kpad.at[:, :], in_sem.at[4])
    est_copy = pltpu.make_async_copy(est_hbm, est.at[:, pl.ds(CHUNK, YW * Z)], in_sem.at[5])
    ker_copy.start()
    for i in range(4):
        rec_in_copy(i).start()
    est_copy.start()

    def rim_copy(phase, d, src, dst):
        return pltpu.make_async_remote_copy(
            src_ref=src, dst_ref=dst, send_sem=h_s.at[phase, d], recv_sem=h_r.at[phase, d],
            device_id=to_device[d], device_id_type=MESH,
        )

    def volume_rim(phase, d):
        if d == 4:
            return rim_copy(phase, d, rim_send.at[phase], rim_land.at[phase])
        layout = 1 if d < 2 else 0
        if d % 2 == 0:
            return rim_copy(phase, d, grid.at[layout, pl.ds(16, 15)], grid.at[layout, pl.ds(32, 15)])
        return rim_copy(phase, d, grid.at[layout, pl.ds(17, 15)], grid.at[layout, pl.ds(1, 15)])

    def sum_rim(phase, d):
        if d == 4:
            return rim_copy(phase, d, rim_send.at[phase], rim_land.at[phase])
        layout = 1 if d < 2 else 0
        first = 1 if d % 2 == 0 else 32
        return rim_copy(phase, d, total.at[layout, pl.ds(first, 15)], land.at[phase // 2, d])

    def start_rims(make, phase, dirs):
        for d in dirs:
            when(goes[d], lambda d=d: make(phase, d).start())

    def recv_rims(make, phase, dirs):
        for d in dirs:
            when(comes[d], lambda d=d: make(phase, d).wait_recv())

    def sent_rims(make, phase, dirs):
        for d in dirs:
            when(goes[d], lambda d=d: make(phase, d).wait_send())

    def from_view(v, dst, r):
        return pltpu.make_async_remote_copy(
            src_ref=dst, dst_ref=dst, send_sem=r.at[v], recv_sem=r.at[v], device_id=(v, tile), device_id_type=MESH
        )

    def out_to(v, src, dst, s, r):
        return pltpu.make_async_remote_copy(
            src_ref=src, dst_ref=dst, send_sem=s.at[v], recv_sem=r.at[view], device_id=(v, tile), device_id_type=MESH
        )

    def lit_copy(d):
        return pltpu.make_async_remote_copy(
            src_ref=lit_send, dst_ref=lit_got.at[d], send_sem=l_s.at[d], recv_sem=l_r.at[d],
            device_id=to_device[d], device_id_type=MESH,
        )

    ker_copy.wait()
    lane32 = lane_of((32, LANES))
    row32 = lax.broadcasted_iota(jnp.int32, (32, LANES), 0)
    axis_now = det_ref[0].astype(F32)
    lit_now = (lit_ref[0, 0] > 0).astype(F32)
    flags = jnp.where(lane32 < 48, axis_now, lit_now)
    k0 = jnp.concatenate([kpad[:, 0:LANES], jnp.zeros((1, LANES), F32)], axis=0)
    k1 = jnp.concatenate([kpad[:, LANES:Z], jnp.zeros((TAPS, 2 * LANES - Z), F32)], axis=1)
    k1 = jnp.concatenate([k1, jnp.zeros((1, LANES), F32)], axis=0)
    for half in range(2):
        taps = roll(k0, 16) if half == 0 else jnp.where(lane32 < 48, roll(k0, 48), roll(k1, 48))
        taps = jnp.where(row32 == TAPS, flags, taps)
        for i, t in enumerate(pack([taps[8 * j : 8 * j + 8] for j in range(4)])):
            tap_send[half, i] = t
    tap_got[view] = tap_send[deep_half]

    def pack_rows(i):
        rec_in_copy(i).wait()
        rows = lax.rem(cx + ROUND[i], XC)

        def pack_part(part, carry):
            base = pl.multiple_of(rows * CHUNK + part * 4 * Z, LANES)
            tiles = [rec[:, pl.ds(base + LANES * j, LANES)] for j in range(6)]
            one, two = pair_halves(*tiles[:3]), pair_halves(*tiles[3:])
            for half in range(2):
                packed = pack([*one[half], *two[half]])
                for j in range(3):
                    send[rows * 2 + lax.rem(half + odd, 2), part * 3 + j] = packed[j]
            return carry

        lax.fori_loop(0, 4, pack_part, 0)

    def send_block(dx, dz):
        v = at(dx, dz)
        out_to(v, send.at[v], got.at[view], a_s, a_r).start()

    pack_rows(0)
    pl.semaphore_wait(barrier, 7 + (tile > 0).astype(jnp.int32) + (tile < TILES - 1).astype(jnp.int32))
    for dx, dz in others:
        v = at(dx, dz)
        out_to(v, tap_send.at[lax.rem(v + odd, 2)], tap_got.at[view], t_s, t_r).start()
    send_block(0, 1)
    for i in range(1, 4):
        pack_rows(i)
        send_block(ROUND[i], 1)
        send_block(ROUND[i], 0)
    got[view] = send[view]

    zero_rim = jnp.zeros((16, 16, LANES), F32)
    for d, into in ((0, 32), (1, 0)):
        @pl.when(jnp.logical_not(comes[d]))
        def _(d=d, into=into):
            grid[1, into : into + 16] = zero_rim
            lit_got[d] = jnp.zeros((8, LANES), F32)

    for d in range(4):
        @pl.when(jnp.logical_not(comes[d]))
        def _(d=d):
            for i in range(ITERS):
                land[i, d] = zero_rim[:15]

    est[:, 0:CHUNK] = jnp.zeros((CX, CHUNK), F32)
    est[:, CHUNK + YW * Z : 2 * CHUNK + YW * Z] = jnp.zeros((CX, CHUNK), F32)
    est_copy.wait()
    lane16 = lane_of((CX, LANES))
    edge = (lane16 >= jnp.where(upper, 0, RIM)) & (lane16 < jnp.where(upper, RIM + DEPTH, LANES))
    high_half = jnp.broadcast_to(deep_half, (CX, LANES)) == 1

    def est_pair(j, carry):
        base = pl.multiple_of(cx * CHUNK + j * 2 * Z, LANES)
        tiles = [est[:, pl.ds(base + LANES * i, LANES)] for i in range(3)]
        low, high = pair_halves(*tiles)
        for i in range(2):
            grid[0, 2 * j + i] = jnp.where(edge, jnp.where(high_half, high[i], low[i]), 0.0)
        return carry

    lax.fori_loop(8, 16, est_pair, 0)
    centre = grid[0, 16:32]
    grid[1, 16:32] = swap(centre)
    start_rims(volume_rim, 0, (0, 1))
    depth_in[...] = split3(centre.reshape(256, LANES), (0, 0, 1))
    lax.fori_loop(0, 8, est_pair, 0)
    lax.fori_loop(16, 24, est_pair, 0)

    for dx, dz in others:
        v = at(dx, dz)
        from_view(v, tap_got.at[v], t_r).wait_recv()

    def prepare(v, carry):
        taps = jnp.concatenate(unpack([tap_got[v, i] for i in range(3)]), axis=0)
        marks = taps[31:32]
        lane = lane_of((1, LANES))
        axis = jnp.sum(jnp.where(lane == 32, marks, 0.0), axis=1, keepdims=True)
        lit = jnp.sum(jnp.where(lane == 64, marks, 0.0), axis=1, keepdims=True)
        inner = (lane32 >= RIM) & (lane32 < RIM + DEPTH) & (row32 < TAPS)
        taps = jnp.where(inner, taps, 0.0)
        along = [jnp.broadcast_to(jnp.where(axis == float(d), 1.0, 0.0), (1, LANES)) for d in range(3)]
        lit = jnp.broadcast_to(lit, (1, LANES))
        flags_of[v] = jnp.concatenate([along[0], along[1], lit, jnp.zeros((5, LANES), F32)], axis=0)
        lit_send[pl.ds(v, 1)] = lit
        weight[v] = taps * (along[0] + along[1])
        deep = jnp.concatenate([taps * along[2], jnp.zeros((LANES - 32, LANES), F32)], axis=0)
        full = pltpu.roll(jnp.transpose(deep), LANES - HALF, 1, stride=1, stride_axis=0)
        band[v] = split3(full, (0, 1, 0))
        band_t[v] = split3(jnp.transpose(full), (0, 1, 0))
        return carry

    lax.fori_loop(0, VIEWS, prepare, 0)
    for d in (0, 1):
        when(goes[d], lambda d=d: lit_copy(d).start())

    def dot3(a, parts):
        out = jnp.zeros((256, LANES), F32)
        for i in range(3):
            out += jnp.dot(
                a[:, LANES * i : LANES * (i + 1)], parts[:, LANES * i : LANES * (i + 1)], preferred_element_type=F32
            )
        return out.reshape(16, 16, LANES)

    def tap_sum(out, first, count, source, origin, sign, v):
        length = source.shape[0]
        for k in range(TAPS):
            shift = sign * (k - HALF)
            lo = max(first, origin - shift)
            hi = min(first + count, origin + length - shift)
            if lo >= hi:
                continue
            part = source[lo + shift - origin : hi + shift - origin] * weight[v, k : k + 1][None]
            pieces = []
            if lo > first:
                pieces.append(out[: lo - first])
            pieces.append(out[lo - first : hi - first] + part)
            if hi < first + count:
                pieces.append(out[hi - first :])
            out = jnp.concatenate(pieces, axis=0) if len(pieces) > 1 else pieces[0]
        return out

    def along_x(v):
        return jnp.broadcast_to(flags_of[v, 0:1], (8, LANES))

    def in_layout(v, first, count, s):
        return jnp.where(
            (along_x(v) > 0.5)[None],
            grid[1, first : first + count, 8 * s : 8 * s + 8],
            grid[0, first : first + count, 8 * s : 8 * s + 8],
        )

    def blur_inside(v, carry):
        for s in range(2):
            blurred[v, :, 8 * s : 8 * s + 8] = tap_sum(
                jnp.zeros((16, 8, LANES), F32), 0, 16, in_layout(v, 16, 16, s), 0, 1, v
            )
        return carry

    def blur_rims(v, carry):
        deep = dot3(depth_in[...], band_t[v])
        for s in range(2):
            acc = blurred[v, :, 8 * s : 8 * s + 8] + deep[:, 8 * s : 8 * s + 8]
            acc = tap_sum(acc, 0, 16, in_layout(v, 1, 15, s), -15, 1, v)
            blurred[v, :, 8 * s : 8 * s + 8] = tap_sum(acc, 0, 16, in_layout(v, 32, 15, s), 16, 1, v)
        return carry

    lane3 = lane_of((16, 16, LANES))
    inner3 = (lane3 >= RIM) & (lane3 < RIM + DEPTH)

    def spread_rims(v):
        first_dim = jnp.broadcast_to((along_x(v) > 0.5)[None, :1], (16, 16, LANES))
        ratio = jnp.where(inner3, jnp.where(first_dim, rec_in[1, v], rec_in[0, v]) / blurred[v], 0.0)
        blurred[v] = ratio
        x = along_x(v)
        y = jnp.broadcast_to(flags_of[v, 1:2], (8, LANES))
        lit = jnp.broadcast_to(flags_of[v, 2:3], (8, LANES))
        deep = dot3(split3(ratio.reshape(256, LANES), (0, 0, 1)), band[v])
        total[0, 16:32] += deep * lit[:1][None]
        for s in range(2):
            r = ratio[:, 8 * s : 8 * s + 8]
            for first, row in ((-HALF, 1), (16, 0)):
                acc = tap_sum(jnp.zeros((HALF, 8, LANES), F32), first, HALF, r, 0, -1, v)
                cells = slice(first + 16, first + 16 + HALF)
                lit_x = jnp.broadcast_to(lit_got[row, pl.ds(v, 1)], (8, LANES))
                total[1, cells, 8 * s : 8 * s + 8] += acc * (x * lit_x)[None]
                total[0, cells, 8 * s : 8 * s + 8] += acc * (y * lit)[None]

    def spread_inside(v, carry):
        x = along_x(v)
        y = jnp.broadcast_to(flags_of[v, 1:2], (8, LANES))
        lit = jnp.broadcast_to(flags_of[v, 2:3], (8, LANES))
        for s in range(2):
            acc = tap_sum(
                jnp.zeros((16, 8, LANES), F32), 0, 16, blurred[v, :, 8 * s : 8 * s + 8], 0, -1, v
            )
            total[1, 16:32, 8 * s : 8 * s + 8] += acc * (x * lit)[None]
            total[0, 16:32, 8 * s : 8 * s + 8] += acc * (y * lit)[None]
        return carry

    def update(phase):
        for d in range(4):
            layout = 1 if d < 2 else 0
            first = 17 if d % 2 == 0 else 16
            total[layout, first : first + 15] += land[phase // 2, d]
        unlit = jnp.zeros((1, LANES), F32)
        for v in range(VIEWS):
            unlit = unlit + (1.0 - flags_of[v, 2:3])
        rim = unpack_rim(rim_land[phase], jnp.where(upper, 16, 96)).reshape(16, 16, LANES)
        summed = total[0, 16:32] + swap(total[1, 16:32]) + rim + unlit[None]
        return jnp.where(inner3, grid[0, 16:32] * summed * (1.0 / VIEWS), 0.0)

    lax.fori_loop(0, VIEWS, blur_inside, 0)
    recv_rims(volume_rim, 0, (0, 1))
    lax.fori_loop(0, VIEWS, blur_rims, 0)
    for d in (0, 1):
        when(comes[d], lambda d=d: lit_copy(d).wait_recv())

    def arrive(v):
        for part in range(4):
            rows = unpack([got[v, 3 * part + i] for i in range(3)])
            for i in range(4):
                rec_in[0, v, 4 * part + i] = rows[i]
        rec_in[1, v] = swap(rec_in[0, v])

    total[...] = jnp.zeros((2, 48, 16, LANES), F32)
    arrive(view)
    spread_rims(view)

    def spread_arrived(step, carry):
        order = lax.rem(step, 4)
        v = lax.rem(cx + order, XC) * 2 + lax.rem(zh + step // 4, 2)
        from_view(v, got.at[v], a_r).wait_recv()
        arrive(v)
        spread_rims(v)
        return carry

    lax.fori_loop(1, VIEWS, spread_arrived, 0)

    def send_sums(phase):
        start_rims(sum_rim, phase, range(4))
        rim_send[phase] = pack_rim(total[0, 16:32].reshape(256, LANES), jnp.where(upper, 0, 16))
        start_rims(sum_rim, phase, (4,))
        lax.fori_loop(0, VIEWS, spread_inside, 0)
        recv_rims(sum_rim, phase, range(5))

    sent_rims(volume_rim, 0, (0, 1))
    send_sums(1)
    fresh = update(1)
    grid[0, 16:32] = fresh
    start_rims(volume_rim, 2, (2, 3))
    grid[1, 16:32] = swap(fresh)
    start_rims(volume_rim, 2, (0, 1))
    rim_send[2] = pack_rim(fresh.reshape(256, LANES), jnp.where(upper, 112, 32))
    start_rims(volume_rim, 2, (4,))
    sent_rims(sum_rim, 1, range(5))
    total[...] = jnp.zeros((2, 48, 16, LANES), F32)
    lax.fori_loop(0, VIEWS, blur_inside, 0)
    recv_rims(volume_rim, 2, range(5))
    deep_rim = unpack_rim(rim_land[2], jnp.where(upper, 0, 112))
    depth_in[...] = split3(grid[0, 16:32].reshape(256, LANES) + deep_rim, (0, 0, 1))

    def second(v, carry):
        blur_rims(v, 0)
        spread_rims(v)
        return carry

    lax.fori_loop(0, VIEWS, second, 0)
    send_sums(3)
    fresh = update(3)

    for part in range(4):
        packed = pack([fresh[4 * part + i] for i in range(4)])
        for i in range(3):
            gathered[view, 3 * part + i] = packed[i]
    size = PACKED // PIECES

    def half_copy(i, block):
        cells = gathered.at[block, pl.ds(size * i, size)]
        return pltpu.make_async_remote_copy(
            src_ref=cells, dst_ref=cells, send_sem=z_s.at[i], recv_sem=z_r.at[i], device_id=(mate, tile), device_id_type=MESH
        )

    def row_copy(dx, block):
        cells = gathered.at[block]
        return pltpu.make_async_remote_copy(
            src_ref=cells, dst_ref=cells, send_sem=g_s.at[dx - 1], recv_sem=g_r.at[dx - 1],
            device_id=(at(dx, 0), tile), device_id_type=MESH,
        )

    def forward_copy(dx, i, block):
        cells = gathered.at[block, pl.ds(size * i, size)]
        return pltpu.make_async_remote_copy(
            src_ref=cells, dst_ref=cells, send_sem=f_s.at[dx - 1, i], recv_sem=f_r.at[dx - 1, i],
            device_id=(at(dx, 0), tile), device_id_type=MESH,
        )

    for i in range(PIECES):
        half_copy(i, view).start()
    for dx in (1, 3, 2):
        row_copy(dx, view).start()
    for i in range(PIECES):
        half_copy(i, mate).wait_recv()
        for dx in (1, 3, 2):
            forward_copy(dx, i, mate).start()

    def out_copy(i, rows):
        cells = pl.ds(pl.multiple_of(rows * CHUNK, LANES), CHUNK)
        return pltpu.make_async_copy(out.at[:, cells], out_hbm.at[:, cells], out_sem.at[i])

    def unpack_out(i, rows):
        for part in range(4):
            low = unpack([gathered[2 * rows + odd, 3 * part + j] for j in range(3)])
            high = unpack([gathered[2 * rows + 1 - odd, 3 * part + j] for j in range(3)])
            base = pl.multiple_of(rows * CHUNK + part * 4 * Z, LANES)
            for p in range(2):
                for j, t in enumerate(halves_pair(low[2 * p], high[2 * p], low[2 * p + 1], high[2 * p + 1])):
                    out[:, pl.ds(base + LANES * (3 * p + j), LANES)] = t
        out_copy(i, rows).start()

    unpack_out(0, cx)
    for n, dx in enumerate((1, 3, 2)):
        source = at(XC - dx, 0)
        row_copy(dx, source).wait_recv()
        for i in range(PIECES):
            forward_copy(dx, i, at(XC - dx, 1)).wait_recv()
        unpack_out(n + 1, source // 2)

    for d in (0, 1):
        when(goes[d], lambda d=d: lit_copy(d).wait_send())
    for dx, dz in others:
        v = at(dx, dz)
        out_to(v, tap_send.at[0], tap_got.at[view], t_s, t_r).wait_send()
        out_to(v, send.at[v], got.at[view], a_s, a_r).wait_send()
    sent_rims(volume_rim, 2, range(5))
    sent_rims(sum_rim, 3, range(5))
    for i in range(PIECES):
        half_copy(i, view).wait_send()
    for dx in (1, 3, 2):
        row_copy(dx, view).wait_send()
        for i in range(PIECES):
            forward_copy(dx, i, mate).wait_send()
    for i in range(4):
        out_copy(i, cx).wait()


def on_device(estimate, recorded, kernels, illuminated, detection):
    dma = pltpu.SemaphoreType.DMA
    vmem = lambda *shape: pltpu.VMEM(shape, F32)
    any_space = pl.BlockSpec(memory_space=pl.ANY)
    return pl.pallas_call(
        kernel,
        out_shape=jax.ShapeDtypeStruct((CX, YW * Z), F32),
        in_specs=[
            any_space,
            any_space,
            any_space,
            pl.BlockSpec(memory_space=pltpu.SMEM),
            pl.BlockSpec(memory_space=pltpu.SMEM),
        ],
        out_specs=any_space,
        scratch_shapes=[
            vmem(CX, YW * Z + 2 * CHUNK),
            vmem(CX, YW * Z),
            vmem(TAPS, Z),
            vmem(VIEWS, PACKED, CX, LANES),
            vmem(VIEWS, PACKED, CX, LANES),
            vmem(2, 3, 8, LANES),
            vmem(VIEWS, 3, 8, LANES),
            vmem(8, LANES),
            vmem(2, 8, LANES),
            vmem(VIEWS, 8, LANES),
            vmem(VIEWS, 32, LANES),
            pltpu.VMEM((VIEWS, LANES, 3 * LANES), BF16),
            pltpu.VMEM((VIEWS, LANES, 3 * LANES), BF16),
            vmem(2, 48, 16, LANES),
            pltpu.VMEM((256, 3 * LANES), BF16),
            vmem(2, VIEWS, 16, 16, LANES),
            vmem(VIEWS, 16, 16, LANES),
            vmem(2, 48, 16, LANES),
            vmem(ITERS, 4, HALF, 16, LANES),
            vmem(4, 32, LANES),
            vmem(4, 32, LANES),
            vmem(VIEWS, PACKED, CX, LANES),
            vmem(CX, YW * Z),
            dma((6,)),
            dma((4,)),
            dma((VIEWS,)), dma((VIEWS,)),
            dma((VIEWS,)), dma((VIEWS,)),
            dma((2,)), dma((2,)),
            dma((4, 5)), dma((4, 5)),
            dma((3,)), dma((3,)),
            dma((PIECES,)), dma((PIECES,)),
            dma((3, PIECES)), dma((3, PIECES)),
        ],
        compiler_params=pltpu.CompilerParams(
            collective_id=0, has_side_effects=True, vmem_limit_bytes=VMEM_BYTES
        ),
    )(estimate, recorded, kernels, illuminated, detection)


def solution(mesh):
    in_specs = (
        P("tile", None),
        P("view", "tile", None),
        P("view", None, None),
        P("view", "tile"),
        P("view"),
    )
    return jax.shard_map(
        on_device, mesh=mesh, in_specs=in_specs, out_specs=P("tile", None), check_vma=False
    )
```

```python
import jax
import jax.numpy as jnp
from jax import lax
from jax.experimental import pallas as pl
from jax.experimental.pallas import tpu as pltpu
from jax.sharding import PartitionSpec as P


YW = 64
Z = 192
TAPS = 31
HALF = 15
ITERS = 2
VIEWS = 8
XC = 4
TILES = 32
CX = 16
ROWS = 16
DEPTH = 96
LANES = 128
RIM = 16
CHUNK = ROWS * Z
PACKED = 12
PIECES = 4
VMEM_BYTES = 53 * 1024 * 1024
MESH = pl.DeviceIdType.MESH
F32 = jnp.float32
BF16 = jnp.bfloat16


def lane_of(shape):
    return lax.broadcasted_iota(jnp.int32, shape, len(shape) - 1)


def roll(a, shift):
    return pltpu.roll(a, shift, a.ndim - 1)


def pair_halves(t0, t1, t2):
    lane = lane_of(t0.shape)
    a0 = roll(t0, 16)
    a1 = jnp.where(lane < 48, roll(t0, 48), roll(t1, 48))
    b0 = jnp.where(lane < 80, roll(t1, 80), roll(t2, 80))
    b1 = roll(t2, 112)
    return (a0, b0), (a1, b1)


def halves_pair(a0, a1, b0, b1):
    lane = lane_of(a0.shape)
    a1r, b0r = roll(a1, 80), roll(b0, 48)
    t0 = jnp.where(lane < 96, roll(a0, 112), a1r)
    t1 = jnp.where(lane < 64, a1r, b0r)
    t2 = jnp.where(lane < 32, b0r, roll(b1, 16))
    return t0, t1, t2


def pack(rows):
    lane = lane_of(rows[0].shape)
    inner = (lane >= RIM) & (lane < RIM + DEPTH)
    return [jnp.where(inner, rows[i], roll(rows[3], 96 - 32 * i)) for i in range(3)]


def unpack(tiles):
    lane = lane_of(tiles[0].shape)
    r = [roll(tiles[i], 32 + 32 * i) for i in range(3)]
    return [tiles[0], tiles[1], tiles[2], jnp.where(lane < 48, r[0], jnp.where(lane < 80, r[1], r[2]))]


def swap(a):
    return jnp.swapaxes(a, 0, 1)


def pack_rim(a, shift):
    lane = lane_of((32, LANES))
    out = jnp.zeros((32, LANES), F32)
    for g in range(8):
        moved = roll(a[32 * g : 32 * g + 32], lax.rem(shift + 16 * g, 128))
        out = jnp.where((lane >= 16 * g) & (lane < 16 * g + 16), moved, out)
    return out


def unpack_rim(p, first):
    lane = lane_of((32, LANES))
    keep = (lane >= first) & (lane < first + 16)
    return jnp.concatenate(
        [jnp.where(keep, roll(p, lax.rem(first + 128 - 16 * g, 128)), 0.0) for g in range(8)], axis=0
    )


def split3(a, order):
    high = a.astype(BF16)
    low = (a - high.astype(F32)).astype(BF16)
    return jnp.concatenate([(high, low)[i] for i in order], axis=-1)


def kernel(
    est_hbm, rec_hbm, ker_hbm, lit_ref, det_ref, out,
    est, rec, kpad, send, got, tap_send, tap_got, lit_send, lit_got, flags_of,
    weight, band, band_t, grid, depth_in, rec_in, blurred, total, land, rim_send, rim_land, gathered,
    in_sem, a_s, a_r, t_s, t_r, l_s, l_r, h_s, h_r, g_s, g_r, z_s, z_r, f_s, f_r,
):
    view = lax.axis_index("view")
    tile = lax.axis_index("tile")
    cx, zh = view // 2, lax.rem(view, 2)
    odd = lax.rem(tile // 8, 2)
    deep_half = lax.rem(zh + odd, 2)
    upper = deep_half == 1

    def at(dx, dz):
        return lax.rem(cx + dx, XC) * 2 + lax.rem(zh + dz, 2)

    mate = at(0, 1)
    others = [(0, 1), (1, 1), (1, 0), (3, 1), (3, 0), (2, 1), (2, 0)]

    to_device = [
        (jnp.where(lax.rem(tile, 8) == 0, mate, view), lax.rem(tile + TILES - 1, TILES)),
        (jnp.where(lax.rem(tile, 8) == 7, mate, view), lax.rem(tile + 1, TILES)),
        (lax.rem(view + VIEWS - 2, VIEWS), tile),
        (lax.rem(view + 2, VIEWS), tile),
        (mate, tile),
    ]
    goes = [tile > 0, tile < TILES - 1, cx > 0, cx < XC - 1, None]
    comes = [tile < TILES - 1, tile > 0, cx < XC - 1, cx > 0, None]

    def when(cond, f):
        if cond is None:
            f()
        else:
            pl.when(cond)(f)

    barrier = pltpu.get_barrier_semaphore()

    def greet(device):
        pl.semaphore_signal(barrier, inc=1, device_id=device, device_id_type=MESH)

    for dx, dz in others:
        greet((at(dx, dz), tile))
    for d in (0, 1):
        when(goes[d], lambda d=d: greet(to_device[d]))

    ROUND = (0, 1, 3, 2)

    def rec_in_copy(i):
        cells = pl.ds(pl.multiple_of(lax.rem(cx + ROUND[i], XC) * CHUNK, LANES), CHUNK)
        return pltpu.make_async_copy(rec_hbm.at[0, :, cells], rec.at[:, cells], in_sem.at[i])

    ker_copy = pltpu.make_async_copy(ker_hbm, kpad, in_sem.at[4])
    est_copy = pltpu.make_async_copy(est_hbm, est.at[:, pl.ds(CHUNK, YW * Z)], in_sem.at[5])
    ker_copy.start()
    for i in range(4):
        rec_in_copy(i).start()
    est_copy.start()

    def rim_copy(phase, d, src, dst):
        return pltpu.make_async_remote_copy(
            src_ref=src, dst_ref=dst, send_sem=h_s.at[phase, d], recv_sem=h_r.at[phase, d],
            device_id=to_device[d], device_id_type=MESH,
        )

    def volume_rim(phase, d):
        if d == 4:
            return rim_copy(phase, d, rim_send.at[phase], rim_land.at[phase])
        layout = 1 if d < 2 else 0
        if d % 2 == 0:
            return rim_copy(phase, d, grid.at[layout, pl.ds(16, 15)], grid.at[layout, pl.ds(32, 15)])
        return rim_copy(phase, d, grid.at[layout, pl.ds(17, 15)], grid.at[layout, pl.ds(1, 15)])

    def sum_rim(phase, d):
        if d == 4:
            return rim_copy(phase, d, rim_send.at[phase], rim_land.at[phase])
        layout = 1 if d < 2 else 0
        first = 1 if d % 2 == 0 else 32
        return rim_copy(phase, d, total.at[layout, pl.ds(first, 15)], land.at[phase // 2, d])

    def start_rims(make, phase, dirs):
        for d in dirs:
            when(goes[d], lambda d=d: make(phase, d).start())

    def recv_rims(make, phase, dirs):
        for d in dirs:
            when(comes[d], lambda d=d: make(phase, d).wait_recv())

    def sent_rims(make, phase, dirs):
        for d in dirs:
            when(goes[d], lambda d=d: make(phase, d).wait_send())

    def from_view(v, dst, r):
        return pltpu.make_async_remote_copy(
            src_ref=dst, dst_ref=dst, send_sem=r.at[v], recv_sem=r.at[v], device_id=(v, tile), device_id_type=MESH
        )

    def out_to(v, src, dst, s, r):
        return pltpu.make_async_remote_copy(
            src_ref=src, dst_ref=dst, send_sem=s.at[v], recv_sem=r.at[view], device_id=(v, tile), device_id_type=MESH
        )

    def lit_copy(d):
        return pltpu.make_async_remote_copy(
            src_ref=lit_send, dst_ref=lit_got.at[d], send_sem=l_s.at[d], recv_sem=l_r.at[d],
            device_id=to_device[d], device_id_type=MESH,
        )

    ker_copy.wait()
    lane32 = lane_of((32, LANES))
    row32 = lax.broadcasted_iota(jnp.int32, (32, LANES), 0)
    axis_now = det_ref[0].astype(F32)
    lit_now = (lit_ref[0, 0] > 0).astype(F32)
    flags = jnp.where(lane32 < 48, axis_now, lit_now)
    k0 = jnp.concatenate([kpad[:, 0, 0:LANES], jnp.zeros((1, LANES), F32)], axis=0)
    k1 = jnp.concatenate([kpad[:, 0, LANES:Z], jnp.zeros((TAPS, 2 * LANES - Z), F32)], axis=1)
    k1 = jnp.concatenate([k1, jnp.zeros((1, LANES), F32)], axis=0)
    for half in range(2):
        taps = roll(k0, 16) if half == 0 else jnp.where(lane32 < 48, roll(k0, 48), roll(k1, 48))
        taps = jnp.where(row32 == TAPS, flags, taps)
        for i, t in enumerate(pack([taps[8 * j : 8 * j + 8] for j in range(4)])):
            tap_send[half, i] = t
    tap_got[view] = tap_send[deep_half]

    def pack_rows(i):
        rec_in_copy(i).wait()
        rows = lax.rem(cx + ROUND[i], XC)

        def pack_part(part, carry):
            base = pl.multiple_of(rows * CHUNK + part * 4 * Z, LANES)
            tiles = [rec[:, pl.ds(base + LANES * j, LANES)] for j in range(6)]
            one, two = pair_halves(*tiles[:3]), pair_halves(*tiles[3:])
            for half in range(2):
                packed = pack([*one[half], *two[half]])
                for j in range(3):
                    send[rows * 2 + lax.rem(half + odd, 2), part * 3 + j] = packed[j]
            return carry

        lax.fori_loop(0, 4, pack_part, 0)

    def send_block(dx, dz):
        v = at(dx, dz)
        out_to(v, send.at[v], got.at[view], a_s, a_r).start()

    pack_rows(0)
    pl.semaphore_wait(barrier, 7 + (tile > 0).astype(jnp.int32) + (tile < TILES - 1).astype(jnp.int32))
    for dx, dz in others:
        v = at(dx, dz)
        out_to(v, tap_send.at[lax.rem(v + odd, 2)], tap_got.at[view], t_s, t_r).start()
    send_block(0, 1)
    pack_rows(1)
    send_block(ROUND[1], 1)
    send_block(ROUND[1], 0)
    for i in range(2, 4):
        pack_rows(i)
        send_block(ROUND[i], 0)
    got[view] = send[view]

    zero_rim = jnp.zeros((16, 16, LANES), F32)
    for d, into in ((0, 32), (1, 0)):
        @pl.when(jnp.logical_not(comes[d]))
        def _(d=d, into=into):
            grid[1, into : into + 16] = zero_rim
            lit_got[d] = jnp.zeros((8, LANES), F32)

    for d in range(4):
        @pl.when(jnp.logical_not(comes[d]))
        def _(d=d):
            for i in range(ITERS):
                land[i, d] = zero_rim[:15]

    est[:, 0:CHUNK] = jnp.zeros((CX, CHUNK), F32)
    est[:, CHUNK + YW * Z : 2 * CHUNK + YW * Z] = jnp.zeros((CX, CHUNK), F32)
    est_copy.wait()
    lane16 = lane_of((CX, LANES))
    edge = (lane16 >= jnp.where(upper, 0, RIM)) & (lane16 < jnp.where(upper, RIM + DEPTH, LANES))
    high_half = jnp.broadcast_to(deep_half, (CX, LANES)) == 1

    def est_pair(j, carry):
        base = pl.multiple_of(cx * CHUNK + j * 2 * Z, LANES)
        tiles = [est[:, pl.ds(base + LANES * i, LANES)] for i in range(3)]
        low, high = pair_halves(*tiles)
        for i in range(2):
            grid[0, 2 * j + i] = jnp.where(edge, jnp.where(high_half, high[i], low[i]), 0.0)
        return carry

    def block_left(dx, dz):
        v = at(dx, dz)
        out_to(v, send.at[v], got.at[view], a_s, a_r).wait_send()

    lax.fori_loop(8, 16, est_pair, 0)
    block_left(0, 1)
    send_block(ROUND[2], 1)
    centre = grid[0, 16:32]
    grid[1, 16:32] = swap(centre)
    start_rims(volume_rim, 0, (0, 1))
    depth_in[...] = split3(centre.reshape(256, LANES), (0, 0, 1))
    lax.fori_loop(0, 8, est_pair, 0)
    lax.fori_loop(16, 24, est_pair, 0)

    for dx, dz in others:
        v = at(dx, dz)
        from_view(v, tap_got.at[v], t_r).wait_recv()

    def prepare(v, carry):
        taps = jnp.concatenate(unpack([tap_got[v, i] for i in range(3)]), axis=0)
        marks = taps[31:32]
        lane = lane_of((1, LANES))
        axis = jnp.sum(jnp.where(lane == 32, marks, 0.0), axis=1, keepdims=True)
        lit = jnp.sum(jnp.where(lane == 64, marks, 0.0), axis=1, keepdims=True)
        inner = (lane32 >= RIM) & (lane32 < RIM + DEPTH) & (row32 < TAPS)
        taps = jnp.where(inner, taps, 0.0)
        along = [jnp.broadcast_to(jnp.where(axis == float(d), 1.0, 0.0), (1, LANES)) for d in range(3)]
        lit = jnp.broadcast_to(lit, (1, LANES))
        flags_of[v] = jnp.concatenate([along[0], along[1], lit, jnp.zeros((5, LANES), F32)], axis=0)
        lit_send[pl.ds(v, 1)] = lit
        weight[v] = taps * (along[0] + along[1])
        deep = jnp.concatenate([taps * along[2], jnp.zeros((LANES - 32, LANES), F32)], axis=0)
        full = pltpu.roll(jnp.transpose(deep), LANES - HALF, 1, stride=1, stride_axis=0)
        band[v] = split3(full, (0, 1, 0))
        band_t[v] = split3(jnp.transpose(full), (0, 1, 0))
        return carry

    lax.fori_loop(0, VIEWS, prepare, 0)
    block_left(ROUND[1], 1)
    send_block(ROUND[3], 1)
    for d in (0, 1):
        when(goes[d], lambda d=d: lit_copy(d).start())

    def dot3(a, parts):
        out = jnp.zeros((256, LANES), F32)
        for i in range(3):
            out += jnp.dot(
                a[:, LANES * i : LANES * (i + 1)], parts[:, LANES * i : LANES * (i + 1)], preferred_element_type=F32
            )
        return out.reshape(16, 16, LANES)

    def tap_sum(out, first, count, source, origin, sign, v):
        length = source.shape[0]
        for k in range(TAPS):
            shift = sign * (k - HALF)
            lo = max(first, origin - shift)
            hi = min(first + count, origin + length - shift)
            if lo >= hi:
                continue
            part = source[lo + shift - origin : hi + shift - origin] * weight[v, k : k + 1][None]
            pieces = []
            if lo > first:
                pieces.append(out[: lo - first])
            pieces.append(out[lo - first : hi - first] + part)
            if hi < first + count:
                pieces.append(out[hi - first :])
            out = jnp.concatenate(pieces, axis=0) if len(pieces) > 1 else pieces[0]
        return out

    def along_x(v):
        return jnp.broadcast_to(flags_of[v, 0:1], (8, LANES))

    def in_layout(v, first, count, s):
        return jnp.where(
            (along_x(v) > 0.5)[None],
            grid[1, first : first + count, 8 * s : 8 * s + 8],
            grid[0, first : first + count, 8 * s : 8 * s + 8],
        )

    def blur_inside(v, carry):
        for s in range(2):
            blurred[v, :, 8 * s : 8 * s + 8] = tap_sum(
                jnp.zeros((16, 8, LANES), F32), 0, 16, in_layout(v, 16, 16, s), 0, 1, v
            )
        return carry

    def blur_rims(v, carry):
        deep = dot3(depth_in[...], band_t[v])
        for s in range(2):
            acc = tap_sum(blurred[v, :, 8 * s : 8 * s + 8], 0, 16, in_layout(v, 1, 15, s), -15, 1, v)
            acc = tap_sum(acc, 0, 16, in_layout(v, 32, 15, s), 16, 1, v)
            blurred[v, :, 8 * s : 8 * s + 8] = acc + deep[:, 8 * s : 8 * s + 8]
        return carry

    lane3 = lane_of((16, 16, LANES))
    inner3 = (lane3 >= RIM) & (lane3 < RIM + DEPTH)

    def spread_rims(v):
        first_dim = jnp.broadcast_to((along_x(v) > 0.5)[None, :1], (16, 16, LANES))
        ratio = jnp.where(inner3, jnp.where(first_dim, rec_in[1, v], rec_in[0, v]) / blurred[v], 0.0)
        blurred[v] = ratio
        x = along_x(v)
        y = jnp.broadcast_to(flags_of[v, 1:2], (8, LANES))
        lit = jnp.broadcast_to(flags_of[v, 2:3], (8, LANES))
        deep = dot3(split3(ratio.reshape(256, LANES), (0, 0, 1)), band[v])
        for s in range(2):
            r = ratio[:, 8 * s : 8 * s + 8]
            for first, row in ((-HALF, 1), (16, 0)):
                acc = tap_sum(jnp.zeros((HALF, 8, LANES), F32), first, HALF, r, 0, -1, v)
                cells = slice(first + 16, first + 16 + HALF)
                lit_x = jnp.broadcast_to(lit_got[row, pl.ds(v, 1)], (8, LANES))
                total[1, cells, 8 * s : 8 * s + 8] += acc * (x * lit_x)[None]
                total[0, cells, 8 * s : 8 * s + 8] += acc * (y * lit)[None]
        total[0, 16:32] += deep * lit[:1][None]

    def spread_inside(v, carry):
        x = along_x(v)
        y = jnp.broadcast_to(flags_of[v, 1:2], (8, LANES))
        lit = jnp.broadcast_to(flags_of[v, 2:3], (8, LANES))
        for s in range(2):
            acc = tap_sum(
                jnp.zeros((16, 8, LANES), F32), 0, 16, blurred[v, :, 8 * s : 8 * s + 8], 0, -1, v
            )
            total[1, 16:32, 8 * s : 8 * s + 8] += acc * (x * lit)[None]
            total[0, 16:32, 8 * s : 8 * s + 8] += acc * (y * lit)[None]
        return carry

    def update(phase):
        for d in range(4):
            layout = 1 if d < 2 else 0
            first = 17 if d % 2 == 0 else 16
            total[layout, first : first + 15] += land[phase // 2, d]
        unlit = jnp.zeros((1, LANES), F32)
        for v in range(VIEWS):
            unlit = unlit + (1.0 - flags_of[v, 2:3])
        rim = unpack_rim(rim_land[phase], jnp.where(upper, 16, 96)).reshape(16, 16, LANES)
        summed = total[0, 16:32] + swap(total[1, 16:32]) + rim + unlit[None]
        return jnp.where(inner3, grid[0, 16:32] * summed * (1.0 / VIEWS), 0.0)

    lax.fori_loop(0, VIEWS, blur_inside, 0)
    recv_rims(volume_rim, 0, (0, 1))
    lax.fori_loop(0, VIEWS, blur_rims, 0)
    for d in (0, 1):
        when(comes[d], lambda d=d: lit_copy(d).wait_recv())

    def arrive(v):
        for part in range(4):
            rows = unpack([got[v, 3 * part + i] for i in range(3)])
            for i in range(4):
                rec_in[0, v, 4 * part + i] = rows[i]
        rec_in[1, v] = swap(rec_in[0, v])

    total[...] = jnp.zeros((2, 48, 16, LANES), F32)
    arrive(view)
    spread_rims(view)

    def spread_arrived(step, carry):
        order = lax.rem(step, 4)
        v = lax.rem(cx + order, XC) * 2 + lax.rem(zh + step // 4, 2)
        from_view(v, got.at[v], a_r).wait_recv()
        arrive(v)
        spread_rims(v)
        return carry

    lax.fori_loop(1, VIEWS, spread_arrived, 0)

    def send_sums(phase):
        start_rims(sum_rim, phase, (2, 3, 0, 1))
        rim_send[phase] = pack_rim(total[0, 16:32].reshape(256, LANES), jnp.where(upper, 0, 16))
        start_rims(sum_rim, phase, (4,))
        lax.fori_loop(0, VIEWS, spread_inside, 0)
        recv_rims(sum_rim, phase, range(5))

    sent_rims(volume_rim, 0, (0, 1))
    send_sums(1)
    fresh = update(1)
    grid[0, 16:32] = fresh
    start_rims(volume_rim, 2, (2, 3))
    grid[1, 16:32] = swap(fresh)
    start_rims(volume_rim, 2, (0, 1))
    rim_send[2] = pack_rim(fresh.reshape(256, LANES), jnp.where(upper, 112, 32))
    start_rims(volume_rim, 2, (4,))
    sent_rims(sum_rim, 1, range(5))
    total[...] = jnp.zeros((2, 48, 16, LANES), F32)
    lax.fori_loop(0, VIEWS, blur_inside, 0)
    recv_rims(volume_rim, 2, range(5))
    deep_rim = unpack_rim(rim_land[2], jnp.where(upper, 0, 112))
    depth_in[...] = split3(grid[0, 16:32].reshape(256, LANES) + deep_rim, (0, 0, 1))

    def second(v, carry):
        blur_rims(v, 0)
        spread_rims(v)
        return carry

    lax.fori_loop(0, VIEWS, second, 0)
    send_sums(3)
    fresh = update(3)

    for part in range(4):
        packed = pack([fresh[4 * part + i] for i in range(4)])
        for i in range(3):
            gathered[view, 3 * part + i] = packed[i]
    size = PACKED // PIECES

    def half_copy(i, block):
        cells = gathered.at[block, pl.ds(size * i, size)]
        return pltpu.make_async_remote_copy(
            src_ref=cells, dst_ref=cells, send_sem=z_s.at[i], recv_sem=z_r.at[i], device_id=(mate, tile), device_id_type=MESH
        )

    def row_copy(dx, block):
        cells = gathered.at[block]
        return pltpu.make_async_remote_copy(
            src_ref=cells, dst_ref=cells, send_sem=g_s.at[dx - 1], recv_sem=g_r.at[dx - 1],
            device_id=(at(dx, 0), tile), device_id_type=MESH,
        )

    def forward_copy(dx, i, block):
        cells = gathered.at[block, pl.ds(size * i, size)]
        return pltpu.make_async_remote_copy(
            src_ref=cells, dst_ref=cells, send_sem=f_s.at[dx - 1, i], recv_sem=f_r.at[dx - 1, i],
            device_id=(at(dx, 0), tile), device_id_type=MESH,
        )

    for i in range(PIECES):
        half_copy(i, view).start()
    for dx in (1, 3, 2):
        row_copy(dx, view).start()
    for i in range(PIECES):
        half_copy(i, mate).wait_recv()
        for dx in (1, 3, 2):
            forward_copy(dx, i, mate).start()

    def unpack_out(rows):
        for part in range(4):
            low = unpack([gathered[2 * rows + odd, 3 * part + j] for j in range(3)])
            high = unpack([gathered[2 * rows + 1 - odd, 3 * part + j] for j in range(3)])
            base = pl.multiple_of(rows * CHUNK + part * 4 * Z, LANES)
            for p in range(2):
                for j, t in enumerate(halves_pair(low[2 * p], high[2 * p], low[2 * p + 1], high[2 * p + 1])):
                    out[:, pl.ds(base + LANES * (3 * p + j), LANES)] = t

    unpack_out(cx)
    for dx in (1, 3, 2):
        source = at(XC - dx, 0)
        row_copy(dx, source).wait_recv()
        for i in range(PIECES):
            forward_copy(dx, i, at(XC - dx, 1)).wait_recv()
        unpack_out(source // 2)

    for d in (0, 1):
        when(goes[d], lambda d=d: lit_copy(d).wait_send())
    for dx, dz in others:
        v = at(dx, dz)
        out_to(v, tap_send.at[0], tap_got.at[view], t_s, t_r).wait_send()
        if (dx, dz) not in ((0, 1), (ROUND[1], 1)):
            block_left(dx, dz)
    sent_rims(volume_rim, 2, range(5))
    sent_rims(sum_rim, 3, range(5))
    for i in range(PIECES):
        half_copy(i, view).wait_send()
    for dx in (1, 3, 2):
        row_copy(dx, view).wait_send()
        for i in range(PIECES):
            forward_copy(dx, i, mate).wait_send()


def on_device(estimate, recorded, kernels, illuminated, detection):
    dma = pltpu.SemaphoreType.DMA
    vmem = lambda *shape: pltpu.VMEM(shape, F32)
    any_space = pl.BlockSpec(memory_space=pltpu.HBM)
    return pl.pallas_call(
        kernel,
        out_shape=jax.ShapeDtypeStruct((CX, YW * Z), F32),
        in_specs=[
            any_space,
            any_space,
            any_space,
            pl.BlockSpec(memory_space=pltpu.SMEM),
            pl.BlockSpec(memory_space=pltpu.SMEM),
        ],
        out_specs=pl.BlockSpec(memory_space=pltpu.VMEM),
        scratch_shapes=[
            vmem(CX, YW * Z + 2 * CHUNK),
            vmem(CX, YW * Z),
            vmem(TAPS, 1, Z),
            vmem(VIEWS, PACKED, CX, LANES),
            vmem(VIEWS, PACKED, CX, LANES),
            vmem(2, 3, 8, LANES),
            vmem(VIEWS, 3, 8, LANES),
            vmem(8, LANES),
            vmem(2, 8, LANES),
            vmem(VIEWS, 8, LANES),
            vmem(VIEWS, 32, LANES),
            pltpu.VMEM((VIEWS, LANES, 3 * LANES), BF16),
            pltpu.VMEM((VIEWS, LANES, 3 * LANES), BF16),
            vmem(2, 48, 16, LANES),
            pltpu.VMEM((256, 3 * LANES), BF16),
            vmem(2, VIEWS, 16, 16, LANES),
            vmem(VIEWS, 16, 16, LANES),
            vmem(2, 48, 16, LANES),
            vmem(ITERS, 4, HALF, 16, LANES),
            vmem(4, 32, LANES),
            vmem(4, 32, LANES),
            vmem(VIEWS, PACKED, CX, LANES),
            dma((6,)),
            dma((VIEWS,)), dma((VIEWS,)),
            dma((VIEWS,)), dma((VIEWS,)),
            dma((2,)), dma((2,)),
            dma((4, 5)), dma((4, 5)),
            dma((3,)), dma((3,)),
            dma((PIECES,)), dma((PIECES,)),
            dma((3, PIECES)), dma((3, PIECES)),
        ],
        compiler_params=pltpu.CompilerParams(
            collective_id=0, has_side_effects=True, vmem_limit_bytes=VMEM_BYTES
        ),
    )(estimate, recorded, jnp.swapaxes(kernels, 0, 1), illuminated, detection)


def solution(mesh):
    in_specs = (
        P("tile", None),
        P("view", "tile", None),
        P("view", None, None),
        P("view", "tile"),
        P("view"),
    )
    return jax.shard_map(
        on_device, mesh=mesh, in_specs=in_specs, out_specs=P("tile", None), check_vma=False
    )
```

```python
import jax
import jax.numpy as jnp
from jax import lax
from jax.experimental import pallas as pl
from jax.experimental.pallas import tpu as pltpu
from jax.sharding import PartitionSpec as P


YW = 64
Z = 192
TAPS = 31
HALF = 15
ITERS = 2
VIEWS = 8
XC = 4
TILES = 32
CX = 16
ROWS = 16
DEPTH = 96
LANES = 128
RIM = 16
CHUNK = ROWS * Z
PACKED = 12
PIECES = 4
VMEM_BYTES = 53 * 1024 * 1024
MESH = pl.DeviceIdType.MESH
F32 = jnp.float32
BF16 = jnp.bfloat16


def lane_of(shape):
    return lax.broadcasted_iota(jnp.int32, shape, len(shape) - 1)


def roll(a, shift):
    return pltpu.roll(a, shift, a.ndim - 1)


def pair_halves(t0, t1, t2):
    lane = lane_of(t0.shape)
    a0 = roll(t0, 16)
    a1 = jnp.where(lane < 48, roll(t0, 48), roll(t1, 48))
    b0 = jnp.where(lane < 80, roll(t1, 80), roll(t2, 80))
    b1 = roll(t2, 112)
    return (a0, b0), (a1, b1)


def halves_pair(a0, a1, b0, b1):
    lane = lane_of(a0.shape)
    a1r, b0r = roll(a1, 80), roll(b0, 48)
    t0 = jnp.where(lane < 96, roll(a0, 112), a1r)
    t1 = jnp.where(lane < 64, a1r, b0r)
    t2 = jnp.where(lane < 32, b0r, roll(b1, 16))
    return t0, t1, t2


def pack(rows):
    lane = lane_of(rows[0].shape)
    inner = (lane >= RIM) & (lane < RIM + DEPTH)
    return [jnp.where(inner, rows[i], roll(rows[3], 96 - 32 * i)) for i in range(3)]


def unpack(tiles):
    lane = lane_of(tiles[0].shape)
    r = [roll(tiles[i], 32 + 32 * i) for i in range(3)]
    return [tiles[0], tiles[1], tiles[2], jnp.where(lane < 48, r[0], jnp.where(lane < 80, r[1], r[2]))]


def swap(a):
    return jnp.swapaxes(a, 0, 1)


def pack_rim(a, shift):
    lane = lane_of((32, LANES))
    out = jnp.zeros((32, LANES), F32)
    for g in range(8):
        moved = roll(a[32 * g : 32 * g + 32], lax.rem(shift + 16 * g, 128))
        out = jnp.where((lane >= 16 * g) & (lane < 16 * g + 16), moved, out)
    return out


def unpack_rim(p, first):
    lane = lane_of((32, LANES))
    keep = (lane >= first) & (lane < first + 16)
    return jnp.concatenate(
        [jnp.where(keep, roll(p, lax.rem(first + 128 - 16 * g, 128)), 0.0) for g in range(8)], axis=0
    )


def parts_of(a, order):
    high = a.astype(BF16)
    low = (a - high.astype(F32)).astype(BF16)
    return [(high, low)[i] for i in order]


def split3(a):
    return jnp.concatenate(parts_of(a, (0, 0, 1)), axis=-1)


def kernel(
    est_hbm, rec_hbm, ker_hbm, lit_ref, det_ref, out,
    est, rec, kpad, send, got, tap_send, tap_got, lit_send, lit_got, flags_of,
    weight, band, band_t, grid, depth_in, deep, ratios, rec_in, blurred, total, land, rim_send, rim_land, gathered,
    in_sem, a_s, a_r, t_s, t_r, l_s, l_r, h_s, h_r, g_s, g_r, z_s, z_r, f_s, f_r,
):
    view = lax.axis_index("view")
    tile = lax.axis_index("tile")
    cx, zh = view // 2, lax.rem(view, 2)
    odd = lax.rem(tile // 8, 2)
    deep_half = lax.rem(zh + odd, 2)
    upper = deep_half == 1

    def at(dx, dz):
        return lax.rem(cx + dx, XC) * 2 + lax.rem(zh + dz, 2)

    mate = at(0, 1)
    others = [(0, 1), (1, 1), (1, 0), (3, 1), (3, 0), (2, 1), (2, 0)]

    to_device = [
        (jnp.where(lax.rem(tile, 8) == 0, mate, view), lax.rem(tile + TILES - 1, TILES)),
        (jnp.where(lax.rem(tile, 8) == 7, mate, view), lax.rem(tile + 1, TILES)),
        (lax.rem(view + VIEWS - 2, VIEWS), tile),
        (lax.rem(view + 2, VIEWS), tile),
        (mate, tile),
    ]
    goes = [tile > 0, tile < TILES - 1, cx > 0, cx < XC - 1, None]
    comes = [tile < TILES - 1, tile > 0, cx < XC - 1, cx > 0, None]

    def when(cond, f):
        if cond is None:
            f()
        else:
            pl.when(cond)(f)

    barrier = pltpu.get_barrier_semaphore()

    def greet(device):
        pl.semaphore_signal(barrier, inc=1, device_id=device, device_id_type=MESH)

    for dx, dz in others:
        greet((at(dx, dz), tile))
    for d in (0, 1):
        when(goes[d], lambda d=d: greet(to_device[d]))

    ROUND = (0, 1, 3, 2)

    def rec_in_copy(i):
        cells = pl.ds(pl.multiple_of(lax.rem(cx + ROUND[i], XC) * CHUNK, LANES), CHUNK)
        return pltpu.make_async_copy(rec_hbm.at[0, :, cells], rec.at[:, cells], in_sem.at[i])

    ker_copy = pltpu.make_async_copy(ker_hbm, kpad, in_sem.at[4])
    est_copy = pltpu.make_async_copy(est_hbm, est.at[:, pl.ds(CHUNK, YW * Z)], in_sem.at[5])
    ker_copy.start()
    for i in range(4):
        rec_in_copy(i).start()
    est_copy.start()

    def rim_copy(phase, d, src, dst, half=0):
        return pltpu.make_async_remote_copy(
            src_ref=src, dst_ref=dst, send_sem=h_s.at[phase, d, half], recv_sem=h_r.at[phase, d, half],
            device_id=to_device[d], device_id_type=MESH,
        )

    def volume_rim(phase, d):
        layout = 1 if d < 2 else 0
        if d % 2 == 0:
            return rim_copy(phase, d, grid.at[layout, pl.ds(16, 15)], grid.at[layout, pl.ds(32, 15)])
        return rim_copy(phase, d, grid.at[layout, pl.ds(17, 15)], grid.at[layout, pl.ds(1, 15)])

    def sum_rim(half):
        def make(phase, d):
            layout = 1 if d < 2 else 0
            first = 1 if d % 2 == 0 else 32
            part = pl.ds(8 * half, 8)
            return rim_copy(
                phase, d, total.at[layout, pl.ds(first, 15), part], land.at[phase // 2, d, :, part], half
            )

        return make

    def depth_rim(phase, d):
        return rim_copy(phase, d, rim_send.at[phase], rim_land.at[phase])

    def start_rims(make, phase, dirs):
        for d in dirs:
            when(goes[d], lambda d=d: make(phase, d).start())

    def recv_rims(make, phase, dirs):
        for d in dirs:
            when(comes[d], lambda d=d: make(phase, d).wait_recv())

    def sent_rims(make, phase, dirs):
        for d in dirs:
            when(goes[d], lambda d=d: make(phase, d).wait_send())

    def from_view(v, dst, r):
        return pltpu.make_async_remote_copy(
            src_ref=dst, dst_ref=dst, send_sem=r.at[v], recv_sem=r.at[v], device_id=(v, tile), device_id_type=MESH
        )

    def out_to(v, src, dst, s, r):
        return pltpu.make_async_remote_copy(
            src_ref=src, dst_ref=dst, send_sem=s.at[v], recv_sem=r.at[view], device_id=(v, tile), device_id_type=MESH
        )

    def lit_copy(d):
        return pltpu.make_async_remote_copy(
            src_ref=lit_send, dst_ref=lit_got.at[d], send_sem=l_s.at[d], recv_sem=l_r.at[d],
            device_id=to_device[d], device_id_type=MESH,
        )

    ker_copy.wait()
    lane32 = lane_of((32, LANES))
    row32 = lax.broadcasted_iota(jnp.int32, (32, LANES), 0)
    axis_now = det_ref[0].astype(F32)
    lit_now = (lit_ref[0, 0] > 0).astype(F32)
    flags = jnp.where(lane32 < 48, axis_now, lit_now)
    k0 = jnp.concatenate([kpad[:, 0, 0:LANES], jnp.zeros((1, LANES), F32)], axis=0)
    k1 = jnp.concatenate([kpad[:, 0, LANES:Z], jnp.zeros((TAPS, 2 * LANES - Z), F32)], axis=1)
    k1 = jnp.concatenate([k1, jnp.zeros((1, LANES), F32)], axis=0)
    for half in range(2):
        taps = roll(k0, 16) if half == 0 else jnp.where(lane32 < 48, roll(k0, 48), roll(k1, 48))
        taps = jnp.where(row32 == TAPS, flags, taps)
        for i, t in enumerate(pack([taps[8 * j : 8 * j + 8] for j in range(4)])):
            tap_send[half, i] = t
    tap_got[view] = tap_send[deep_half]

    def pack_rows(i):
        rec_in_copy(i).wait()
        rows = lax.rem(cx + ROUND[i], XC)

        def pack_part(part, carry):
            base = pl.multiple_of(rows * CHUNK + part * 4 * Z, LANES)
            tiles = [rec[:, pl.ds(base + LANES * j, LANES)] for j in range(6)]
            one, two = pair_halves(*tiles[:3]), pair_halves(*tiles[3:])
            for half in range(2):
                packed = pack([*one[half], *two[half]])
                for j in range(3):
                    send[rows * 2 + lax.rem(half + odd, 2), part * 3 + j] = packed[j]
            return carry

        lax.fori_loop(0, 4, pack_part, 0)

    def send_block(dx, dz):
        v = at(dx, dz)
        out_to(v, send.at[v], got.at[view], a_s, a_r).start()

    pack_rows(0)
    pl.semaphore_wait(barrier, 7 + (tile > 0).astype(jnp.int32) + (tile < TILES - 1).astype(jnp.int32))
    for dx, dz in others:
        v = at(dx, dz)
        out_to(v, tap_send.at[lax.rem(v + odd, 2)], tap_got.at[view], t_s, t_r).start()
    send_block(0, 1)
    for i in range(1, 4):
        pack_rows(i)
        send_block(ROUND[i], 0)
    got[view] = send[view]

    zero_rim = jnp.zeros((16, 16, LANES), F32)
    for d, into in ((0, 32), (1, 0)):
        @pl.when(jnp.logical_not(comes[d]))
        def _(d=d, into=into):
            grid[1, into : into + 16] = zero_rim
            lit_got[d] = jnp.zeros((8, LANES), F32)

    for d in range(4):
        @pl.when(jnp.logical_not(comes[d]))
        def _(d=d):
            for i in range(ITERS):
                land[i, d] = zero_rim[:15]

    est[:, 0:CHUNK] = jnp.zeros((CX, CHUNK), F32)
    est[:, CHUNK + YW * Z : 2 * CHUNK + YW * Z] = jnp.zeros((CX, CHUNK), F32)
    est_copy.wait()
    lane16 = lane_of((CX, LANES))
    edge = (lane16 >= jnp.where(upper, 0, RIM)) & (lane16 < jnp.where(upper, RIM + DEPTH, LANES))
    high_half = jnp.broadcast_to(deep_half, (CX, LANES)) == 1

    def est_pair(j, carry):
        base = pl.multiple_of(cx * CHUNK + j * 2 * Z, LANES)
        tiles = [est[:, pl.ds(base + LANES * i, LANES)] for i in range(3)]
        low, high = pair_halves(*tiles)
        for i in range(2):
            grid[0, 2 * j + i] = jnp.where(edge, jnp.where(high_half, high[i], low[i]), 0.0)
        return carry

    def block_left(dx, dz):
        v = at(dx, dz)
        out_to(v, send.at[v], got.at[view], a_s, a_r).wait_send()

    lax.fori_loop(8, 16, est_pair, 0)
    centre = grid[0, 16:32]
    grid[1, 16:32] = swap(centre)
    start_rims(volume_rim, 0, (0, 1))
    send_block(ROUND[1], 1)
    depth_in[...] = split3(centre.reshape(256, LANES))
    lax.fori_loop(0, 8, est_pair, 0)
    lax.fori_loop(16, 24, est_pair, 0)
    block_left(0, 1)
    send_block(ROUND[2], 1)

    for dx, dz in others:
        v = at(dx, dz)
        from_view(v, tap_got.at[v], t_r).wait_recv()

    def prepare(v, carry):
        taps = jnp.concatenate(unpack([tap_got[v, i] for i in range(3)]), axis=0)
        marks = taps[31:32]
        lane = lane_of((1, LANES))
        axis = jnp.sum(jnp.where(lane == 32, marks, 0.0), axis=1, keepdims=True)
        lit = jnp.sum(jnp.where(lane == 64, marks, 0.0), axis=1, keepdims=True)
        inner = (lane32 >= RIM) & (lane32 < RIM + DEPTH) & (row32 < TAPS)
        taps = jnp.where(inner, taps, 0.0)
        along = [jnp.broadcast_to(jnp.where(axis == float(d), 1.0, 0.0), (1, LANES)) for d in range(3)]
        lit = jnp.broadcast_to(lit, (1, LANES))
        flags_of[v] = jnp.concatenate([along[0], along[1], lit, jnp.zeros((5, LANES), F32)], axis=0)
        lit_send[pl.ds(v, 1)] = lit
        weight[v] = taps * (along[0] + along[1])
        tall = jnp.concatenate([taps * along[2], jnp.zeros((LANES - 32, LANES), F32)], axis=0)
        full = pltpu.roll(jnp.transpose(tall), LANES - HALF, 1, stride=1, stride_axis=0)
        for i, part in enumerate(parts_of(full * lit, (0, 1, 0))):
            band[pl.ds(pl.multiple_of(v * 3 * LANES + i * LANES, LANES), LANES)] = part
        here = pl.ds(pl.multiple_of(v * LANES, LANES), LANES)
        for i, part in enumerate(parts_of(jnp.transpose(full), (0, 1, 0))):
            band_t[LANES * i : LANES * (i + 1), here] = part
        return carry

    lax.fori_loop(0, VIEWS, prepare, 0)
    block_left(ROUND[1], 1)
    send_block(ROUND[3], 1)
    for d in (0, 1):
        when(goes[d], lambda d=d: lit_copy(d).start())

    def depth_products():
        product = jnp.dot(depth_in[...], band_t[...], preferred_element_type=F32)
        for v in range(VIEWS):
            deep[v] = product[:, LANES * v : LANES * (v + 1)].reshape(16, 16, LANES)

    def depth_sums():
        product = jnp.dot(ratios[...], band[...], preferred_element_type=F32)
        total[0, 16:32] += product.reshape(16, 16, LANES)

    def tap_sum(out, first, count, source, origin, sign, v):
        length = source.shape[0]
        for k in range(TAPS):
            shift = sign * (k - HALF)
            lo = max(first, origin - shift)
            hi = min(first + count, origin + length - shift)
            if lo >= hi:
                continue
            part = source[lo + shift - origin : hi + shift - origin] * weight[v, k : k + 1][None]
            pieces = []
            if lo > first:
                pieces.append(out[: lo - first])
            pieces.append(out[lo - first : hi - first] + part)
            if hi < first + count:
                pieces.append(out[hi - first :])
            out = jnp.concatenate(pieces, axis=0) if len(pieces) > 1 else pieces[0]
        return out

    def along_x(v):
        return jnp.broadcast_to(flags_of[v, 0:1], (8, LANES))

    def in_layout(v, first, count, s):
        return jnp.where(
            (along_x(v) > 0.5)[None],
            grid[1, first : first + count, 8 * s : 8 * s + 8],
            grid[0, first : first + count, 8 * s : 8 * s + 8],
        )

    def blur_inside(v, carry):
        for s in range(2):
            blurred[v, :, 8 * s : 8 * s + 8] = tap_sum(
                jnp.zeros((16, 8, LANES), F32), 0, 16, in_layout(v, 16, 16, s), 0, 1, v
            )
        return carry

    def blur_rims(v, carry):
        for s in range(2):
            acc = tap_sum(blurred[v, :, 8 * s : 8 * s + 8], 0, 16, in_layout(v, 1, 15, s), -15, 1, v)
            acc = tap_sum(acc, 0, 16, in_layout(v, 32, 15, s), 16, 1, v)
            blurred[v, :, 8 * s : 8 * s + 8] = acc + deep[v, :, 8 * s : 8 * s + 8]
        return carry

    lane3 = lane_of((16, 16, LANES))
    inner3 = (lane3 >= RIM) & (lane3 < RIM + DEPTH)

    def take_ratio(v):
        first_dim = jnp.broadcast_to((along_x(v) > 0.5)[None, :1], (16, 16, LANES))
        ratio = jnp.where(inner3, jnp.where(first_dim, rec_in[1, v], rec_in[0, v]) / blurred[v], 0.0)
        blurred[v] = ratio
        ratios[:, pl.ds(pl.multiple_of(v * 3 * LANES, LANES), 3 * LANES)] = split3(ratio.reshape(256, LANES))

    def spread_rims(v, s):
        x = along_x(v)
        y = jnp.broadcast_to(flags_of[v, 1:2], (8, LANES))
        lit = jnp.broadcast_to(flags_of[v, 2:3], (8, LANES))
        r = blurred[v, :, 8 * s : 8 * s + 8]
        for first, row in ((-HALF, 1), (16, 0)):
            acc = tap_sum(jnp.zeros((HALF, 8, LANES), F32), first, HALF, r, 0, -1, v)
            cells = slice(first + 16, first + 16 + HALF)
            lit_x = jnp.broadcast_to(lit_got[row, pl.ds(v, 1)], (8, LANES))
            total[1, cells, 8 * s : 8 * s + 8] += acc * (x * lit_x)[None]
            total[0, cells, 8 * s : 8 * s + 8] += acc * (y * lit)[None]

    def spread_inside(v, carry):
        x = along_x(v)
        y = jnp.broadcast_to(flags_of[v, 1:2], (8, LANES))
        lit = jnp.broadcast_to(flags_of[v, 2:3], (8, LANES))
        for s in range(2):
            acc = tap_sum(
                jnp.zeros((16, 8, LANES), F32), 0, 16, blurred[v, :, 8 * s : 8 * s + 8], 0, -1, v
            )
            total[1, 16:32, 8 * s : 8 * s + 8] += acc * (x * lit)[None]
            total[0, 16:32, 8 * s : 8 * s + 8] += acc * (y * lit)[None]
        return carry

    def update(phase):
        for d in range(4):
            layout = 1 if d < 2 else 0
            first = 17 if d % 2 == 0 else 16
            total[layout, first : first + 15] += land[phase // 2, d]
        unlit = jnp.zeros((1, LANES), F32)
        for v in range(VIEWS):
            unlit = unlit + (1.0 - flags_of[v, 2:3])
        rim = unpack_rim(rim_land[phase], jnp.where(upper, 16, 96)).reshape(16, 16, LANES)
        summed = total[0, 16:32] + swap(total[1, 16:32]) + rim + unlit[None]
        return jnp.where(inner3, grid[0, 16:32] * summed * (1.0 / VIEWS), 0.0)

    lax.fori_loop(0, VIEWS, blur_inside, 0)
    depth_products()
    recv_rims(volume_rim, 0, (0, 1))
    lax.fori_loop(0, VIEWS, blur_rims, 0)
    for d in (0, 1):
        when(comes[d], lambda d=d: lit_copy(d).wait_recv())

    def arrive(v):
        for part in range(4):
            rows = unpack([got[v, 3 * part + i] for i in range(3)])
            for i in range(4):
                rec_in[0, v, 4 * part + i] = rows[i]
        rec_in[1, v] = swap(rec_in[0, v])

    total[...] = jnp.zeros((2, 48, 16, LANES), F32)
    arrive(view)
    take_ratio(view)
    for s in range(2):
        spread_rims(view, s)

    def spread_arrived(step, carry):
        i = lax.rem(step, 4)
        order = jnp.where(i == 0, 0, lax.rem(i + 1, 3) + 1)
        v = lax.rem(cx + order, XC) * 2 + lax.rem(zh + step // 4, 2)
        from_view(v, got.at[v], a_r).wait_recv()
        arrive(v)
        take_ratio(v)
        for s in range(2):
            spread_rims(v, s)
        return carry

    lax.fori_loop(1, VIEWS, spread_arrived, 0)

    SIDES = (2, 3, 0, 1)

    def send_depth_sums(phase):
        depth_sums()
        rim_send[phase] = pack_rim(total[0, 16:32].reshape(256, LANES), jnp.where(upper, 0, 16))
        start_rims(depth_rim, phase, (4,))

    def finish_sums(phase):
        lax.fori_loop(0, VIEWS, spread_inside, 0)
        for half in range(2):
            recv_rims(sum_rim(half), phase, SIDES)
        recv_rims(depth_rim, phase, (4,))

    def sums_left(phase):
        for half in range(2):
            sent_rims(sum_rim(half), phase, SIDES)
        sent_rims(depth_rim, phase, (4,))

    sent_rims(volume_rim, 0, (0, 1))
    for half in range(2):
        start_rims(sum_rim(half), 1, SIDES)
    send_depth_sums(1)
    finish_sums(1)
    fresh = update(1)
    grid[0, 16:32] = fresh
    start_rims(volume_rim, 2, (2, 3))
    grid[1, 16:32] = swap(fresh)
    start_rims(volume_rim, 2, (0, 1))
    rim_send[2] = pack_rim(fresh.reshape(256, LANES), jnp.where(upper, 112, 32))
    start_rims(depth_rim, 2, (4,))
    sums_left(1)
    total[...] = jnp.zeros((2, 48, 16, LANES), F32)
    lax.fori_loop(0, VIEWS, blur_inside, 0)
    recv_rims(depth_rim, 2, (4,))
    deep_rim = unpack_rim(rim_land[2], jnp.where(upper, 0, 112))
    depth_in[...] = split3(grid[0, 16:32].reshape(256, LANES) + deep_rim)
    depth_products()
    recv_rims(volume_rim, 2, SIDES)

    def second(v, carry):
        blur_rims(v, 0)
        take_ratio(v)
        return carry

    lax.fori_loop(0, VIEWS, second, 0)
    send_depth_sums(3)
    for half in range(2):
        def beyond(v, carry, half=half):
            spread_rims(v, half)
            return carry

        lax.fori_loop(0, VIEWS, beyond, 0)
        start_rims(sum_rim(half), 3, SIDES)
    finish_sums(3)
    fresh = update(3)

    for part in range(4):
        packed = pack([fresh[4 * part + i] for i in range(4)])
        for i in range(3):
            gathered[view, 3 * part + i] = packed[i]
    size = PACKED // PIECES

    def half_copy(i, block):
        cells = gathered.at[block, pl.ds(size * i, size)]
        return pltpu.make_async_remote_copy(
            src_ref=cells, dst_ref=cells, send_sem=z_s.at[i], recv_sem=z_r.at[i], device_id=(mate, tile), device_id_type=MESH
        )

    def row_copy(dx, block):
        cells = gathered.at[block]
        return pltpu.make_async_remote_copy(
            src_ref=cells, dst_ref=cells, send_sem=g_s.at[dx - 1], recv_sem=g_r.at[dx - 1],
            device_id=(at(dx, 0), tile), device_id_type=MESH,
        )

    def forward_copy(dx, i, block):
        cells = gathered.at[block, pl.ds(size * i, size)]
        return pltpu.make_async_remote_copy(
            src_ref=cells, dst_ref=cells, send_sem=f_s.at[dx - 1, i], recv_sem=f_r.at[dx - 1, i],
            device_id=(at(dx, 0), tile), device_id_type=MESH,
        )

    for i in range(PIECES):
        half_copy(i, view).start()
    for dx in (1, 3, 2):
        row_copy(dx, view).start()
    for i in range(PIECES):
        half_copy(i, mate).wait_recv()
        for dx in (1, 3, 2):
            forward_copy(dx, i, mate).start()

    def unpack_out(rows):
        for part in range(4):
            low = unpack([gathered[2 * rows + odd, 3 * part + j] for j in range(3)])
            high = unpack([gathered[2 * rows + 1 - odd, 3 * part + j] for j in range(3)])
            base = pl.multiple_of(rows * CHUNK + part * 4 * Z, LANES)
            for p in range(2):
                for j, t in enumerate(halves_pair(low[2 * p], high[2 * p], low[2 * p + 1], high[2 * p + 1])):
                    out[:, pl.ds(base + LANES * (3 * p + j), LANES)] = t

    unpack_out(cx)
    for dx in (1, 3, 2):
        source = at(XC - dx, 0)
        row_copy(dx, source).wait_recv()
        for i in range(PIECES):
            forward_copy(dx, i, at(XC - dx, 1)).wait_recv()
        unpack_out(source // 2)

    for d in (0, 1):
        when(goes[d], lambda d=d: lit_copy(d).wait_send())
    for dx, dz in others:
        v = at(dx, dz)
        out_to(v, tap_send.at[0], tap_got.at[view], t_s, t_r).wait_send()
        if (dx, dz) not in ((0, 1), (ROUND[1], 1)):
            block_left(dx, dz)
    sent_rims(volume_rim, 2, SIDES)
    sent_rims(depth_rim, 2, (4,))
    sums_left(3)
    for i in range(PIECES):
        half_copy(i, view).wait_send()
    for dx in (1, 3, 2):
        row_copy(dx, view).wait_send()
        for i in range(PIECES):
            forward_copy(dx, i, mate).wait_send()


def on_device(estimate, recorded, kernels, illuminated, detection):
    dma = pltpu.SemaphoreType.DMA
    vmem = lambda *shape: pltpu.VMEM(shape, F32)
    any_space = pl.BlockSpec(memory_space=pltpu.HBM)
    return pl.pallas_call(
        kernel,
        out_shape=jax.ShapeDtypeStruct((CX, YW * Z), F32),
        in_specs=[
            any_space,
            any_space,
            any_space,
            pl.BlockSpec(memory_space=pltpu.SMEM),
            pl.BlockSpec(memory_space=pltpu.SMEM),
        ],
        out_specs=pl.BlockSpec(memory_space=pltpu.VMEM),
        scratch_shapes=[
            vmem(CX, YW * Z + 2 * CHUNK),
            vmem(CX, YW * Z),
            vmem(TAPS, 1, Z),
            vmem(VIEWS, PACKED, CX, LANES),
            vmem(VIEWS, PACKED, CX, LANES),
            vmem(2, 3, 8, LANES),
            vmem(VIEWS, 3, 8, LANES),
            vmem(8, LANES),
            vmem(2, 8, LANES),
            vmem(VIEWS, 8, LANES),
            vmem(VIEWS, 32, LANES),
            pltpu.VMEM((VIEWS * 3 * LANES, LANES), BF16),
            pltpu.VMEM((3 * LANES, VIEWS * LANES), BF16),
            vmem(2, 48, 16, LANES),
            pltpu.VMEM((256, 3 * LANES), BF16),
            vmem(VIEWS, 16, 16, LANES),
            pltpu.VMEM((256, VIEWS * 3 * LANES), BF16),
            vmem(2, VIEWS, 16, 16, LANES),
            vmem(VIEWS, 16, 16, LANES),
            vmem(2, 48, 16, LANES),
            vmem(ITERS, 4, HALF, 16, LANES),
            vmem(4, 32, LANES),
            vmem(4, 32, LANES),
            vmem(VIEWS, PACKED, CX, LANES),
            dma((6,)),
            dma((VIEWS,)), dma((VIEWS,)),
            dma((VIEWS,)), dma((VIEWS,)),
            dma((2,)), dma((2,)),
            dma((4, 5, 2)), dma((4, 5, 2)),
            dma((3,)), dma((3,)),
            dma((PIECES,)), dma((PIECES,)),
            dma((3, PIECES)), dma((3, PIECES)),
        ],
        compiler_params=pltpu.CompilerParams(
            collective_id=0, has_side_effects=True, vmem_limit_bytes=VMEM_BYTES
        ),
    )(estimate, recorded, jnp.swapaxes(kernels, 0, 1), illuminated, detection)


def solution(mesh):
    in_specs = (
        P("tile", None),
        P("view", "tile", None),
        P("view", None, None),
        P("view", "tile"),
        P("view"),
    )
    return jax.shard_map(
        on_device, mesh=mesh, in_specs=in_specs, out_specs=P("tile", None), check_vma=False
    )
```

```python
import jax
import jax.numpy as jnp
from jax import lax
from jax.experimental import pallas as pl
from jax.experimental.pallas import tpu as pltpu
from jax.sharding import PartitionSpec as P


YW = 64
Z = 192
TAPS = 31
HALF = 15
ITERS = 2
VIEWS = 8
XC = 4
TILES = 32
CX = 16
ROWS = 16
DEPTH = 96
LANES = 128
RIM = 16
CHUNK = ROWS * Z
PACKED = 12
PIECES = 4
VMEM_BYTES = 53 * 1024 * 1024
MESH = pl.DeviceIdType.MESH
F32 = jnp.float32
BF16 = jnp.bfloat16


def lane_of(shape):
    return lax.broadcasted_iota(jnp.int32, shape, len(shape) - 1)


def roll(a, shift):
    return pltpu.roll(a, shift, a.ndim - 1)


def pair_halves(t0, t1, t2):
    lane = lane_of(t0.shape)
    a0 = roll(t0, 16)
    a1 = jnp.where(lane < 48, roll(t0, 48), roll(t1, 48))
    b0 = jnp.where(lane < 80, roll(t1, 80), roll(t2, 80))
    b1 = roll(t2, 112)
    return (a0, b0), (a1, b1)


def halves_pair(a0, a1, b0, b1):
    lane = lane_of(a0.shape)
    a1r, b0r = roll(a1, 80), roll(b0, 48)
    t0 = jnp.where(lane < 96, roll(a0, 112), a1r)
    t1 = jnp.where(lane < 64, a1r, b0r)
    t2 = jnp.where(lane < 32, b0r, roll(b1, 16))
    return t0, t1, t2


def pack(rows):
    lane = lane_of(rows[0].shape)
    inner = (lane >= RIM) & (lane < RIM + DEPTH)
    return [jnp.where(inner, rows[i], roll(rows[3], 96 - 32 * i)) for i in range(3)]


def unpack(tiles):
    lane = lane_of(tiles[0].shape)
    r = [roll(tiles[i], 32 + 32 * i) for i in range(3)]
    return [tiles[0], tiles[1], tiles[2], jnp.where(lane < 48, r[0], jnp.where(lane < 80, r[1], r[2]))]


def swap(a):
    return jnp.swapaxes(a, 0, 1)


def pack_rim(a, shift):
    lane = lane_of((32, LANES))
    out = jnp.zeros((32, LANES), F32)
    for g in range(8):
        moved = roll(a[32 * g : 32 * g + 32], lax.rem(shift + 16 * g, 128))
        out = jnp.where((lane >= 16 * g) & (lane < 16 * g + 16), moved, out)
    return out


def unpack_rim(p, first):
    lane = lane_of((32, LANES))
    keep = (lane >= first) & (lane < first + 16)
    return jnp.concatenate(
        [jnp.where(keep, roll(p, lax.rem(first + 128 - 16 * g, 128)), 0.0) for g in range(8)], axis=0
    )


def parts_of(a, order):
    high = a.astype(BF16)
    low = (a - high.astype(F32)).astype(BF16)
    return [(high, low)[i] for i in order]


def split3(a):
    return jnp.concatenate(parts_of(a, (0, 0, 1)), axis=-1)


def kernel(
    est_hbm, rec_hbm, ker_hbm, lit_ref, det_ref, out,
    est, rec, kpad, send, got, tap_send, tap_got, lit_of, lit_got, flags_of,
    weight, band, band_t, grid, depth_in, deep, ratios, rec_in, blurred, total, land, rim_send, rim_land, gathered,
    in_sem, a_s, a_r, t_s, t_r, m_s, m_r, e_s, e_r, l_s, l_r, h_s, h_r, g_s, g_r, z_s, z_r, f_s, f_r,
):
    view = lax.axis_index("view")
    tile = lax.axis_index("tile")
    cx, zh = view // 2, lax.rem(view, 2)
    odd = lax.rem(tile // 8, 2)
    core = lax.rem(tile, 2)
    chip_mate = (view, tile + 1 - 2 * core)
    deep_half = lax.rem(zh + odd, 2)
    upper = deep_half == 1

    def at(dx, dz):
        return lax.rem(cx + dx, XC) * 2 + lax.rem(zh + dz, 2)

    mate = at(0, 1)
    others = [(0, 1), (1, 1), (1, 0), (3, 1), (3, 0), (2, 1), (2, 0)]

    to_device = [
        (jnp.where(lax.rem(tile, 8) == 0, mate, view), lax.rem(tile + TILES - 1, TILES)),
        (jnp.where(lax.rem(tile, 8) == 7, mate, view), lax.rem(tile + 1, TILES)),
        (lax.rem(view + VIEWS - 2, VIEWS), tile),
        (lax.rem(view + 2, VIEWS), tile),
        (mate, tile),
    ]
    goes = [tile > 0, tile < TILES - 1, cx > 0, cx < XC - 1, None]
    comes = [tile < TILES - 1, tile > 0, cx < XC - 1, cx > 0, None]

    def when(cond, f):
        if cond is None:
            f()
        else:
            pl.when(cond)(f)

    barrier = pltpu.get_barrier_semaphore()

    def greet(device):
        pl.semaphore_signal(barrier, inc=1, device_id=device, device_id_type=MESH)

    for dx, dz in others:
        greet((at(dx, dz), tile))
    for d in (0, 1):
        when(goes[d], lambda d=d: greet(to_device[d]))

    ROUND = (0, 1, 3, 2)

    def rec_in_copy(i):
        cells = pl.ds(pl.multiple_of(lax.rem(cx + ROUND[i], XC) * CHUNK, LANES), CHUNK)
        return pltpu.make_async_copy(rec_hbm.at[0, :, cells], rec.at[:, cells], in_sem.at[i])

    ker_copy = pltpu.make_async_copy(ker_hbm, kpad, in_sem.at[4])
    est_copy = pltpu.make_async_copy(est_hbm, est.at[:, pl.ds(CHUNK, YW * Z)], in_sem.at[5])
    ker_copy.start()
    for i in range(4):
        rec_in_copy(i).start()
    est_copy.start()

    def rim_copy(phase, d, src, dst, half=0):
        return pltpu.make_async_remote_copy(
            src_ref=src, dst_ref=dst, send_sem=h_s.at[phase, d, half], recv_sem=h_r.at[phase, d, half],
            device_id=to_device[d], device_id_type=MESH,
        )

    def volume_rim(phase, d):
        layout = 1 if d < 2 else 0
        if d % 2 == 0:
            return rim_copy(phase, d, grid.at[layout, pl.ds(16, 15)], grid.at[layout, pl.ds(32, 15)])
        return rim_copy(phase, d, grid.at[layout, pl.ds(17, 15)], grid.at[layout, pl.ds(1, 15)])

    def sum_rim(half):
        def make(phase, d):
            layout = 1 if d < 2 else 0
            first = 1 if d % 2 == 0 else 32
            part = pl.ds(8 * half, 8)
            return rim_copy(
                phase, d, total.at[layout, pl.ds(first, 15), part], land.at[phase // 2, d, :, part], half
            )

        return make

    def depth_rim(phase, d):
        return rim_copy(phase, d, rim_send.at[phase], rim_land.at[phase])

    def start_rims(make, phase, dirs):
        for d in dirs:
            when(goes[d], lambda d=d: make(phase, d).start())

    def recv_rims(make, phase, dirs):
        for d in dirs:
            when(comes[d], lambda d=d: make(phase, d).wait_recv())

    def sent_rims(make, phase, dirs):
        for d in dirs:
            when(goes[d], lambda d=d: make(phase, d).wait_send())

    def from_view(v, dst, r):
        return pltpu.make_async_remote_copy(
            src_ref=dst, dst_ref=dst, send_sem=r.at[v], recv_sem=r.at[v], device_id=(v, tile), device_id_type=MESH
        )

    def out_to(v, src, dst, s, r):
        return pltpu.make_async_remote_copy(
            src_ref=src, dst_ref=dst, send_sem=s.at[v], recv_sem=r.at[view], device_id=(v, tile), device_id_type=MESH
        )

    def lit_copy(d):
        return pltpu.make_async_remote_copy(
            src_ref=lit_of, dst_ref=lit_got.at[d], send_sem=l_s.at[d], recv_sem=l_r.at[d],
            device_id=to_device[d], device_id_type=MESH,
        )

    ker_copy.wait()
    lane32 = lane_of((32, LANES))
    row32 = lax.broadcasted_iota(jnp.int32, (32, LANES), 0)
    axis_now = det_ref[0].astype(F32)
    lit_now = (lit_ref[0, 0] > 0).astype(F32)
    k0 = jnp.concatenate([kpad[:, 0, 0:LANES], jnp.zeros((1, LANES), F32)], axis=0)
    k1 = jnp.concatenate([kpad[:, 0, LANES:Z], jnp.zeros((TAPS, 2 * LANES - Z), F32)], axis=1)
    k1 = jnp.concatenate([k1, jnp.zeros((1, LANES), F32)], axis=0)
    for half in range(2):
        taps = roll(k0, 16) if half == 0 else jnp.where(lane32 < 48, roll(k0, 48), roll(k1, 48))
        taps = jnp.where(row32 == TAPS, axis_now, taps)
        for i, t in enumerate(pack([taps[8 * j : 8 * j + 8] for j in range(4)])):
            tap_send[half, i] = t
    tap_got[view] = tap_send[deep_half]
    lit_of[view] = jnp.full((1, LANES), lit_now, F32)

    def pack_rows(i):
        rec_in_copy(i).wait()
        rows = lax.rem(cx + ROUND[i], XC)

        def pack_part(part, carry):
            base = pl.multiple_of(rows * CHUNK + part * 4 * Z, LANES)
            tiles = [rec[:, pl.ds(base + LANES * j, LANES)] for j in range(6)]
            one, two = pair_halves(*tiles[:3]), pair_halves(*tiles[3:])
            for half in range(2):
                packed = pack([*one[half], *two[half]])
                for j in range(3):
                    send[rows * 2 + lax.rem(half + odd, 2), part * 3 + j] = packed[j]
            return carry

        lax.fori_loop(0, 4, pack_part, 0)

    def send_block(dx, dz):
        v = at(dx, dz)
        out_to(v, send.at[v], got.at[view], a_s, a_r).start()

    pack_rows(0)
    pl.semaphore_wait(barrier, 7 + (tile > 0).astype(jnp.int32) + (tile < TILES - 1).astype(jnp.int32))

    FAR = ((0, 0), (1, 1), (3, 0), (2, 1))

    def tap_copy(v):
        return out_to(v, tap_send.at[lax.rem(v + odd, 2)], tap_got.at[view], t_s, t_r)

    def tap_pass(v):
        return pltpu.make_async_remote_copy(
            src_ref=tap_got.at[v], dst_ref=tap_got.at[v], send_sem=m_s.at[v], recv_sem=m_r.at[v],
            device_id=chip_mate, device_id_type=MESH,
        )

    for dx, c in FAR:
        pl.when(core == c)(lambda dx=dx: tap_copy(at(dx, 1)).start())
    send_block(0, 1)
    for dx in (1, 3, 2):
        tap_copy(at(dx, 0)).start()
    for dx, dz in others:
        out_to(at(dx, dz), lit_of.at[view], lit_of.at[view], e_s, e_r).start()
    for i in range(1, 4):
        pack_rows(i)
        send_block(ROUND[i], 0)
    got[view] = send[view]

    zero_rim = jnp.zeros((16, 16, LANES), F32)
    for d, into in ((0, 32), (1, 0)):
        @pl.when(jnp.logical_not(comes[d]))
        def _(d=d, into=into):
            grid[1, into : into + 16] = zero_rim
            lit_got[d] = jnp.zeros((VIEWS, 1, LANES), F32)

    for d in range(4):
        @pl.when(jnp.logical_not(comes[d]))
        def _(d=d):
            for i in range(ITERS):
                land[i, d] = zero_rim[:15]

    est[:, 0:CHUNK] = jnp.zeros((CX, CHUNK), F32)
    est[:, CHUNK + YW * Z : 2 * CHUNK + YW * Z] = jnp.zeros((CX, CHUNK), F32)
    est_copy.wait()
    lane16 = lane_of((CX, LANES))
    edge = (lane16 >= jnp.where(upper, 0, RIM)) & (lane16 < jnp.where(upper, RIM + DEPTH, LANES))
    high_half = jnp.broadcast_to(deep_half, (CX, LANES)) == 1

    def est_pair(j, carry):
        base = pl.multiple_of(cx * CHUNK + j * 2 * Z, LANES)
        tiles = [est[:, pl.ds(base + LANES * i, LANES)] for i in range(3)]
        low, high = pair_halves(*tiles)
        for i in range(2):
            grid[0, 2 * j + i] = jnp.where(edge, jnp.where(high_half, high[i], low[i]), 0.0)
        return carry

    def block_left(dx, dz):
        v = at(dx, dz)
        out_to(v, send.at[v], got.at[view], a_s, a_r).wait_send()

    lax.fori_loop(8, 16, est_pair, 0)
    centre = grid[0, 16:32]
    grid[1, 16:32] = swap(centre)
    send_block(ROUND[1], 1)
    start_rims(volume_rim, 0, (0, 1))
    send_block(ROUND[2], 1)
    send_block(ROUND[3], 1)
    depth_in[...] = split3(centre.reshape(256, LANES))
    lax.fori_loop(0, 8, est_pair, 0)
    lax.fori_loop(16, 24, est_pair, 0)

    for dx, c in FAR:
        def take_far(dx=dx):
            v = at(XC - dx, 1)
            from_view(v, tap_got.at[v], t_r).wait_recv()
            tap_pass(v).start()

        pl.when(core == c)(take_far)
    for dx in (1, 3, 2):
        v = at(dx, 0)
        from_view(v, tap_got.at[v], t_r).wait_recv()
    for dx, dz in others:
        v = at(dx, dz)
        from_view(v, lit_of.at[v], e_r).wait_recv()
    for dx, c in FAR:
        pl.when(core != c)(lambda dx=dx: tap_pass(at(XC - dx, 1)).wait_recv())

    def slot(v):
        return lax.rem(v + zh, 2) * XC + v // 2

    def prepare(v, carry):
        taps = jnp.concatenate(unpack([tap_got[v, i] for i in range(3)]), axis=0)
        marks = taps[31:32]
        lane = lane_of((1, LANES))
        axis = jnp.sum(jnp.where(lane == 32, marks, 0.0), axis=1, keepdims=True)
        lit = lit_of[v]
        inner = (lane32 >= RIM) & (lane32 < RIM + DEPTH) & (row32 < TAPS)
        taps = jnp.where(inner, taps, 0.0)
        along = [jnp.broadcast_to(jnp.where(axis == float(d), 1.0, 0.0), (1, LANES)) for d in range(3)]
        flags_of[v] = jnp.concatenate([along[0], along[1], lit, jnp.zeros((5, LANES), F32)], axis=0)
        weight[v] = taps * (along[0] + along[1])
        tall = jnp.concatenate([taps * along[2], jnp.zeros((LANES - 32, LANES), F32)], axis=0)
        full = pltpu.roll(jnp.transpose(tall), LANES - HALF, 1, stride=1, stride_axis=0)
        for i, part in enumerate(parts_of(full * lit, (0, 1, 0))):
            band[pl.ds(pl.multiple_of(slot(v) * 3 * LANES + i * LANES, LANES), LANES)] = part
        here = pl.ds(pl.multiple_of(v * LANES, LANES), LANES)
        for i, part in enumerate(parts_of(jnp.transpose(full), (0, 1, 0))):
            band_t[LANES * i : LANES * (i + 1), here] = part
        return carry

    lax.fori_loop(0, VIEWS, prepare, 0)
    for d in (0, 1):
        when(goes[d], lambda d=d: lit_copy(d).start())

    def depth_products():
        product = jnp.dot(depth_in[...], band_t[...], preferred_element_type=F32)
        for v in range(VIEWS):
            deep[v] = product[:, LANES * v : LANES * (v + 1)].reshape(16, 16, LANES)

    def depth_sums(part):
        span = slice(part * XC * 3 * LANES, (part + 1) * XC * 3 * LANES)
        product = jnp.dot(ratios[:, span], band[span], preferred_element_type=F32)
        total[0, 16:32] += product.reshape(16, 16, LANES)

    def tap_sum(out, first, count, source, origin, sign, v):
        length = source.shape[0]
        for k in range(TAPS):
            shift = sign * (k - HALF)
            lo = max(first, origin - shift)
            hi = min(first + count, origin + length - shift)
            if lo >= hi:
                continue
            part = source[lo + shift - origin : hi + shift - origin] * weight[v, k : k + 1][None]
            pieces = []
            if lo > first:
                pieces.append(out[: lo - first])
            pieces.append(out[lo - first : hi - first] + part)
            if hi < first + count:
                pieces.append(out[hi - first :])
            out = jnp.concatenate(pieces, axis=0) if len(pieces) > 1 else pieces[0]
        return out

    def along_x(v):
        return jnp.broadcast_to(flags_of[v, 0:1], (8, LANES))

    def in_layout(v, first, count, s):
        return jnp.where(
            (along_x(v) > 0.5)[None],
            grid[1, first : first + count, 8 * s : 8 * s + 8],
            grid[0, first : first + count, 8 * s : 8 * s + 8],
        )

    def blur_inside(v, carry):
        for s in range(2):
            blurred[v, :, 8 * s : 8 * s + 8] = tap_sum(
                jnp.zeros((16, 8, LANES), F32), 0, 16, in_layout(v, 16, 16, s), 0, 1, v
            )
        return carry

    def blur_rims(v, carry):
        for s in range(2):
            acc = tap_sum(blurred[v, :, 8 * s : 8 * s + 8], 0, 16, in_layout(v, 1, 15, s), -15, 1, v)
            acc = tap_sum(acc, 0, 16, in_layout(v, 32, 15, s), 16, 1, v)
            blurred[v, :, 8 * s : 8 * s + 8] = acc + deep[v, :, 8 * s : 8 * s + 8]
        return carry

    lane3 = lane_of((16, 16, LANES))
    inner3 = (lane3 >= RIM) & (lane3 < RIM + DEPTH)

    def take_ratio(v):
        first_dim = jnp.broadcast_to((along_x(v) > 0.5)[None, :1], (16, 16, LANES))
        ratio = jnp.where(inner3, jnp.where(first_dim, rec_in[1, v], rec_in[0, v]) / blurred[v], 0.0)
        blurred[v] = ratio
        ratios[:, pl.ds(pl.multiple_of(slot(v) * 3 * LANES, LANES), 3 * LANES)] = split3(ratio.reshape(256, LANES))

    def spread_rims(v, s):
        x = along_x(v)
        y = jnp.broadcast_to(flags_of[v, 1:2], (8, LANES))
        lit = jnp.broadcast_to(flags_of[v, 2:3], (8, LANES))
        r = blurred[v, :, 8 * s : 8 * s + 8]
        for first, row in ((-HALF, 1), (16, 0)):
            acc = tap_sum(jnp.zeros((HALF, 8, LANES), F32), first, HALF, r, 0, -1, v)
            cells = slice(first + 16, first + 16 + HALF)
            lit_x = jnp.broadcast_to(lit_got[row, v], (8, LANES))
            total[1, cells, 8 * s : 8 * s + 8] += acc * (x * lit_x)[None]
            total[0, cells, 8 * s : 8 * s + 8] += acc * (y * lit)[None]

    def spread_inside(v, carry):
        x = along_x(v)
        y = jnp.broadcast_to(flags_of[v, 1:2], (8, LANES))
        lit = jnp.broadcast_to(flags_of[v, 2:3], (8, LANES))
        for s in range(2):
            acc = tap_sum(
                jnp.zeros((16, 8, LANES), F32), 0, 16, blurred[v, :, 8 * s : 8 * s + 8], 0, -1, v
            )
            total[1, 16:32, 8 * s : 8 * s + 8] += acc * (x * lit)[None]
            total[0, 16:32, 8 * s : 8 * s + 8] += acc * (y * lit)[None]
        return carry

    def update(phase):
        for d in range(4):
            layout = 1 if d < 2 else 0
            first = 17 if d % 2 == 0 else 16
            total[layout, first : first + 15] += land[phase // 2, d]
        unlit = jnp.zeros((1, LANES), F32)
        for v in range(VIEWS):
            unlit = unlit + (1.0 - flags_of[v, 2:3])
        rim = unpack_rim(rim_land[phase], jnp.where(upper, 16, 96)).reshape(16, 16, LANES)
        summed = total[0, 16:32] + swap(total[1, 16:32]) + rim + unlit[None]
        return jnp.where(inner3, grid[0, 16:32] * summed * (1.0 / VIEWS), 0.0)

    lax.fori_loop(0, VIEWS, blur_inside, 0)
    depth_products()
    recv_rims(volume_rim, 0, (0, 1))
    lax.fori_loop(0, VIEWS, blur_rims, 0)
    for d in (0, 1):
        when(comes[d], lambda d=d: lit_copy(d).wait_recv())

    def arrive(v):
        for part in range(4):
            rows = unpack([got[v, 3 * part + i] for i in range(3)])
            for i in range(4):
                rec_in[0, v, 4 * part + i] = rows[i]
        rec_in[1, v] = swap(rec_in[0, v])

    total[...] = jnp.zeros((2, 48, 16, LANES), F32)
    arrive(view)
    take_ratio(view)
    for s in range(2):
        spread_rims(view, s)

    def view_of(step):
        i = lax.rem(step, 4)
        order = jnp.where(i == 0, 0, lax.rem(i + 1, 3) + 1)
        return lax.rem(cx + order, XC) * 2 + lax.rem(zh + step // 4, 2)

    def take_arrived(step, carry):
        v = view_of(step)
        from_view(v, got.at[v], a_r).wait_recv()
        arrive(v)
        take_ratio(v)
        return carry

    def spread_arrived(step, carry):
        take_arrived(step, carry)
        for s in range(2):
            spread_rims(view_of(step), s)
        return carry

    lax.fori_loop(1, XC, spread_arrived, 0)
    depth_sums(0)
    lax.fori_loop(XC, VIEWS, take_arrived, 0)

    SIDES = (2, 3, 0, 1)

    def send_depth_sums(phase):
        rim_send[phase] = pack_rim(total[0, 16:32].reshape(256, LANES), jnp.where(upper, 0, 16))
        start_rims(depth_rim, phase, (4,))

    def finish_sums(phase):
        lax.fori_loop(0, VIEWS, spread_inside, 0)
        for half in range(2):
            recv_rims(sum_rim(half), phase, SIDES)
        recv_rims(depth_rim, phase, (4,))

    def sums_left(phase):
        for half in range(2):
            sent_rims(sum_rim(half), phase, SIDES)
        sent_rims(depth_rim, phase, (4,))

    def spread_halves(phase, first):
        for half in range(2):
            def beyond(step, carry, half=half):
                spread_rims(view_of(step), half)
                return carry

            lax.fori_loop(first, VIEWS, beyond, 0)
            start_rims(sum_rim(half), phase, SIDES)

    sent_rims(volume_rim, 0, (0, 1))
    depth_sums(1)
    send_depth_sums(1)
    spread_halves(1, XC)
    finish_sums(1)
    fresh = update(1)
    grid[0, 16:32] = fresh
    start_rims(volume_rim, 2, (2, 3))
    grid[1, 16:32] = swap(fresh)
    start_rims(volume_rim, 2, (0, 1))
    rim_send[2] = pack_rim(fresh.reshape(256, LANES), jnp.where(upper, 112, 32))
    start_rims(depth_rim, 2, (4,))
    sums_left(1)
    total[...] = jnp.zeros((2, 48, 16, LANES), F32)
    lax.fori_loop(0, VIEWS, blur_inside, 0)
    recv_rims(depth_rim, 2, (4,))
    deep_rim = unpack_rim(rim_land[2], jnp.where(upper, 0, 112))
    depth_in[...] = split3(grid[0, 16:32].reshape(256, LANES) + deep_rim)
    depth_products()
    recv_rims(volume_rim, 2, SIDES)

    def second(v, carry):
        blur_rims(v, 0)
        take_ratio(v)
        return carry

    lax.fori_loop(0, VIEWS, second, 0)
    depth_sums(0)
    depth_sums(1)
    send_depth_sums(3)
    spread_halves(3, 0)
    finish_sums(3)
    fresh = update(3)

    for part in range(4):
        packed = pack([fresh[4 * part + i] for i in range(4)])
        for i in range(3):
            gathered[view, 3 * part + i] = packed[i]
    size = PACKED // PIECES

    def half_copy(i, block):
        cells = gathered.at[block, pl.ds(size * i, size)]
        return pltpu.make_async_remote_copy(
            src_ref=cells, dst_ref=cells, send_sem=z_s.at[i], recv_sem=z_r.at[i], device_id=(mate, tile), device_id_type=MESH
        )

    def row_copy(dx, block):
        cells = gathered.at[block]
        return pltpu.make_async_remote_copy(
            src_ref=cells, dst_ref=cells, send_sem=g_s.at[dx - 1], recv_sem=g_r.at[dx - 1],
            device_id=(at(dx, 0), tile), device_id_type=MESH,
        )

    def forward_copy(dx, i, block):
        cells = gathered.at[block, pl.ds(size * i, size)]
        return pltpu.make_async_remote_copy(
            src_ref=cells, dst_ref=cells, send_sem=f_s.at[dx - 1, i], recv_sem=f_r.at[dx - 1, i],
            device_id=(at(dx, 0), tile), device_id_type=MESH,
        )

    for i in range(PIECES):
        half_copy(i, view).start()
    for dx in (1, 3, 2):
        row_copy(dx, view).start()
    for i in range(PIECES):
        half_copy(i, mate).wait_recv()
        for dx in (1, 3, 2):
            forward_copy(dx, i, mate).start()

    def unpack_out(rows):
        for part in range(4):
            low = unpack([gathered[2 * rows + odd, 3 * part + j] for j in range(3)])
            high = unpack([gathered[2 * rows + 1 - odd, 3 * part + j] for j in range(3)])
            base = pl.multiple_of(rows * CHUNK + part * 4 * Z, LANES)
            for p in range(2):
                for j, t in enumerate(halves_pair(low[2 * p], high[2 * p], low[2 * p + 1], high[2 * p + 1])):
                    out[:, pl.ds(base + LANES * (3 * p + j), LANES)] = t

    unpack_out(cx)
    for dx in (1, 3, 2):
        source = at(XC - dx, 0)
        row_copy(dx, source).wait_recv()
        for i in range(PIECES):
            forward_copy(dx, i, at(XC - dx, 1)).wait_recv()
        unpack_out(source // 2)

    for d in (0, 1):
        when(goes[d], lambda d=d: lit_copy(d).wait_send())
    for dx, dz in others:
        v = at(dx, dz)
        out_to(v, lit_of.at[view], lit_of.at[view], e_s, e_r).wait_send()
        block_left(dx, dz)
    for dx, c in FAR:
        pl.when(core == c)(lambda dx=dx: tap_copy(at(dx, 1)).wait_send())
        pl.when(core == c)(lambda dx=dx: tap_pass(at(XC - dx, 1)).wait_send())
    for dx in (1, 3, 2):
        tap_copy(at(dx, 0)).wait_send()
    sent_rims(volume_rim, 2, SIDES)
    sent_rims(depth_rim, 2, (4,))
    sums_left(3)
    for i in range(PIECES):
        half_copy(i, view).wait_send()
    for dx in (1, 3, 2):
        row_copy(dx, view).wait_send()
        for i in range(PIECES):
            forward_copy(dx, i, mate).wait_send()


def on_device(estimate, recorded, kernels, illuminated, detection):
    dma = pltpu.SemaphoreType.DMA
    vmem = lambda *shape: pltpu.VMEM(shape, F32)
    any_space = pl.BlockSpec(memory_space=pltpu.HBM)
    return pl.pallas_call(
        kernel,
        out_shape=jax.ShapeDtypeStruct((CX, YW * Z), F32),
        in_specs=[
            any_space,
            any_space,
            any_space,
            pl.BlockSpec(memory_space=pltpu.SMEM),
            pl.BlockSpec(memory_space=pltpu.SMEM),
        ],
        out_specs=pl.BlockSpec(memory_space=pltpu.VMEM),
        scratch_shapes=[
            vmem(CX, YW * Z + 2 * CHUNK),
            vmem(CX, YW * Z),
            vmem(TAPS, 1, Z),
            vmem(VIEWS, PACKED, CX, LANES),
            vmem(VIEWS, PACKED, CX, LANES),
            vmem(2, 3, 8, LANES),
            vmem(VIEWS, 3, 8, LANES),
            vmem(VIEWS, 1, LANES),
            vmem(2, VIEWS, 1, LANES),
            vmem(VIEWS, 8, LANES),
            vmem(VIEWS, 32, LANES),
            pltpu.VMEM((VIEWS * 3 * LANES, LANES), BF16),
            pltpu.VMEM((3 * LANES, VIEWS * LANES), BF16),
            vmem(2, 48, 16, LANES),
            pltpu.VMEM((256, 3 * LANES), BF16),
            vmem(VIEWS, 16, 16, LANES),
            pltpu.VMEM((256, VIEWS * 3 * LANES), BF16),
            vmem(2, VIEWS, 16, 16, LANES),
            vmem(VIEWS, 16, 16, LANES),
            vmem(2, 48, 16, LANES),
            vmem(ITERS, 4, HALF, 16, LANES),
            vmem(4, 32, LANES),
            vmem(4, 32, LANES),
            vmem(VIEWS, PACKED, CX, LANES),
            dma((6,)),
            dma((VIEWS,)), dma((VIEWS,)),
            dma((VIEWS,)), dma((VIEWS,)),
            dma((VIEWS,)), dma((VIEWS,)),
            dma((VIEWS,)), dma((VIEWS,)),
            dma((2,)), dma((2,)),
            dma((4, 5, 2)), dma((4, 5, 2)),
            dma((3,)), dma((3,)),
            dma((PIECES,)), dma((PIECES,)),
            dma((3, PIECES)), dma((3, PIECES)),
        ],
        compiler_params=pltpu.CompilerParams(
            collective_id=0, has_side_effects=True, vmem_limit_bytes=VMEM_BYTES
        ),
    )(estimate, recorded, jnp.swapaxes(kernels, 0, 1), illuminated, detection)


def solution(mesh):
    in_specs = (
        P("tile", None),
        P("view", "tile", None),
        P("view", None, None),
        P("view", "tile"),
        P("view"),
    )
    return jax.shard_map(
        on_device, mesh=mesh, in_specs=in_specs, out_specs=P("tile", None), check_vma=False
    )
```

```python
import functools

import jax
import jax.numpy as jnp
from jax import lax
from jax.experimental import pallas as pl
from jax.experimental.pallas import tpu as pltpu
from jax.sharding import PartitionSpec as P


YW = 64
Z = 192
TAPS = 31
HALF = 15
ITERS = 2
VIEWS = 8
XC = 4
TILES = 32
CX = 16
ROWS = 16
DEPTH = 96
LANES = 128
RIM = 16
CHUNK = ROWS * Z
PACKED = 12
PIECES = 4
VMEM_BYTES = 53 * 1024 * 1024
MESH = pl.DeviceIdType.MESH
F32 = jnp.float32
BF16 = jnp.bfloat16


def lane_of(shape):
    return lax.broadcasted_iota(jnp.int32, shape, len(shape) - 1)


def roll(a, shift):
    return pltpu.roll(a, shift, a.ndim - 1)


def pair_halves(t0, t1, t2):
    lane = lane_of(t0.shape)
    a0 = roll(t0, 16)
    a1 = jnp.where(lane < 48, roll(t0, 48), roll(t1, 48))
    b0 = jnp.where(lane < 80, roll(t1, 80), roll(t2, 80))
    b1 = roll(t2, 112)
    return (a0, b0), (a1, b1)


def halves_pair(a0, a1, b0, b1):
    lane = lane_of(a0.shape)
    a1r, b0r = roll(a1, 80), roll(b0, 48)
    t0 = jnp.where(lane < 96, roll(a0, 112), a1r)
    t1 = jnp.where(lane < 64, a1r, b0r)
    t2 = jnp.where(lane < 32, b0r, roll(b1, 16))
    return t0, t1, t2


def pack(rows):
    lane = lane_of(rows[0].shape)
    inner = (lane >= RIM) & (lane < RIM + DEPTH)
    return [jnp.where(inner, rows[i], roll(rows[3], 96 - 32 * i)) for i in range(3)]


def unpack(tiles):
    lane = lane_of(tiles[0].shape)
    r = [roll(tiles[i], 32 + 32 * i) for i in range(3)]
    return [tiles[0], tiles[1], tiles[2], jnp.where(lane < 48, r[0], jnp.where(lane < 80, r[1], r[2]))]


def swap(a):
    return jnp.swapaxes(a, 0, 1)


def pack_rim(a, shift):
    lane = lane_of((32, LANES))
    out = jnp.zeros((32, LANES), F32)
    for g in range(8):
        moved = roll(a[32 * g : 32 * g + 32], lax.rem(shift + 16 * g, 128))
        out = jnp.where((lane >= 16 * g) & (lane < 16 * g + 16), moved, out)
    return out


def unpack_rim(p, first):
    lane = lane_of((32, LANES))
    keep = (lane >= first) & (lane < first + 16)
    return jnp.concatenate(
        [jnp.where(keep, roll(p, lax.rem(first + 128 - 16 * g, 128)), 0.0) for g in range(8)], axis=0
    )


def parts_of(a, order):
    high = a.astype(BF16)
    low = (a - high.astype(F32)).astype(BF16)
    return [(high, low)[i] for i in order]


def split3(a):
    return jnp.concatenate(parts_of(a, (0, 0, 1)), axis=-1)


def kernel(
    est_hbm, rec_hbm, ker_hbm, lit_ref, det_ref, out,
    est, rec, kpad, send, got, tap_send, tap_got, lit_of, lit_got, flags_of,
    weight, band, band_t, grid, depth_in, deep, ratios, rec_in, blurred, total, land, rim_send, rim_land, gathered,
    in_sem, a_s, a_r, t_s, t_r, m_s, m_r, e_s, e_r, l_s, l_r, h_s, h_r, g_s, g_r, z_s, z_r, f_s, f_r,
):
    view = lax.axis_index("view")
    tile = lax.axis_index("tile")
    cx, zh = view // 2, lax.rem(view, 2)
    odd = lax.rem(tile // 8, 2)
    core = lax.rem(tile, 2)
    chip_mate = (view, tile + 1 - 2 * core)
    deep_half = lax.rem(zh + odd, 2)
    upper = deep_half == 1

    def at(dx, dz):
        return lax.rem(cx + dx, XC) * 2 + lax.rem(zh + dz, 2)

    mate = at(0, 1)
    others = [(0, 1), (1, 1), (1, 0), (3, 1), (3, 0), (2, 1), (2, 0)]

    to_device = [
        (jnp.where(lax.rem(tile, 8) == 0, mate, view), lax.rem(tile + TILES - 1, TILES)),
        (jnp.where(lax.rem(tile, 8) == 7, mate, view), lax.rem(tile + 1, TILES)),
        (lax.rem(view + VIEWS - 2, VIEWS), tile),
        (lax.rem(view + 2, VIEWS), tile),
        (mate, tile),
    ]
    goes = [tile > 0, tile < TILES - 1, cx > 0, cx < XC - 1, None]
    comes = [tile < TILES - 1, tile > 0, cx < XC - 1, cx > 0, None]

    def when(cond, f):
        if cond is None:
            f()
        else:
            pl.when(cond)(f)

    barrier = pltpu.get_barrier_semaphore()

    def greet(device):
        pl.semaphore_signal(barrier, inc=1, device_id=device, device_id_type=MESH)

    for dx, dz in others:
        greet((at(dx, dz), tile))
    for d in (0, 1):
        when(goes[d], lambda d=d: greet(to_device[d]))

    ROUND = (0, 1, 3, 2)

    def rec_in_copy(i):
        cells = pl.ds(pl.multiple_of(lax.rem(cx + ROUND[i], XC) * CHUNK, LANES), CHUNK)
        return pltpu.make_async_copy(rec_hbm.at[0, :, cells], rec.at[:, cells], in_sem.at[i])

    ker_copy = pltpu.make_async_copy(ker_hbm, kpad, in_sem.at[4])
    est_copy = pltpu.make_async_copy(est_hbm, est.at[:, pl.ds(CHUNK, YW * Z)], in_sem.at[5])
    ker_copy.start()
    for i in range(4):
        rec_in_copy(i).start()
    est_copy.start()

    def rim_copy(phase, d, src, dst, half=0):
        return pltpu.make_async_remote_copy(
            src_ref=src, dst_ref=dst, send_sem=h_s.at[phase, d, half], recv_sem=h_r.at[phase, d, half],
            device_id=to_device[d], device_id_type=MESH,
        )

    def volume_rim(half):
        def make(phase, d):
            layout = 1 if d < 2 else 0
            source, target = (16, 32) if d % 2 == 0 else (17, 1)
            part = pl.ds(8 * half, 8)
            return rim_copy(
                phase, d, grid.at[layout, pl.ds(source, 15), part], grid.at[layout, pl.ds(target, 15), part], half
            )

        return make

    def sum_rim(half):
        def make(phase, d):
            layout = 1 if d < 2 else 0
            first = 1 if d % 2 == 0 else 32
            part = pl.ds(8 * half, 8)
            return rim_copy(
                phase, d, total.at[layout, pl.ds(first, 15), part], land.at[phase // 2, d, :, part], half
            )

        return make

    def depth_rim(phase, d):
        return rim_copy(phase, d, rim_send.at[phase], rim_land.at[phase])

    def start_rims(make, phase, dirs):
        for d in dirs:
            when(goes[d], lambda d=d: make(phase, d).start())

    def recv_rims(make, phase, dirs):
        for d in dirs:
            when(comes[d], lambda d=d: make(phase, d).wait_recv())

    def sent_rims(make, phase, dirs):
        for d in dirs:
            when(goes[d], lambda d=d: make(phase, d).wait_send())

    def from_view(v, dst, r):
        return pltpu.make_async_remote_copy(
            src_ref=dst, dst_ref=dst, send_sem=r.at[v], recv_sem=r.at[v], device_id=(v, tile), device_id_type=MESH
        )

    def out_to(v, src, dst, s, r):
        return pltpu.make_async_remote_copy(
            src_ref=src, dst_ref=dst, send_sem=s.at[v], recv_sem=r.at[view], device_id=(v, tile), device_id_type=MESH
        )

    def lit_copy(d):
        return pltpu.make_async_remote_copy(
            src_ref=lit_of, dst_ref=lit_got.at[d], send_sem=l_s.at[d], recv_sem=l_r.at[d],
            device_id=to_device[d], device_id_type=MESH,
        )

    ker_copy.wait()
    lane32 = lane_of((32, LANES))
    row32 = lax.broadcasted_iota(jnp.int32, (32, LANES), 0)
    axis_now = det_ref[0].astype(F32)
    lit_now = (lit_ref[0, 0] > 0).astype(F32)
    k0 = jnp.concatenate([kpad[:, 0, 0:LANES], jnp.zeros((1, LANES), F32)], axis=0)
    k1 = jnp.concatenate([kpad[:, 0, LANES:Z], jnp.zeros((TAPS, 2 * LANES - Z), F32)], axis=1)
    k1 = jnp.concatenate([k1, jnp.zeros((1, LANES), F32)], axis=0)
    for half in range(2):
        taps = roll(k0, 16) if half == 0 else jnp.where(lane32 < 48, roll(k0, 48), roll(k1, 48))
        taps = jnp.where(row32 == TAPS, axis_now, taps)
        for i, t in enumerate(pack([taps[8 * j : 8 * j + 8] for j in range(4)])):
            tap_send[half, i] = t
    tap_got[view] = tap_send[deep_half]
    lit_of[view] = jnp.full((1, LANES), lit_now, F32)

    def pack_rows(i):
        rec_in_copy(i).wait()
        rows = lax.rem(cx + ROUND[i], XC)

        def pack_part(part, carry):
            base = pl.multiple_of(rows * CHUNK + part * 4 * Z, LANES)
            tiles = [rec[:, pl.ds(base + LANES * j, LANES)] for j in range(6)]
            one, two = pair_halves(*tiles[:3]), pair_halves(*tiles[3:])
            for half in range(2):
                packed = pack([*one[half], *two[half]])
                for j in range(3):
                    send[rows * 2 + lax.rem(half + odd, 2), part * 3 + j] = packed[j]
            return carry

        lax.fori_loop(0, 4, pack_part, 0)

    def send_block(dx, dz):
        v = at(dx, dz)
        out_to(v, send.at[v], got.at[view], a_s, a_r).start()

    pack_rows(0)
    pl.semaphore_wait(barrier, 7 + (tile > 0).astype(jnp.int32) + (tile < TILES - 1).astype(jnp.int32))

    FAR = ((0, 0), (1, 1), (3, 0), (2, 1))

    def tap_copy(v):
        return out_to(v, tap_send.at[lax.rem(v + odd, 2)], tap_got.at[view], t_s, t_r)

    def tap_pass(v):
        return pltpu.make_async_remote_copy(
            src_ref=tap_got.at[v], dst_ref=tap_got.at[v], send_sem=m_s.at[v], recv_sem=m_r.at[v],
            device_id=chip_mate, device_id_type=MESH,
        )

    for dx, c in FAR:
        pl.when(core == c)(lambda dx=dx: tap_copy(at(dx, 1)).start())
    send_block(0, 1)
    for dx in (1, 3, 2):
        tap_copy(at(dx, 0)).start()
    for dx, dz in others:
        out_to(at(dx, dz), lit_of.at[view], lit_of.at[view], e_s, e_r).start()
    pack_rows(1)
    send_block(ROUND[1], 1)
    send_block(ROUND[1], 0)
    for i in range(2, 4):
        pack_rows(i)
        send_block(ROUND[i], 0)
    got[view] = send[view]

    zero_rim = jnp.zeros((16, 16, LANES), F32)
    for d, into in ((0, 32), (1, 0)):
        @pl.when(jnp.logical_not(comes[d]))
        def _(d=d, into=into):
            grid[1, into : into + 16] = zero_rim
            lit_got[d] = jnp.zeros((VIEWS, 1, LANES), F32)

    for d in range(4):
        @pl.when(jnp.logical_not(comes[d]))
        def _(d=d):
            for i in range(ITERS):
                land[i, d] = zero_rim[:15]

    est[:, 0:CHUNK] = jnp.zeros((CX, CHUNK), F32)
    est[:, CHUNK + YW * Z : 2 * CHUNK + YW * Z] = jnp.zeros((CX, CHUNK), F32)
    est_copy.wait()
    lane16 = lane_of((CX, LANES))
    edge = (lane16 >= jnp.where(upper, 0, RIM)) & (lane16 < jnp.where(upper, RIM + DEPTH, LANES))
    high_half = jnp.broadcast_to(deep_half, (CX, LANES)) == 1

    def est_pair(j, carry):
        base = pl.multiple_of(cx * CHUNK + j * 2 * Z, LANES)
        tiles = [est[:, pl.ds(base + LANES * i, LANES)] for i in range(3)]
        low, high = pair_halves(*tiles)
        for i in range(2):
            grid[0, 2 * j + i] = jnp.where(edge, jnp.where(high_half, high[i], low[i]), 0.0)
        return carry

    def block_left(dx, dz):
        v = at(dx, dz)
        out_to(v, send.at[v], got.at[view], a_s, a_r).wait_send()

    lax.fori_loop(8, 16, est_pair, 0)
    centre = grid[0, 16:32]
    grid[1, 16:32] = swap(centre)
    for half in range(2):
        start_rims(volume_rim(half), 0, (0, 1))
    send_block(ROUND[2], 1)
    send_block(ROUND[3], 1)
    depth_in[...] = split3(centre.reshape(256, LANES))
    lax.fori_loop(0, 8, est_pair, 0)
    lax.fori_loop(16, 24, est_pair, 0)

    for dx, c in FAR:
        def take_far(dx=dx):
            v = at(XC - dx, 1)
            from_view(v, tap_got.at[v], t_r).wait_recv()
            tap_pass(v).start()

        pl.when(core == c)(take_far)
    for dx in (1, 3, 2):
        v = at(dx, 0)
        from_view(v, tap_got.at[v], t_r).wait_recv()
    for dx, dz in others:
        v = at(dx, dz)
        from_view(v, lit_of.at[v], e_r).wait_recv()
    for dx, c in FAR:
        pl.when(core != c)(lambda dx=dx: tap_pass(at(XC - dx, 1)).wait_recv())

    def slot(v):
        return lax.rem(v + zh, 2) * XC + v // 2

    def prepare(v, carry):
        taps = jnp.concatenate(unpack([tap_got[v, i] for i in range(3)]), axis=0)
        marks = taps[31:32]
        lane = lane_of((1, LANES))
        axis = jnp.sum(jnp.where(lane == 32, marks, 0.0), axis=1, keepdims=True)
        lit = lit_of[v]
        inner = (lane32 >= RIM) & (lane32 < RIM + DEPTH) & (row32 < TAPS)
        taps = jnp.where(inner, taps, 0.0)
        along = [jnp.broadcast_to(jnp.where(axis == float(d), 1.0, 0.0), (1, LANES)) for d in range(3)]
        flags_of[v] = jnp.concatenate([along[0], along[1], lit, jnp.zeros((5, LANES), F32)], axis=0)
        weight[v] = taps * (along[0] + along[1])
        tall = jnp.concatenate([taps * along[2], jnp.zeros((LANES - 32, LANES), F32)], axis=0)
        full = pltpu.roll(jnp.transpose(tall), LANES - HALF, 1, stride=1, stride_axis=0)
        for i, part in enumerate(parts_of(full * lit, (0, 1, 0))):
            band[pl.ds(pl.multiple_of(slot(v) * 3 * LANES + i * LANES, LANES), LANES)] = part
        here = pl.ds(pl.multiple_of(v * LANES, LANES), LANES)
        for i, part in enumerate(parts_of(jnp.transpose(full), (0, 1, 0))):
            band_t[LANES * i : LANES * (i + 1), here] = part
        return carry

    lax.fori_loop(0, VIEWS, prepare, 0)
    for d in (0, 1):
        when(goes[d], lambda d=d: lit_copy(d).start())

    def depth_products():
        product = jnp.dot(depth_in[...], band_t[...], preferred_element_type=F32)
        for v in range(VIEWS):
            deep[v] = product[:, LANES * v : LANES * (v + 1)].reshape(16, 16, LANES)

    def depth_sums(part):
        span = slice(part * XC * 3 * LANES, (part + 1) * XC * 3 * LANES)
        product = jnp.dot(ratios[:, span], band[span], preferred_element_type=F32)
        total[0, 16:32] += product.reshape(16, 16, LANES)

    def tap_sum(out, first, count, source, origin, sign, v):
        length = source.shape[0]
        for k in range(TAPS):
            shift = sign * (k - HALF)
            lo = max(first, origin - shift)
            hi = min(first + count, origin + length - shift)
            if lo >= hi:
                continue
            part = source[lo + shift - origin : hi + shift - origin] * weight[v, k : k + 1][None]
            pieces = []
            if lo > first:
                pieces.append(out[: lo - first])
            pieces.append(out[lo - first : hi - first] + part)
            if hi < first + count:
                pieces.append(out[hi - first :])
            out = jnp.concatenate(pieces, axis=0) if len(pieces) > 1 else pieces[0]
        return out

    def along_x(v):
        return jnp.broadcast_to(flags_of[v, 0:1], (8, LANES))

    def in_layout(v, first, count, s):
        return jnp.where(
            (along_x(v) > 0.5)[None],
            grid[1, first : first + count, 8 * s : 8 * s + 8],
            grid[0, first : first + count, 8 * s : 8 * s + 8],
        )

    def blur_inside(v, carry):
        for s in range(2):
            blurred[v, :, 8 * s : 8 * s + 8] = tap_sum(
                jnp.zeros((16, 8, LANES), F32), 0, 16, in_layout(v, 16, 16, s), 0, 1, v
            )
        return carry

    def blur_rims(s, v, carry):
        acc = tap_sum(blurred[v, :, 8 * s : 8 * s + 8], 0, 16, in_layout(v, 1, 15, s), -15, 1, v)
        acc = tap_sum(acc, 0, 16, in_layout(v, 32, 15, s), 16, 1, v)
        blurred[v, :, 8 * s : 8 * s + 8] = acc + deep[v, :, 8 * s : 8 * s + 8]
        return carry

    lane3 = lane_of((16, 16, LANES))
    inner3 = (lane3 >= RIM) & (lane3 < RIM + DEPTH)

    def take_ratio(v):
        ratio = jnp.where(inner3, rec_in[v] / blurred[v], 0.0)
        blurred[v] = ratio
        ratios[:, pl.ds(pl.multiple_of(slot(v) * 3 * LANES, LANES), 3 * LANES)] = split3(ratio.reshape(256, LANES))

    def spread_rims(v, s):
        x = along_x(v)
        y = jnp.broadcast_to(flags_of[v, 1:2], (8, LANES))
        lit = jnp.broadcast_to(flags_of[v, 2:3], (8, LANES))
        r = blurred[v, :, 8 * s : 8 * s + 8]
        for first, row in ((-HALF, 1), (16, 0)):
            acc = tap_sum(jnp.zeros((HALF, 8, LANES), F32), first, HALF, r, 0, -1, v)
            cells = slice(first + 16, first + 16 + HALF)
            lit_x = jnp.broadcast_to(lit_got[row, v], (8, LANES))
            total[1, cells, 8 * s : 8 * s + 8] += acc * (x * lit_x)[None]
            total[0, cells, 8 * s : 8 * s + 8] += acc * (y * lit)[None]

    def spread_inside(v, carry):
        x = along_x(v)
        y = jnp.broadcast_to(flags_of[v, 1:2], (8, LANES))
        lit = jnp.broadcast_to(flags_of[v, 2:3], (8, LANES))
        for s in range(2):
            acc = tap_sum(
                jnp.zeros((16, 8, LANES), F32), 0, 16, blurred[v, :, 8 * s : 8 * s + 8], 0, -1, v
            )
            total[1, 16:32, 8 * s : 8 * s + 8] += acc * (x * lit)[None]
            total[0, 16:32, 8 * s : 8 * s + 8] += acc * (y * lit)[None]
        return carry

    def update(phase):
        for d in range(4):
            layout = 1 if d < 2 else 0
            first = 17 if d % 2 == 0 else 16
            total[layout, first : first + 15] += land[phase // 2, d]
        unlit = jnp.zeros((1, LANES), F32)
        for v in range(VIEWS):
            unlit = unlit + (1.0 - flags_of[v, 2:3])
        rim = unpack_rim(rim_land[phase], jnp.where(upper, 16, 96)).reshape(16, 16, LANES)
        summed = total[0, 16:32] + swap(total[1, 16:32]) + rim + unlit[None]
        return jnp.where(inner3, grid[0, 16:32] * summed * (1.0 / VIEWS), 0.0)

    lax.fori_loop(0, VIEWS, blur_inside, 0)
    depth_products()
    for half in range(2):
        recv_rims(volume_rim(half), 0, (0, 1))
        lax.fori_loop(0, VIEWS, functools.partial(blur_rims, half), 0)
    for d in (0, 1):
        when(comes[d], lambda d=d: lit_copy(d).wait_recv())

    def arrive(v):
        rows = []
        for part in range(4):
            rows += unpack([got[v, 3 * part + i] for i in range(3)])
        cells = jnp.stack(rows)
        first_dim = jnp.broadcast_to((along_x(v) > 0.5)[None, :1], (16, 16, LANES))
        rec_in[v] = jnp.where(first_dim, swap(cells), cells)

    total[...] = jnp.zeros((2, 48, 16, LANES), F32)
    arrive(view)
    take_ratio(view)
    for s in range(2):
        spread_rims(view, s)

    def view_of(step):
        i = lax.rem(step, 4)
        order = jnp.where(i == 0, 0, lax.rem(i + 1, 3) + 1)
        return lax.rem(cx + order, XC) * 2 + lax.rem(zh + step // 4, 2)

    def take_arrived(step, carry):
        v = view_of(step)
        from_view(v, got.at[v], a_r).wait_recv()
        arrive(v)
        take_ratio(v)
        return carry

    def spread_arrived(step, carry):
        take_arrived(step, carry)
        for s in range(2):
            spread_rims(view_of(step), s)
        return carry

    lax.fori_loop(1, XC, spread_arrived, 0)
    depth_sums(0)
    lax.fori_loop(XC, VIEWS, take_arrived, 0)

    SIDES = (2, 3, 0, 1)

    def send_depth_sums(phase):
        rim_send[phase] = pack_rim(total[0, 16:32].reshape(256, LANES), jnp.where(upper, 0, 16))
        start_rims(depth_rim, phase, (4,))

    def finish_sums(phase):
        lax.fori_loop(0, VIEWS, spread_inside, 0)
        for half in range(2):
            recv_rims(sum_rim(half), phase, SIDES)
        recv_rims(depth_rim, phase, (4,))

    def sums_left(phase):
        for half in range(2):
            sent_rims(sum_rim(half), phase, SIDES)
        sent_rims(depth_rim, phase, (4,))

    def spread_halves(phase, first):
        for half in range(2):
            def beyond(step, carry, half=half):
                spread_rims(view_of(step), half)
                return carry

            lax.fori_loop(first, VIEWS, beyond, 0)
            start_rims(sum_rim(half), phase, SIDES)

    for half in range(2):
        sent_rims(volume_rim(half), 0, (0, 1))
    depth_sums(1)
    send_depth_sums(1)
    spread_halves(1, XC)
    finish_sums(1)
    fresh = update(1)
    grid[0, 16:32] = fresh
    start_rims(volume_rim(0), 2, (2, 3))
    grid[1, 16:32] = swap(fresh)
    start_rims(volume_rim(0), 2, (0, 1))
    rim_send[2] = pack_rim(fresh.reshape(256, LANES), jnp.where(upper, 112, 32))
    start_rims(depth_rim, 2, (4,))
    start_rims(volume_rim(1), 2, SIDES)
    sums_left(1)
    total[...] = jnp.zeros((2, 48, 16, LANES), F32)
    lax.fori_loop(0, VIEWS, blur_inside, 0)
    recv_rims(depth_rim, 2, (4,))
    deep_rim = unpack_rim(rim_land[2], jnp.where(upper, 0, 112))
    depth_in[...] = split3(grid[0, 16:32].reshape(256, LANES) + deep_rim)
    depth_products()
    recv_rims(volume_rim(0), 2, SIDES)
    lax.fori_loop(0, VIEWS, functools.partial(blur_rims, 0), 0)
    recv_rims(volume_rim(1), 2, SIDES)

    def second(v, carry):
        blur_rims(1, v, 0)
        take_ratio(v)
        return carry

    lax.fori_loop(0, VIEWS, second, 0)
    depth_sums(0)
    depth_sums(1)
    send_depth_sums(3)
    spread_halves(3, 0)
    finish_sums(3)
    fresh = update(3)

    size = PACKED // PIECES

    def half_copy(i, block):
        cells = gathered.at[block, pl.ds(size * i, size)]
        return pltpu.make_async_remote_copy(
            src_ref=cells, dst_ref=cells, send_sem=z_s.at[i], recv_sem=z_r.at[i], device_id=(mate, tile), device_id_type=MESH
        )

    def row_copy(dx, block):
        cells = gathered.at[block]
        return pltpu.make_async_remote_copy(
            src_ref=cells, dst_ref=cells, send_sem=g_s.at[dx - 1], recv_sem=g_r.at[dx - 1],
            device_id=(at(dx, 0), tile), device_id_type=MESH,
        )

    def forward_copy(dx, i, block):
        cells = gathered.at[block, pl.ds(size * i, size)]
        return pltpu.make_async_remote_copy(
            src_ref=cells, dst_ref=cells, send_sem=f_s.at[dx - 1, i], recv_sem=f_r.at[dx - 1, i],
            device_id=(at(dx, 0), tile), device_id_type=MESH,
        )

    for part in range(PIECES):
        packed = pack([fresh[4 * part + i] for i in range(4)])
        for i in range(3):
            gathered[view, 3 * part + i] = packed[i]
        half_copy(part, view).start()
    for dx in (1, 3, 2):
        row_copy(dx, view).start()

    def unpack_out(rows, part):
        low = unpack([gathered[2 * rows + odd, 3 * part + j] for j in range(3)])
        high = unpack([gathered[2 * rows + 1 - odd, 3 * part + j] for j in range(3)])
        base = pl.multiple_of(rows * CHUNK + part * 4 * Z, LANES)
        for p in range(2):
            for j, t in enumerate(halves_pair(low[2 * p], high[2 * p], low[2 * p + 1], high[2 * p + 1])):
                out[:, pl.ds(base + LANES * (3 * p + j), LANES)] = t

    for part in range(PIECES):
        half_copy(part, mate).wait_recv()
        for dx in (1, 3, 2):
            forward_copy(dx, part, mate).start()
        unpack_out(cx, part)
    for dx in (1, 3, 2):
        row_copy(dx, at(XC - dx, 0)).wait_recv()
    for part in range(PIECES):
        for dx in (1, 3, 2):
            forward_copy(dx, part, at(XC - dx, 1)).wait_recv()
            unpack_out(at(XC - dx, 0) // 2, part)

    for d in (0, 1):
        when(goes[d], lambda d=d: lit_copy(d).wait_send())
    for dx, dz in others:
        v = at(dx, dz)
        out_to(v, lit_of.at[view], lit_of.at[view], e_s, e_r).wait_send()
        block_left(dx, dz)
    for dx, c in FAR:
        pl.when(core == c)(lambda dx=dx: tap_copy(at(dx, 1)).wait_send())
        pl.when(core == c)(lambda dx=dx: tap_pass(at(XC - dx, 1)).wait_send())
    for dx in (1, 3, 2):
        tap_copy(at(dx, 0)).wait_send()
    for half in range(2):
        sent_rims(volume_rim(half), 2, SIDES)
    sent_rims(depth_rim, 2, (4,))
    sums_left(3)
    for i in range(PIECES):
        half_copy(i, view).wait_send()
    for dx in (1, 3, 2):
        row_copy(dx, view).wait_send()
        for i in range(PIECES):
            forward_copy(dx, i, mate).wait_send()


def on_device(estimate, recorded, kernels, illuminated, detection):
    dma = pltpu.SemaphoreType.DMA
    vmem = lambda *shape: pltpu.VMEM(shape, F32)
    any_space = pl.BlockSpec(memory_space=pltpu.HBM)
    return pl.pallas_call(
        kernel,
        out_shape=jax.ShapeDtypeStruct((CX, YW * Z), F32),
        in_specs=[
            any_space,
            any_space,
            any_space,
            pl.BlockSpec(memory_space=pltpu.SMEM),
            pl.BlockSpec(memory_space=pltpu.SMEM),
        ],
        out_specs=pl.BlockSpec(memory_space=pltpu.VMEM),
        scratch_shapes=[
            vmem(CX, YW * Z + 2 * CHUNK),
            vmem(CX, YW * Z),
            vmem(TAPS, 1, Z),
            vmem(VIEWS, PACKED, CX, LANES),
            vmem(VIEWS, PACKED, CX, LANES),
            vmem(2, 3, 8, LANES),
            vmem(VIEWS, 3, 8, LANES),
            vmem(VIEWS, 1, LANES),
            vmem(2, VIEWS, 1, LANES),
            vmem(VIEWS, 8, LANES),
            vmem(VIEWS, 32, LANES),
            pltpu.VMEM((VIEWS * 3 * LANES, LANES), BF16),
            pltpu.VMEM((3 * LANES, VIEWS * LANES), BF16),
            vmem(2, 48, 16, LANES),
            pltpu.VMEM((256, 3 * LANES), BF16),
            vmem(VIEWS, 16, 16, LANES),
            pltpu.VMEM((256, VIEWS * 3 * LANES), BF16),
            vmem(VIEWS, 16, 16, LANES),
            vmem(VIEWS, 16, 16, LANES),
            vmem(2, 48, 16, LANES),
            vmem(ITERS, 4, HALF, 16, LANES),
            vmem(4, 32, LANES),
            vmem(4, 32, LANES),
            vmem(VIEWS, PACKED, CX, LANES),
            dma((6,)),
            dma((VIEWS,)), dma((VIEWS,)),
            dma((VIEWS,)), dma((VIEWS,)),
            dma((VIEWS,)), dma((VIEWS,)),
            dma((VIEWS,)), dma((VIEWS,)),
            dma((2,)), dma((2,)),
            dma((4, 5, 2)), dma((4, 5, 2)),
            dma((3,)), dma((3,)),
            dma((PIECES,)), dma((PIECES,)),
            dma((3, PIECES)), dma((3, PIECES)),
        ],
        compiler_params=pltpu.CompilerParams(
            collective_id=0, has_side_effects=True, vmem_limit_bytes=VMEM_BYTES
        ),
    )(estimate, recorded, jnp.swapaxes(kernels, 0, 1), illuminated, detection)


def solution(mesh):
    in_specs = (
        P("tile", None),
        P("view", "tile", None),
        P("view", None, None),
        P("view", "tile"),
        P("view"),
    )
    return jax.shard_map(
        on_device, mesh=mesh, in_specs=in_specs, out_specs=P("tile", None), check_vma=False
    )
```

```python
import functools

import jax
import jax.numpy as jnp
from jax import lax
from jax.experimental import pallas as pl
from jax.experimental.pallas import tpu as pltpu
from jax.sharding import PartitionSpec as P


YW = 64
Z = 192
TAPS = 31
HALF = 15
ITERS = 2
VIEWS = 8
XC = 4
TILES = 32
CX = 16
ROWS = 16
DEPTH = 96
LANES = 128
RIM = 16
CHUNK = ROWS * Z
PACKED = 12
PIECES = 4
VMEM_BYTES = 53 * 1024 * 1024
MESH = pl.DeviceIdType.MESH
F32 = jnp.float32
BF16 = jnp.bfloat16


def lane_of(shape):
    return lax.broadcasted_iota(jnp.int32, shape, len(shape) - 1)


def roll(a, shift):
    return pltpu.roll(a, shift, a.ndim - 1)


def pair_halves(t0, t1, t2):
    lane = lane_of(t0.shape)
    a0 = roll(t0, 16)
    a1 = jnp.where(lane < 48, roll(t0, 48), roll(t1, 48))
    b0 = jnp.where(lane < 80, roll(t1, 80), roll(t2, 80))
    b1 = roll(t2, 112)
    return (a0, b0), (a1, b1)


def halves_pair(a0, a1, b0, b1):
    lane = lane_of(a0.shape)
    a1r, b0r = roll(a1, 80), roll(b0, 48)
    t0 = jnp.where(lane < 96, roll(a0, 112), a1r)
    t1 = jnp.where(lane < 64, a1r, b0r)
    t2 = jnp.where(lane < 32, b0r, roll(b1, 16))
    return t0, t1, t2


def pack(rows):
    lane = lane_of(rows[0].shape)
    inner = (lane >= RIM) & (lane < RIM + DEPTH)
    return [jnp.where(inner, rows[i], roll(rows[3], 96 - 32 * i)) for i in range(3)]


def unpack(tiles):
    lane = lane_of(tiles[0].shape)
    r = [roll(tiles[i], 32 + 32 * i) for i in range(3)]
    return [tiles[0], tiles[1], tiles[2], jnp.where(lane < 48, r[0], jnp.where(lane < 80, r[1], r[2]))]


def swap(a):
    return jnp.swapaxes(a, 0, 1)


def pack_rim(a, shift):
    lane = lane_of((32, LANES))
    out = jnp.zeros((32, LANES), F32)
    for g in range(8):
        moved = roll(a[32 * g : 32 * g + 32], lax.rem(shift + 16 * g, 128))
        out = jnp.where((lane >= 16 * g) & (lane < 16 * g + 16), moved, out)
    return out


def unpack_rim(p, first):
    lane = lane_of((32, LANES))
    keep = (lane >= first) & (lane < first + 16)
    return jnp.concatenate(
        [jnp.where(keep, roll(p, lax.rem(first + 128 - 16 * g, 128)), 0.0) for g in range(8)], axis=0
    )


def parts_of(a, order):
    high = a.astype(BF16)
    low = (a - high.astype(F32)).astype(BF16)
    return [(high, low)[i] for i in order]


def split3(a):
    return jnp.concatenate(parts_of(a, (0, 0, 1)), axis=-1)


def kernel(
    est_hbm, rec_hbm, ker_hbm, lit_ref, det_ref, out,
    est, rec, kpad, send, got, tap_send, tap_got, lit_of, lit_got, flags_of,
    weight, band, band_t, grid, depth_in, deep, ratios, rec_in, blurred, total, land, rim_send, rim_land, gathered,
    in_sem, a_s, a_r, t_s, t_r, m_s, m_r, e_s, e_r, l_s, l_r, h_s, h_r, g_s, g_r, z_s, z_r, f_s, f_r,
):
    view = lax.axis_index("view")
    tile = lax.axis_index("tile")
    cx, zh = view // 2, lax.rem(view, 2)
    odd = lax.rem(tile // 8, 2)
    core = lax.rem(tile, 2)
    chip_mate = (view, tile + 1 - 2 * core)
    deep_half = lax.rem(zh + odd, 2)
    upper = deep_half == 1

    def at(dx, dz):
        return lax.rem(cx + dx, XC) * 2 + lax.rem(zh + dz, 2)

    mate = at(0, 1)
    others = [(0, 1), (1, 1), (1, 0), (3, 1), (3, 0), (2, 1), (2, 0)]

    to_device = [
        (jnp.where(lax.rem(tile, 8) == 0, mate, view), lax.rem(tile + TILES - 1, TILES)),
        (jnp.where(lax.rem(tile, 8) == 7, mate, view), lax.rem(tile + 1, TILES)),
        (lax.rem(view + VIEWS - 2, VIEWS), tile),
        (lax.rem(view + 2, VIEWS), tile),
        (mate, tile),
    ]
    goes = [tile > 0, tile < TILES - 1, cx > 0, cx < XC - 1, None]
    comes = [tile < TILES - 1, tile > 0, cx < XC - 1, cx > 0, None]

    def when(cond, f):
        if cond is None:
            f()
        else:
            pl.when(cond)(f)

    barrier = pltpu.get_barrier_semaphore()

    def greet(device):
        pl.semaphore_signal(barrier, inc=1, device_id=device, device_id_type=MESH)

    for dx, dz in others:
        greet((at(dx, dz), tile))
    for d in (0, 1):
        when(goes[d], lambda d=d: greet(to_device[d]))

    ROUND = (0, 1, 3, 2)

    def rec_in_copy(i):
        cells = pl.ds(pl.multiple_of(lax.rem(cx + ROUND[i], XC) * CHUNK, LANES), CHUNK)
        return pltpu.make_async_copy(rec_hbm.at[0, :, cells], rec.at[:, cells], in_sem.at[i])

    ker_copy = pltpu.make_async_copy(ker_hbm, kpad, in_sem.at[4])
    est_copy = pltpu.make_async_copy(est_hbm, est.at[:, pl.ds(CHUNK, YW * Z)], in_sem.at[5])
    ker_copy.start()
    for i in range(4):
        rec_in_copy(i).start()
    est_copy.start()

    def rim_copy(phase, d, src, dst, half=0):
        return pltpu.make_async_remote_copy(
            src_ref=src, dst_ref=dst, send_sem=h_s.at[phase, d, half], recv_sem=h_r.at[phase, d, half],
            device_id=to_device[d], device_id_type=MESH,
        )

    def volume_rim(half):
        def make(phase, d):
            layout = 1 if d < 2 else 0
            source, target = (16, 32) if d % 2 == 0 else (17, 1)
            part = pl.ds(8 * half, 8)
            return rim_copy(
                phase, d, grid.at[layout, pl.ds(source, 15), part], grid.at[layout, pl.ds(target, 15), part], half
            )

        return make

    def sum_rim(half):
        def make(phase, d):
            layout = 1 if d < 2 else 0
            first = 1 if d % 2 == 0 else 32
            part = pl.ds(8 * half, 8)
            return rim_copy(
                phase, d, total.at[layout, pl.ds(first, 15), part], land.at[phase // 2, d, :, part], half
            )

        return make

    def depth_rim(phase, d):
        return rim_copy(phase, d, rim_send.at[phase], rim_land.at[phase])

    def start_rims(make, phase, dirs):
        for d in dirs:
            when(goes[d], lambda d=d: make(phase, d).start())

    def recv_rims(make, phase, dirs):
        for d in dirs:
            when(comes[d], lambda d=d: make(phase, d).wait_recv())

    def sent_rims(make, phase, dirs):
        for d in dirs:
            when(goes[d], lambda d=d: make(phase, d).wait_send())

    def from_view(v, dst, r):
        return pltpu.make_async_remote_copy(
            src_ref=dst, dst_ref=dst, send_sem=r.at[v], recv_sem=r.at[v], device_id=(v, tile), device_id_type=MESH
        )

    def out_to(v, src, dst, s, r):
        return pltpu.make_async_remote_copy(
            src_ref=src, dst_ref=dst, send_sem=s.at[v], recv_sem=r.at[view], device_id=(v, tile), device_id_type=MESH
        )

    def lit_copy(d):
        return pltpu.make_async_remote_copy(
            src_ref=lit_of, dst_ref=lit_got.at[d], send_sem=l_s.at[d], recv_sem=l_r.at[d],
            device_id=to_device[d], device_id_type=MESH,
        )

    ker_copy.wait()
    lane32 = lane_of((32, LANES))
    row32 = lax.broadcasted_iota(jnp.int32, (32, LANES), 0)
    axis_now = det_ref[0].astype(F32)
    lit_now = (lit_ref[0, 0] > 0).astype(F32)
    k0 = jnp.concatenate([kpad[:, 0, 0:LANES], jnp.zeros((1, LANES), F32)], axis=0)
    k1 = jnp.concatenate([kpad[:, 0, LANES:Z], jnp.zeros((TAPS, 2 * LANES - Z), F32)], axis=1)
    k1 = jnp.concatenate([k1, jnp.zeros((1, LANES), F32)], axis=0)
    for half in range(2):
        taps = roll(k0, 16) if half == 0 else jnp.where(lane32 < 48, roll(k0, 48), roll(k1, 48))
        taps = jnp.where(row32 == TAPS, axis_now, taps)
        for i, t in enumerate(pack([taps[8 * j : 8 * j + 8] for j in range(4)])):
            tap_send[half, i] = t
    tap_got[view] = tap_send[deep_half]
    lit_of[view] = jnp.full((1, LANES), lit_now, F32)

    def pack_rows(i):
        rec_in_copy(i).wait()
        rows = lax.rem(cx + ROUND[i], XC)

        def pack_part(part, carry):
            base = pl.multiple_of(rows * CHUNK + part * 4 * Z, LANES)
            tiles = [rec[:, pl.ds(base + LANES * j, LANES)] for j in range(6)]
            one, two = pair_halves(*tiles[:3]), pair_halves(*tiles[3:])
            for half in range(2):
                packed = pack([*one[half], *two[half]])
                for j in range(3):
                    send[rows * 2 + lax.rem(half + odd, 2), part * 3 + j] = packed[j]
            return carry

        lax.fori_loop(0, 4, pack_part, 0)

    def send_block(dx, dz):
        v = at(dx, dz)
        out_to(v, send.at[v], got.at[view], a_s, a_r).start()

    pack_rows(0)
    pl.semaphore_wait(barrier, 7 + (tile > 0).astype(jnp.int32) + (tile < TILES - 1).astype(jnp.int32))

    FAR = ((0, 0), (1, 1), (3, 0), (2, 1))

    def tap_copy(v):
        return out_to(v, tap_send.at[lax.rem(v + odd, 2)], tap_got.at[view], t_s, t_r)

    def tap_pass(v):
        return pltpu.make_async_remote_copy(
            src_ref=tap_got.at[v], dst_ref=tap_got.at[v], send_sem=m_s.at[v], recv_sem=m_r.at[v],
            device_id=chip_mate, device_id_type=MESH,
        )

    for dx, c in FAR:
        pl.when(core == c)(lambda dx=dx: tap_copy(at(dx, 1)).start())
    send_block(0, 1)
    for dx in (1, 3, 2):
        tap_copy(at(dx, 0)).start()
    for dx, dz in others:
        out_to(at(dx, dz), lit_of.at[view], lit_of.at[view], e_s, e_r).start()
    pack_rows(1)
    send_block(ROUND[1], 1)
    send_block(ROUND[1], 0)
    for i in range(2, 4):
        pack_rows(i)
        send_block(ROUND[i], 0)
    got[view] = send[view]

    zero_rim = jnp.zeros((16, 16, LANES), F32)
    for d, into in ((0, 32), (1, 0)):
        @pl.when(jnp.logical_not(comes[d]))
        def _(d=d, into=into):
            grid[1, into : into + 16] = zero_rim
            lit_got[d] = jnp.zeros((VIEWS, 1, LANES), F32)

    for d in range(4):
        @pl.when(jnp.logical_not(comes[d]))
        def _(d=d):
            for i in range(ITERS):
                land[i, d] = zero_rim[:15]

    est[:, 0:CHUNK] = jnp.zeros((CX, CHUNK), F32)
    est[:, CHUNK + YW * Z : 2 * CHUNK + YW * Z] = jnp.zeros((CX, CHUNK), F32)
    est_copy.wait()
    lane16 = lane_of((CX, LANES))
    edge = (lane16 >= jnp.where(upper, 0, RIM)) & (lane16 < jnp.where(upper, RIM + DEPTH, LANES))
    high_half = jnp.broadcast_to(deep_half, (CX, LANES)) == 1

    def est_pair(j, carry):
        base = pl.multiple_of(cx * CHUNK + j * 2 * Z, LANES)
        tiles = [est[:, pl.ds(base + LANES * i, LANES)] for i in range(3)]
        low, high = pair_halves(*tiles)
        for i in range(2):
            grid[0, 2 * j + i] = jnp.where(edge, jnp.where(high_half, high[i], low[i]), 0.0)
        return carry

    def block_left(dx, dz):
        v = at(dx, dz)
        out_to(v, send.at[v], got.at[view], a_s, a_r).wait_send()

    lax.fori_loop(8, 16, est_pair, 0)
    centre = grid[0, 16:32]
    grid[1, 16:32] = swap(centre)
    for half in range(2):
        start_rims(volume_rim(half), 0, (0, 1))
    send_block(ROUND[2], 1)
    send_block(ROUND[3], 1)
    depth_in[...] = split3(centre.reshape(256, LANES))
    lax.fori_loop(0, 8, est_pair, 0)
    lax.fori_loop(16, 24, est_pair, 0)

    for dx, c in FAR:
        def take_far(dx=dx):
            v = at(XC - dx, 1)
            from_view(v, tap_got.at[v], t_r).wait_recv()
            tap_pass(v).start()

        pl.when(core == c)(take_far)
    for dx in (1, 3, 2):
        v = at(dx, 0)
        from_view(v, tap_got.at[v], t_r).wait_recv()
    for dx, dz in others:
        v = at(dx, dz)
        from_view(v, lit_of.at[v], e_r).wait_recv()
    for dx, c in FAR:
        pl.when(core != c)(lambda dx=dx: tap_pass(at(XC - dx, 1)).wait_recv())

    def slot(v):
        return lax.rem(v + zh, 2) * XC + v // 2

    def prepare(v, carry):
        taps = jnp.concatenate(unpack([tap_got[v, i] for i in range(3)]), axis=0)
        marks = taps[31:32]
        lane = lane_of((1, LANES))
        axis = jnp.sum(jnp.where(lane == 32, marks, 0.0), axis=1, keepdims=True)
        lit = lit_of[v]
        inner = (lane32 >= RIM) & (lane32 < RIM + DEPTH) & (row32 < TAPS)
        taps = jnp.where(inner, taps, 0.0)
        along = [jnp.broadcast_to(jnp.where(axis == float(d), 1.0, 0.0), (1, LANES)) for d in range(3)]
        flags_of[v] = jnp.concatenate([along[0], along[1], lit, jnp.zeros((5, LANES), F32)], axis=0)
        weight[v] = taps * (along[0] + along[1])
        tall = jnp.concatenate([taps * along[2], jnp.zeros((LANES - 32, LANES), F32)], axis=0)
        full = pltpu.roll(jnp.transpose(tall), LANES - HALF, 1, stride=1, stride_axis=0)
        for i, part in enumerate(parts_of(full * lit, (0, 1, 0))):
            band[pl.ds(pl.multiple_of(slot(v) * 3 * LANES + i * LANES, LANES), LANES)] = part
        here = pl.ds(pl.multiple_of(v * LANES, LANES), LANES)
        for i, part in enumerate(parts_of(jnp.transpose(full), (0, 1, 0))):
            band_t[LANES * i : LANES * (i + 1), here] = part
        return carry

    lax.fori_loop(0, VIEWS, prepare, 0)
    for d in (0, 1):
        when(goes[d], lambda d=d: lit_copy(d).start())

    def depth_products():
        product = jnp.dot(depth_in[...], band_t[...], preferred_element_type=F32)
        for v in range(VIEWS):
            deep[v] = product[:, LANES * v : LANES * (v + 1)].reshape(16, 16, LANES)

    def depth_sums(part):
        span = slice(part * XC * 3 * LANES, (part + 1) * XC * 3 * LANES)
        product = jnp.dot(ratios[:, span], band[span], preferred_element_type=F32)
        total[0, 16:32] += product.reshape(16, 16, LANES)

    def tap_sum(out, first, count, source, origin, sign, v):
        length = source.shape[0]
        for k in range(TAPS):
            shift = sign * (k - HALF)
            lo = max(first, origin - shift)
            hi = min(first + count, origin + length - shift)
            if lo >= hi:
                continue
            part = source[lo + shift - origin : hi + shift - origin] * weight[v, k : k + 1][None]
            pieces = []
            if lo > first:
                pieces.append(out[: lo - first])
            pieces.append(out[lo - first : hi - first] + part)
            if hi < first + count:
                pieces.append(out[hi - first :])
            out = jnp.concatenate(pieces, axis=0) if len(pieces) > 1 else pieces[0]
        return out

    def along_x(v):
        return jnp.broadcast_to(flags_of[v, 0:1], (8, LANES))

    def in_layout(v, first, count, s):
        return jnp.where(
            (along_x(v) > 0.5)[None],
            grid[1, first : first + count, 8 * s : 8 * s + 8],
            grid[0, first : first + count, 8 * s : 8 * s + 8],
        )

    def blur_inside(v, carry):
        for s in range(2):
            blurred[v, :, 8 * s : 8 * s + 8] = tap_sum(
                jnp.zeros((16, 8, LANES), F32), 0, 16, in_layout(v, 16, 16, s), 0, 1, v
            )
        return carry

    def blur_rims(s, v, carry):
        acc = tap_sum(blurred[v, :, 8 * s : 8 * s + 8], 0, 16, in_layout(v, 1, 15, s), -15, 1, v)
        acc = tap_sum(acc, 0, 16, in_layout(v, 32, 15, s), 16, 1, v)
        blurred[v, :, 8 * s : 8 * s + 8] = acc + deep[v, :, 8 * s : 8 * s + 8]
        return carry

    lane3 = lane_of((16, 16, LANES))
    inner3 = (lane3 >= RIM) & (lane3 < RIM + DEPTH)

    def take_ratio(v):
        ratio = jnp.where(inner3, rec_in[v] / blurred[v], 0.0)
        blurred[v] = ratio
        ratios[:, pl.ds(pl.multiple_of(slot(v) * 3 * LANES, LANES), 3 * LANES)] = split3(ratio.reshape(256, LANES))

    def spread_rims(v, s):
        x = along_x(v)
        y = jnp.broadcast_to(flags_of[v, 1:2], (8, LANES))
        lit = jnp.broadcast_to(flags_of[v, 2:3], (8, LANES))
        r = blurred[v, :, 8 * s : 8 * s + 8]
        for first, row in ((-HALF, 1), (16, 0)):
            acc = tap_sum(jnp.zeros((HALF, 8, LANES), F32), first, HALF, r, 0, -1, v)
            cells = slice(first + 16, first + 16 + HALF)
            lit_x = jnp.broadcast_to(lit_got[row, v], (8, LANES))
            total[1, cells, 8 * s : 8 * s + 8] += acc * (x * lit_x)[None]
            total[0, cells, 8 * s : 8 * s + 8] += acc * (y * lit)[None]

    def spread_inside(v, carry):
        x = along_x(v)
        y = jnp.broadcast_to(flags_of[v, 1:2], (8, LANES))
        lit = jnp.broadcast_to(flags_of[v, 2:3], (8, LANES))
        for s in range(2):
            acc = tap_sum(
                jnp.zeros((16, 8, LANES), F32), 0, 16, blurred[v, :, 8 * s : 8 * s + 8], 0, -1, v
            )
            total[1, 16:32, 8 * s : 8 * s + 8] += acc * (x * lit)[None]
            total[0, 16:32, 8 * s : 8 * s + 8] += acc * (y * lit)[None]
        return carry

    def update(phase):
        for d in range(4):
            layout = 1 if d < 2 else 0
            first = 17 if d % 2 == 0 else 16
            total[layout, first : first + 15] += land[phase // 2, d]
        unlit = jnp.zeros((1, LANES), F32)
        for v in range(VIEWS):
            unlit = unlit + (1.0 - flags_of[v, 2:3])
        rim = unpack_rim(rim_land[phase], jnp.where(upper, 16, 96)).reshape(16, 16, LANES)
        summed = total[0, 16:32] + swap(total[1, 16:32]) + rim + unlit[None]
        return jnp.where(inner3, grid[0, 16:32] * summed * (1.0 / VIEWS), 0.0)

    lax.fori_loop(0, VIEWS, blur_inside, 0)
    depth_products()
    for half in range(2):
        recv_rims(volume_rim(half), 0, (0, 1))
        lax.fori_loop(0, VIEWS, functools.partial(blur_rims, half), 0)
    for d in (0, 1):
        when(comes[d], lambda d=d: lit_copy(d).wait_recv())

    def arrive(v):
        rows = []
        for part in range(4):
            rows += unpack([got[v, 3 * part + i] for i in range(3)])
        cells = jnp.stack(rows)
        first_dim = jnp.broadcast_to((along_x(v) > 0.5)[None, :1], (16, 16, LANES))
        rec_in[v] = jnp.where(first_dim, swap(cells), cells)

    total[...] = jnp.zeros((2, 48, 16, LANES), F32)
    arrive(view)
    take_ratio(view)
    for s in range(2):
        spread_rims(view, s)

    def view_of(step):
        i = lax.rem(step, 4)
        order = jnp.where(i == 0, 0, lax.rem(i + 1, 3) + 1)
        return lax.rem(cx + order, XC) * 2 + lax.rem(zh + step // 4, 2)

    def take_arrived(step, carry):
        v = view_of(step)
        from_view(v, got.at[v], a_r).wait_recv()
        arrive(v)
        take_ratio(v)
        return carry

    def spread_arrived(step, carry):
        take_arrived(step, carry)
        for s in range(2):
            spread_rims(view_of(step), s)
        return carry

    lax.fori_loop(1, XC, spread_arrived, 0)
    depth_sums(0)
    lax.fori_loop(XC, VIEWS, take_arrived, 0)

    SIDES = (2, 3, 0, 1)

    def send_depth_sums(phase):
        rim_send[phase] = pack_rim(total[0, 16:32].reshape(256, LANES), jnp.where(upper, 0, 16))
        start_rims(depth_rim, phase, (4,))

    def finish_sums(phase):
        lax.fori_loop(0, VIEWS, spread_inside, 0)
        for half in range(2):
            recv_rims(sum_rim(half), phase, SIDES)
        recv_rims(depth_rim, phase, (4,))

    def sums_left(phase):
        for half in range(2):
            sent_rims(sum_rim(half), phase, SIDES)
        sent_rims(depth_rim, phase, (4,))

    def spread_halves(phase, first):
        for half in range(2):
            def beyond(step, carry, half=half):
                spread_rims(view_of(step), half)
                return carry

            lax.fori_loop(first, VIEWS, beyond, 0)
            start_rims(sum_rim(half), phase, SIDES)

    for half in range(2):
        sent_rims(volume_rim(half), 0, (0, 1))
    depth_sums(1)
    send_depth_sums(1)
    spread_halves(1, XC)
    finish_sums(1)
    fresh = update(1)
    grid[0, 16:32] = fresh
    start_rims(volume_rim(0), 2, (2, 3))
    grid[1, 16:32] = swap(fresh)
    start_rims(volume_rim(0), 2, (0, 1))
    rim_send[2] = pack_rim(fresh.reshape(256, LANES), jnp.where(upper, 112, 32))
    start_rims(depth_rim, 2, (4,))
    start_rims(volume_rim(1), 2, SIDES)
    sums_left(1)
    total[...] = jnp.zeros((2, 48, 16, LANES), F32)
    lax.fori_loop(0, VIEWS, blur_inside, 0)
    recv_rims(depth_rim, 2, (4,))
    deep_rim = unpack_rim(rim_land[2], jnp.where(upper, 0, 112))
    depth_in[...] = split3(grid[0, 16:32].reshape(256, LANES) + deep_rim)
    depth_products()
    recv_rims(volume_rim(0), 2, SIDES)
    lax.fori_loop(0, VIEWS, functools.partial(blur_rims, 0), 0)
    recv_rims(volume_rim(1), 2, SIDES)

    def second(v, carry):
        blur_rims(1, v, 0)
        take_ratio(v)
        return carry

    lax.fori_loop(0, VIEWS, second, 0)
    depth_sums(0)
    depth_sums(1)
    send_depth_sums(3)
    spread_halves(3, 0)
    finish_sums(3)
    fresh = update(3)

    size = PACKED // PIECES

    def half_copy(i, block):
        cells = gathered.at[block, pl.ds(size * i, size)]
        return pltpu.make_async_remote_copy(
            src_ref=cells, dst_ref=cells, send_sem=z_s.at[i], recv_sem=z_r.at[i], device_id=(mate, tile), device_id_type=MESH
        )

    def row_copy(dx, block):
        cells = gathered.at[block]
        return pltpu.make_async_remote_copy(
            src_ref=cells, dst_ref=cells, send_sem=g_s.at[dx - 1], recv_sem=g_r.at[dx - 1],
            device_id=(at(dx, 0), tile), device_id_type=MESH,
        )

    def forward_copy(dx, i, block):
        cells = gathered.at[block, pl.ds(size * i, size)]
        return pltpu.make_async_remote_copy(
            src_ref=cells, dst_ref=cells, send_sem=f_s.at[dx - 1, i], recv_sem=f_r.at[dx - 1, i],
            device_id=(at(dx, 0), tile), device_id_type=MESH,
        )

    for part in range(PIECES):
        packed = pack([fresh[4 * part + i] for i in range(4)])
        for i in range(3):
            gathered[view, 3 * part + i] = packed[i]
        half_copy(part, view).start()
    for dx in (2, 1, 3):
        row_copy(dx, view).start()

    def unpack_out(rows, part):
        low = unpack([gathered[2 * rows + odd, 3 * part + j] for j in range(3)])
        high = unpack([gathered[2 * rows + 1 - odd, 3 * part + j] for j in range(3)])
        base = pl.multiple_of(rows * CHUNK + part * 4 * Z, LANES)
        for p in range(2):
            for j, t in enumerate(halves_pair(low[2 * p], high[2 * p], low[2 * p + 1], high[2 * p + 1])):
                out[:, pl.ds(base + LANES * (3 * p + j), LANES)] = t

    for part in range(PIECES):
        half_copy(part, mate).wait_recv()
        for dx in (2, 1, 3):
            forward_copy(dx, part, mate).start()
        unpack_out(cx, part)
    for dx in (1, 3, 2):
        row_copy(dx, at(XC - dx, 0)).wait_recv()
    for part in range(PIECES):
        for dx in (1, 3, 2):
            forward_copy(dx, part, at(XC - dx, 1)).wait_recv()
            unpack_out(at(XC - dx, 0) // 2, part)

    for d in (0, 1):
        when(goes[d], lambda d=d: lit_copy(d).wait_send())
    for dx, dz in others:
        v = at(dx, dz)
        out_to(v, lit_of.at[view], lit_of.at[view], e_s, e_r).wait_send()
        block_left(dx, dz)
    for dx, c in FAR:
        pl.when(core == c)(lambda dx=dx: tap_copy(at(dx, 1)).wait_send())
        pl.when(core == c)(lambda dx=dx: tap_pass(at(XC - dx, 1)).wait_send())
    for dx in (1, 3, 2):
        tap_copy(at(dx, 0)).wait_send()
    for half in range(2):
        sent_rims(volume_rim(half), 2, SIDES)
    sent_rims(depth_rim, 2, (4,))
    sums_left(3)
    for i in range(PIECES):
        half_copy(i, view).wait_send()
    for dx in (1, 3, 2):
        row_copy(dx, view).wait_send()
        for i in range(PIECES):
            forward_copy(dx, i, mate).wait_send()


def on_device(estimate, recorded, kernels, illuminated, detection):
    dma = pltpu.SemaphoreType.DMA
    vmem = lambda *shape: pltpu.VMEM(shape, F32)
    any_space = pl.BlockSpec(memory_space=pltpu.HBM)
    return pl.pallas_call(
        kernel,
        out_shape=jax.ShapeDtypeStruct((CX, YW * Z), F32),
        in_specs=[
            any_space,
            any_space,
            any_space,
            pl.BlockSpec(memory_space=pltpu.SMEM),
            pl.BlockSpec(memory_space=pltpu.SMEM),
        ],
        out_specs=pl.BlockSpec(memory_space=pltpu.VMEM),
        scratch_shapes=[
            vmem(CX, YW * Z + 2 * CHUNK),
            vmem(CX, YW * Z),
            vmem(TAPS, 1, Z),
            vmem(VIEWS, PACKED, CX, LANES),
            vmem(VIEWS, PACKED, CX, LANES),
            vmem(2, 3, 8, LANES),
            vmem(VIEWS, 3, 8, LANES),
            vmem(VIEWS, 1, LANES),
            vmem(2, VIEWS, 1, LANES),
            vmem(VIEWS, 8, LANES),
            vmem(VIEWS, 32, LANES),
            pltpu.VMEM((VIEWS * 3 * LANES, LANES), BF16),
            pltpu.VMEM((3 * LANES, VIEWS * LANES), BF16),
            vmem(2, 48, 16, LANES),
            pltpu.VMEM((256, 3 * LANES), BF16),
            vmem(VIEWS, 16, 16, LANES),
            pltpu.VMEM((256, VIEWS * 3 * LANES), BF16),
            vmem(VIEWS, 16, 16, LANES),
            vmem(VIEWS, 16, 16, LANES),
            vmem(2, 48, 16, LANES),
            vmem(ITERS, 4, HALF, 16, LANES),
            vmem(4, 32, LANES),
            vmem(4, 32, LANES),
            vmem(VIEWS, PACKED, CX, LANES),
            dma((6,)),
            dma((VIEWS,)), dma((VIEWS,)),
            dma((VIEWS,)), dma((VIEWS,)),
            dma((VIEWS,)), dma((VIEWS,)),
            dma((VIEWS,)), dma((VIEWS,)),
            dma((2,)), dma((2,)),
            dma((4, 5, 2)), dma((4, 5, 2)),
            dma((3,)), dma((3,)),
            dma((PIECES,)), dma((PIECES,)),
            dma((3, PIECES)), dma((3, PIECES)),
        ],
        compiler_params=pltpu.CompilerParams(
            collective_id=0, has_side_effects=True, vmem_limit_bytes=VMEM_BYTES
        ),
    )(estimate, recorded, jnp.swapaxes(kernels, 0, 1), illuminated, detection)


def solution(mesh):
    in_specs = (
        P("tile", None),
        P("view", "tile", None),
        P("view", None, None),
        P("view", "tile"),
        P("view"),
    )
    return jax.shard_map(
        on_device, mesh=mesh, in_specs=in_specs, out_specs=P("tile", None), check_vma=False
    )
```
